32 devices in a mesh: groups: 2 (over x), lat: 16 (over z, y, core).
Axes of the slice: x: 2, y: 2, z: 4, core: 2. Of those that a mesh axis runs over, the one named last changes fastest.
Arguments:
- codes: bfloat16 [128, 64], P('groups'), parts along dimension 0, may hold values from 0.049804688 to 4
- indices: int32 [128, 64], P('groups'), parts along dimension 0, may hold values from 0 to 8191, as said below
- decoder: bfloat16 [8192, 8192], P('lat'), may hold values from -0.75 to 0.75
- targets: bfloat16 [128, 8192], P(('groups', 'lat')), parts along dimension 0, may hold values from -6 to 6
Outputs:
- error: bfloat16 [128, 8192], P(('groups', 'lat')), parts along dimension 0
- row_loss: float32 [128], P(('groups', 'lat')), parts along dimension 0
- code_grad: float32 [128, 64], P(('groups', 'lat')), parts along dimension 0
The draws below stay inside these ranges and needn't reach their ends.
There are 2 independent parts, one for each index of `groups`. The reference program is written for one: setup_inputs(seed, part) draws one part's arguments, and reference() takes and returns one part's arrays. A program takes and returns all parts, laid end to end along the dimension named above; an argument that names none is the same for every part. Nothing has to cross between parts.
Inputs may be any that keep to these rules, and one draw needn't show every extreme that they name: `indices`: each row names 64 different latents; among the 4 token rows of one device of lat, at most 32 active latents lie in the 512 latents of any one device, and exactly 32 in those of some device.
All inputs are finite; a program needn't handle non-finite values.
Results may differ from the reference program's by a relative error of at most 0.0011.
Values may be sent and summed in bfloat16 or wider, within the bound.
No kernel may reach another device: no remote copies, remote signals or barrier semaphores. Data moves between devices by JAX's collectives and lax.ppermute only.
A program may use at most 128 MiB of HBM per device.

```python
import math
import jax
import jax.numpy as jnp
from jax import lax

D = 4096
LAT_DEV = 512
K = 64
ROW_DEV = 4
ROWS = 64
LATENTS = 8192
CAP = 32


def draw_indices(key, part):
    key = jax.random.fold_in(key, 7)
    shards = LATENTS // LAT_DEV
    blocks = ROWS // ROW_DEV
    per_block = ROW_DEV * K
    key_cap, key_base, key_order, key_shuffle = jax.random.split(key, 4)
    block_ids = lax.iota(jnp.int32, blocks)
    cap_shard = jax.random.randint(key_cap, (blocks,), 0, shards, dtype=jnp.int32)
    cap_shard = jnp.where(block_ids == 0, 0, jnp.where(block_ids == blocks - 1, shards - 1, cap_shard)).astype(jnp.int32)
    bases = jax.random.randint(key_base, (blocks, shards), 0, LAT_DEV, dtype=jnp.int32)
    shard_ids = lax.iota(jnp.int32, shards)
    bases = jnp.where((block_ids[:, None] == 0) & (shard_ids[None, :] == 0), 0, bases)
    bases = jnp.where((block_ids[:, None] == blocks - 1) & (shard_ids[None, :] == shards - 1), LAT_DEV - 1, bases).astype(jnp.int32)
    order_keys = jax.random.split(key_order, blocks)
    orders = jax.vmap(lambda sub: jax.random.permutation(sub, shards - 1))(order_keys).astype(jnp.int32)
    others = (cap_shard[:, None] + 1 + orders) % shards
    slot_ids = lax.iota(jnp.int32, per_block)
    turn = (slot_ids - CAP) % (shards - 1)
    spread = jnp.take_along_axis(others, jnp.broadcast_to(turn[None, :], (blocks, per_block)), axis=1)
    shard_of = jnp.where(slot_ids[None, :] < CAP, cap_shard[:, None], spread).astype(jnp.int32)
    offset = (jnp.take_along_axis(bases, shard_of, axis=1) + slot_ids[None, :]) % LAT_DEV
    latent = (shard_of * LAT_DEV + offset).astype(jnp.int32)
    latent = latent.reshape(blocks, K, ROW_DEV).transpose(0, 2, 1).reshape(ROWS, K)
    shuffle_keys = jax.random.split(key_shuffle, ROWS)
    shuffles = jax.vmap(lambda sub: jax.random.permutation(sub, K))(shuffle_keys).astype(jnp.int32)
    return jnp.take_along_axis(latent, shuffles, axis=1).astype(jnp.int32)


def levels(key, extent, cuts, smallest, high):
    loudness = 1.0
    for dim, shards_of in cuts:
        steps = jax.random.uniform(jax.random.fold_in(jax.random.fold_in(key, 6), dim), (shards_of,), jnp.float32, smallest / len(cuts), high / len(cuts))
        loudness = loudness * jnp.repeat(jnp.exp(steps), extent[dim] // shards_of).reshape((-1,) + (1,) * (len(extent) - 1 - dim))
    return loudness


def centred(own_key, extent, scale, limit, pieces=(), kind=jnp.bfloat16):
    factor_of = levels(own_key, extent, pieces, -0.22, 0.18) if pieces else 1.0
    entries = jax.random.normal(own_key, extent, jnp.float32) * scale * factor_of
    return jnp.minimum(jnp.maximum(entries, -limit), limit).astype(kind)


def setup_inputs(seed: int = 0, part: int = 0) -> dict:
    key_list = jax.random.split(jax.random.key(seed), 5)
    part_splits = jax.random.split(jax.random.fold_in(key_list[4], part), 5)
    return {
        "codes": jnp.clip(jnp.exp(jax.random.uniform(part_splits[0], (ROWS, K), jnp.float32, math.log(0.049804688), math.log(4.0))), 0.049804688, 4.0).astype(jnp.bfloat16),
        "indices": draw_indices(jax.random.fold_in(jax.random.fold_in(key_list[4], part), 71), part),
        "decoder": centred(key_list[2], (LATENTS, 2 * D), K ** -0.5, 0.75, ((0, 16),)),
        "targets": centred(part_splits[3], (ROWS, 2 * D), 1.0, 6.0, ((0, 16),)),
    }


def reference(codes, indices, decoder, targets):
    row_count = codes.shape[0]
    code_blocks = codes.reshape(-1, 16, K)
    index_blocks = indices.reshape(-1, 16, K)

    def decode(packed):
        values, picked = packed
        chosen = decoder[picked].astype(jnp.float32)
        return jnp.einsum('rk,rkc->rc', values.astype(jnp.float32), chosen)

    recon = lax.map(decode, (code_blocks, index_blocks)).reshape(row_count, 2 * D)
    diff = recon - targets.astype(jnp.float32)
    row_loss = jnp.sum(diff * diff, axis=1) / (2 * D)
    error = diff.astype(jnp.bfloat16)

    def backward(packed):
        err_block, picked = packed
        chosen = decoder[picked].astype(jnp.float32)
        return jnp.einsum('rc,rkc->rk', err_block.astype(jnp.float32), chosen)

    code_grad = lax.map(backward, (error.reshape(-1, 16, 2 * D), index_blocks)).reshape(row_count, K)
    return error, row_loss, code_grad
```

```python
import functools

import jax
import jax.numpy as jnp
from jax import lax
from jax.experimental import pallas as pl
from jax.experimental.pallas import tpu as pltpu
from jax.sharding import PartitionSpec as P

CHUNKS = 1
ROW_STEP = 16
VMEM = pl.BlockSpec(memory_space=pltpu.VMEM)
ANY = pl.BlockSpec(memory_space=pl.ANY)


def factors(n):
    c = 2 if n % 2 == 0 else 1
    m = n // c
    y = 1
    while 4 * y * y <= m and m % (2 * y) == 0:
        y *= 2
    return m // y, y, c


def place(n, index):
    _, y, c = factors(n)
    return index // (y * c), (index // c) % y, index % c


def shift(n, dz, dy, dc):
    fz, fy, fc = factors(n)
    pairs = []
    for i in range(n):
        z, y, c = place(n, i)
        to = (((z + dz) % fz) * fy + (y + dy) % fy) * fc + (c + dc) % fc
        pairs.append((i, to))
    return pairs


def cost(flops, size):
    return pl.CostEstimate(flops=flops, bytes_accessed=size, transcendentals=0)


def params():
    return pltpu.CompilerParams(vmem_limit_bytes=48 * 1024 * 1024)


def column_copy(decoder_ref, buf, sem, slot, col, width):
    return pltpu.make_async_copy(
        decoder_ref.at[:, pl.ds(pl.multiple_of(col, width), width)], buf.at[slot], sem.at[slot]
    )


def decode_kernel(n, own, chunk, chunks, dc, first, *refs):
    if first:
        ids_ref, codes_ref, decoder_ref, targets_ref, out_ref, dense_ref, buf, sem = refs
    else:
        dense_ref, decoder_ref, targets_ref, out_ref, buf, sem = refs
    fz, fy, fc = factors(n)
    me = lax.axis_index("lat")
    _, y, c = place(n, me)
    lat_dev = decoder_ref.shape[0]
    sub = buf.shape[2]
    cols = []
    for o in range(fy):
        block = ((c + dc) % fc) * fy + (y + o + 1) % fy
        cols.append((block * chunks + chunk) * sub)
    for o in range(fy):
        column_copy(decoder_ref, buf, sem, o, cols[o], sub).start()
    if first:
        rows, k_count = ids_ref.shape
        lanes = lax.broadcasted_iota(jnp.int32, (ROW_STEP, lat_dev), 1) + me * lat_dev

        def body(g, carry):
            at = pl.ds(pl.multiple_of(g * ROW_STEP, ROW_STEP), ROW_STEP)
            ids = ids_ref[at, :]
            codes = codes_ref[at, :].astype(jnp.float32)
            acc = jnp.zeros((ROW_STEP, lat_dev), jnp.float32)
            for k in range(k_count):
                acc = jnp.where(ids[:, k : k + 1] == lanes, codes[:, k : k + 1], acc)
            dense_ref[at, :] = acc.astype(jnp.bfloat16)
            return carry

        lax.fori_loop(0, rows // ROW_STEP, body, 0)
    rows = dense_ref.shape[0]
    row = lax.broadcasted_iota(jnp.int32, (rows, own), 0)
    want = lax.broadcasted_iota(jnp.int32, (rows, own), 1) + me * own
    mine = jnp.where(row == want, -1.0, 0.0).astype(jnp.bfloat16)
    for o in range(fy):
        column_copy(decoder_ref, buf, sem, o, cols[o], sub).wait()
        part = jnp.dot(dense_ref[...], buf[o], preferred_element_type=jnp.float32)
        tgt = targets_ref[:, pl.ds(pl.multiple_of(cols[o], sub), sub)]
        part += jnp.dot(mine, tgt, preferred_element_type=jnp.float32)
        out_ref[:, o * sub : (o + 1) * sub] = part


def decode(n, own, chunk, chunks, dc, sub, ids, codes, dense, decoder, targets):
    _, fy, _ = factors(n)
    lat_dev = decoder.shape[0]
    first = dense is None
    rows = ids.shape[0]
    out = jax.ShapeDtypeStruct((rows, fy * sub), jnp.float32)
    dense_shape = jax.ShapeDtypeStruct((rows, lat_dev), jnp.bfloat16)
    call = pl.pallas_call(
        functools.partial(decode_kernel, n, own, chunk, chunks, dc, first),
        out_shape=(out, dense_shape) if first else out,
        in_specs=[VMEM, VMEM, ANY, VMEM] if first else [VMEM, ANY, VMEM],
        out_specs=(VMEM, VMEM) if first else VMEM,
        scratch_shapes=[
            pltpu.VMEM((fy, lat_dev, sub), jnp.bfloat16),
            pltpu.SemaphoreType.DMA((fy,)),
        ],
        compiler_params=params(),
        cost_estimate=cost(2 * rows * lat_dev * fy * sub, (2 * lat_dev + 4 * rows) * fy * sub),
        name="decode",
    )
    if first:
        return call(ids, codes, decoder, targets)
    return call(dense, decoder, targets), dense


def grad_kernel(n, blocks, final, with_prev, *refs):
    refs = list(refs)
    errs = [refs.pop(0) for _ in blocks]
    decoder_ref = refs.pop(0)
    prev_ref = refs.pop(0) if with_prev else None
    if final:
        ids_ref, loss_ref, out_ref, buf, sem, totals_ref = refs
    else:
        totals_ref, buf, sem = refs
    fz, fy, fc = factors(n)
    me = lax.axis_index("lat")
    z, y, c = place(n, me)
    sub = buf.shape[2]
    cols = []
    for dc, dy, chunk, chunks in blocks:
        block = ((c + dc) % fc) * fy + (y + fy - dy) % fy
        cols.append((block * chunks + chunk) * sub)
    for i, col in enumerate(cols):
        column_copy(decoder_ref, buf, sem, i, col, sub).start()
    total = prev_ref[...] if with_prev else None
    for i, col in enumerate(cols):
        column_copy(decoder_ref, buf, sem, i, col, sub).wait()
        part = lax.dot_general(
            errs[i][...], buf[i], (((1,), (1,)), ((), ())), preferred_element_type=jnp.float32
        )
        total = part if total is None else total + part
    totals_ref[...] = total
    if final:
        rows, k_count = ids_ref.shape
        lat_dev = decoder_ref.shape[0]
        group = rows // fz
        own = out_ref.shape[1]
        lanes = lax.broadcasted_iota(jnp.int32, (ROW_STEP, lat_dev), 1) + me * lat_dev
        places = lax.broadcasted_iota(jnp.int32, (ROW_STEP, 128), 1)
        steps = group // ROW_STEP
        dests = ROW_STEP // own

        def body(g, carry):
            o, s = g // steps, g % steps
            z_of = (z + fz - o) % fz
            at = pl.multiple_of(z_of * group + s * ROW_STEP, ROW_STEP)
            ids = ids_ref[pl.ds(at, ROW_STEP), :]
            totals = totals_ref[pl.ds(pl.multiple_of(g * ROW_STEP, ROW_STEP), ROW_STEP), :]
            loss = loss_ref[pl.ds(pl.multiple_of(s * ROW_STEP, ROW_STEP), ROW_STEP), :]
            acc = jnp.where((places == k_count) & (o == 0), loss, 0.0)
            for k in range(k_count):
                hit = jnp.where(ids[:, k : k + 1] == lanes, totals, 0.0)
                acc = jnp.where(places == k, jnp.sum(hit, axis=1, keepdims=True), acc)
            for d in range(dests):
                out_ref[at // own + d] = acc[d * own : (d + 1) * own, :]
            return carry

        lax.fori_loop(0, rows // ROW_STEP, body, 0)


def grad(n, blocks, errs, decoder, prev, final=None):
    lat_dev = decoder.shape[0]
    rows, sub = errs[0].shape
    totals = jax.ShapeDtypeStruct((rows, lat_dev), jnp.float32)
    scratch = [
        pltpu.VMEM((len(errs), lat_dev, sub), jnp.bfloat16),
        pltpu.SemaphoreType.DMA((len(errs),)),
    ]
    args = list(errs) + [decoder]
    specs = [VMEM] * len(errs) + [ANY]
    if prev is not None:
        args.append(prev)
        specs.append(VMEM)
    out = totals
    if final is not None:
        args += list(final)
        specs += [VMEM] * len(final)
        out = jax.ShapeDtypeStruct((n, rows // n, 128), jnp.float32)
        scratch.append(pltpu.VMEM(totals.shape, totals.dtype))
    return pl.pallas_call(
        functools.partial(grad_kernel, n, tuple(blocks), final is not None, prev is not None),
        out_shape=out,
        in_specs=specs,
        out_specs=VMEM,
        scratch_shapes=scratch,
        compiler_params=params(),
        cost_estimate=cost(
            2 * rows * lat_dev * sub * len(errs), 2 * (lat_dev + rows) * sub * len(errs)
        ),
        name="grad",
    )(*args)


def own_kernel(n, blocks, own, *refs):
    errs, out_ref = refs[:-1], refs[-1]
    fz, fy, fc = factors(n)
    _, y, c = place(n, lax.axis_index("lat"))
    group, sub = errs[0].shape
    row = lax.broadcasted_iota(jnp.int32, (own, group), 0) + (y * fc + c) * own
    want = lax.broadcasted_iota(jnp.int32, (own, group), 1)
    mine = jnp.where(row == want, 1.0, 0.0).astype(jnp.bfloat16)
    for err, (dc, dy, chunk, chunks) in zip(errs, blocks):
        block = ((c + dc) % fc) * fy + (y + fy - dy) % fy
        col = pl.multiple_of((block * chunks + chunk) * sub, sub)
        rows = jnp.dot(mine, err[...], preferred_element_type=jnp.float32)
        out_ref[:, pl.ds(col, sub)] = rows.astype(jnp.bfloat16)


def own_rows(n, blocks, own, width, errs):
    return pl.pallas_call(
        functools.partial(own_kernel, n, tuple(blocks), own),
        out_shape=jax.ShapeDtypeStruct((own, width), jnp.bfloat16),
        in_specs=[VMEM] * len(errs),
        out_specs=VMEM,
        compiler_params=params(),
        name="own_rows",
    )(*errs)


def local(codes, indices, decoder, targets):
    width = decoder.shape[1]
    rows, k_count = codes.shape
    n = lax.axis_size("lat")
    own = rows // n
    fz, fy, fc = factors(n)
    group = rows // fz
    chunks = CHUNKS
    sub = width // (fc * fy * chunks)
    me = lax.axis_index("lat")
    z, _, _ = place(n, me)

    def send(x, dz=0, dy=0, dc=0):
        return lax.ppermute(x, "lat", shift(n, dz, dy, dc))

    dense = None
    far = {}
    for dc in range(1, fc):
        for p in range(chunks):
            part, dense = decode(n, own, p, chunks, dc, sub, indices, codes, dense, decoder, targets)
            far[dc, p] = send(part, dc=dc)
    kept = []
    for p in range(chunks):
        part, dense = decode(n, own, p, chunks, 0, sub, indices, codes, dense, decoder, targets)
        kept.append(part)

    diffs = []
    for p in range(chunks):
        summed = kept[p]
        for dc in range(1, fc):
            summed = summed + far[dc, p]
        mine = summed[:, (fy - 1) * sub :]
        got = [
            send(summed[:, o * sub : (o + 1) * sub], dy=o + 1) for o in range(fy - 1)
        ]
        for g in got:
            mine = mine + g
        diff = lax.dynamic_slice_in_dim(mine, z * group, group, 0)
        for o in range(1, fz):
            piece = lax.dynamic_slice_in_dim(mine, ((z + o) % fz) * group, group, 0)
            diff = diff + send(piece, dz=o)
        diffs.append(diff)

    loss = sum(jnp.sum(d * d, axis=1, keepdims=True) for d in diffs)

    near, near_blocks, other, other_blocks = [], [], [], []
    for p in range(chunks):
        err = diffs[p].astype(jnp.bfloat16)
        parts = [err] + [send(err, dz=o) for o in range(1, fz)]
        whole = jnp.concatenate(parts, axis=0)
        here = [whole] + [send(whole, dy=o) for o in range(1, fy)]
        for o, e in enumerate(here):
            near.append(e)
            near_blocks.append((0, o, p, chunks))
            for dc in range(1, fc):
                other.append(send(e, dc=dc))
                other_blocks.append((dc, o, p, chunks))

    totals = None
    for e, b in zip(near, near_blocks):
        totals = grad(n, [b], [e], decoder, totals)
    out = grad(n, other_blocks, other, decoder, totals, (indices, loss))
    error = own_rows(
        n, near_blocks + other_blocks, own, width, [e[:group] for e in near + other]
    )

    swapped = lax.all_to_all(out, "lat", 0, 0, tiled=True)
    back = jnp.sum(swapped, axis=0)
    return error, back[:, k_count] / width, back[:, :k_count]


def solution(mesh):
    in_specs = (P("groups", None), P("groups", None), P("lat", None), P(("groups", "lat"), None))
    out_specs = (P(("groups", "lat"), None), P(("groups", "lat")), P(("groups", "lat"), None))
    return jax.shard_map(local, mesh=mesh, in_specs=in_specs, out_specs=out_specs, check_vma=False)
```

```python
import functools

import jax
import jax.numpy as jnp
from jax import lax
from jax.experimental import pallas as pl
from jax.experimental.pallas import tpu as pltpu
from jax.sharding import PartitionSpec as P

CHUNKS = 2
ROW_STEP = 16
LANES = 128
VMEM = pl.BlockSpec(memory_space=pltpu.VMEM)
HBM = pl.BlockSpec(memory_space=pltpu.HBM)


def factors(n):
    c = 2 if n % 2 == 0 else 1
    m = n // c
    y = 1
    while 4 * y * y <= m and m % (2 * y) == 0:
        y *= 2
    return m // y, y, c


def place(n, index):
    _, y, c = factors(n)
    return index // (y * c), (index // c) % y, index % c


def shift(n, dz, dy, dc):
    fz, fy, fc = factors(n)
    pairs = []
    for i in range(n):
        z, y, c = place(n, i)
        to = (((z + dz) % fz) * fy + (y + dy) % fy) * fc + (c + dc) % fc
        pairs.append((i, to))
    return pairs


def cost(flops, size):
    return pl.CostEstimate(flops=flops, bytes_accessed=size, transcendentals=0)


def params():
    return pltpu.CompilerParams(vmem_limit_bytes=24 * 1024 * 1024)


def column_copy(decoder_ref, buf, sem, slot, col, width):
    return pltpu.make_async_copy(
        decoder_ref.at[:, pl.ds(pl.multiple_of(col, width), width)], buf.at[slot], sem.at[slot]
    )


def decode_kernel(n, own, chunk, chunks, dc, first, *refs):
    if first:
        ids_hbm, codes_hbm, decoder_ref, targets_hbm = refs[:4]
        out_ref, buf, dense_ref, sem, ids_ref, codes_ref, targets_ref, small = refs[4:]
    else:
        dense_ref, decoder_ref, targets_ref, out_ref, buf, sem = refs
    fz, fy, fc = factors(n)
    me = lax.axis_index("lat")
    _, y, c = place(n, me)
    lat_dev = decoder_ref.shape[0]
    sub = buf.shape[2]
    cols = []
    for o in range(fy):
        block = ((c + dc) % fc) * fy + (y + o + 1) % fy
        cols.append((block * chunks + chunk) * sub)
    if first:
        pairs = ((ids_hbm, ids_ref), (codes_hbm, codes_ref), (targets_hbm, targets_ref))
        smalls = [pltpu.make_async_copy(a, b, small.at[i]) for i, (a, b) in enumerate(pairs)]
        for copy in smalls:
            copy.start()
    for o in range(fy):
        column_copy(decoder_ref, buf, sem, o, cols[o], sub).start()
    if first:
        for copy in smalls:
            copy.wait()
        rows, k_count = ids_ref.shape
        lanes = lax.broadcasted_iota(jnp.int32, (ROW_STEP, lat_dev), 1) + me * lat_dev

        def body(g, carry):
            at = pl.ds(pl.multiple_of(g * ROW_STEP, ROW_STEP), ROW_STEP)
            ids = ids_ref[at, :]
            codes = codes_ref[at, :].astype(jnp.float32)
            acc = jnp.zeros((ROW_STEP, lat_dev), jnp.float32)
            for k in range(k_count):
                acc = jnp.where(ids[:, k : k + 1] == lanes, codes[:, k : k + 1], acc)
            dense_ref[at, :] = acc.astype(jnp.bfloat16)
            return carry

        lax.fori_loop(0, rows // ROW_STEP, body, 0)
    rows = dense_ref.shape[0]
    row = lax.broadcasted_iota(jnp.int32, (rows, own), 0)
    want = lax.broadcasted_iota(jnp.int32, (rows, own), 1) + me * own
    mine = jnp.where(row == want, -1.0, 0.0).astype(jnp.bfloat16)
    for o in range(fy):
        column_copy(decoder_ref, buf, sem, o, cols[o], sub).wait()
        part = jnp.dot(dense_ref[...], buf[o], preferred_element_type=jnp.float32)
        tgt = targets_ref[:, pl.ds(pl.multiple_of(cols[o], sub), sub)]
        part += jnp.dot(mine, tgt, preferred_element_type=jnp.float32)
        out_ref[:, o * sub : (o + 1) * sub] = part


def decode(n, own, chunk, chunks, dc, sub, ids, codes, dense, decoder, targets):
    _, fy, _ = factors(n)
    lat_dev = decoder.shape[0]
    first = dense is None
    rows = ids.shape[0]
    out = [
        jax.ShapeDtypeStruct((rows, fy * sub), jnp.float32),
        jax.ShapeDtypeStruct((fy, lat_dev, sub), jnp.bfloat16),
    ]
    scratch = [pltpu.SemaphoreType.DMA((fy,))]
    if first:
        out.append(jax.ShapeDtypeStruct((rows, lat_dev), jnp.bfloat16))
        scratch += [pltpu.VMEM(x.shape, x.dtype) for x in (ids, codes, targets)]
        scratch.append(pltpu.SemaphoreType.DMA((3,)))
    got = pl.pallas_call(
        functools.partial(decode_kernel, n, own, chunk, chunks, dc, first),
        out_shape=out,
        in_specs=[HBM, HBM, HBM, HBM] if first else [VMEM, HBM, VMEM],
        out_specs=[VMEM] * len(out),
        scratch_shapes=scratch,
        compiler_params=params(),
        cost_estimate=cost(2 * rows * lat_dev * fy * sub, 4 * lat_dev * fy * sub),
        name="decode",
    )(*((ids, codes, decoder, targets) if first else (dense, decoder, targets)))
    return got[0], got[1], got[2] if first else dense


def grad_kernel(n, slots, final, with_prev, *refs):
    refs = list(refs)
    errs = [refs.pop(0) for _ in slots]
    bufs = [refs.pop(0) for _ in slots]
    prev_ref = refs.pop(0) if with_prev else None
    fz, fy, fc = factors(n)
    me = lax.axis_index("lat")
    z, _, _ = place(n, me)
    total = prev_ref[...] if with_prev else None
    for err, buf, slot in zip(errs, bufs, slots):
        part = lax.dot_general(
            err[...], buf[slot], (((1,), (1,)), ((), ())), preferred_element_type=jnp.float32
        )
        total = part if total is None else total + part
    if not final:
        refs[0][...] = total
        return
    ids_ref, loss_ref, out_ref, totals_ref = refs
    totals_ref[...] = total
    rows, k_count = ids_ref.shape
    lat_dev = total.shape[1]
    group = rows // fz
    steps = group // ROW_STEP
    places = lax.broadcasted_iota(jnp.int32, (ROW_STEP, LANES), 1)
    pad = jnp.zeros((ROW_STEP, LANES - k_count), jnp.int32)

    def body(g, carry):
        at = pl.ds(pl.multiple_of(g * ROW_STEP, ROW_STEP), ROW_STEP)
        ids = jnp.concatenate([ids_ref[at, :] - me * lat_dev, pad], axis=1)
        held = jnp.where(places < k_count, ids // LANES, -1)
        inside = ids % LANES
        loss = loss_ref[pl.ds(pl.multiple_of((g % steps) * ROW_STEP, ROW_STEP), ROW_STEP), :]
        acc = jnp.where((places == k_count) & (g // steps == z), loss, 0.0)
        for t in range(lat_dev // LANES):
            values = totals_ref[at, t * LANES : (t + 1) * LANES]
            found = jnp.take_along_axis(values, inside, axis=1, mode="promise_in_bounds")
            acc = jnp.where(held == t, found, acc)
        out_ref[at, :] = acc
        return carry

    lax.fori_loop(0, rows // ROW_STEP, body, 0)


def grad(n, errs, bufs, slots, prev, final=None):
    lat_dev = bufs[0].shape[1]
    rows, sub = errs[0].shape
    totals = jax.ShapeDtypeStruct((rows, lat_dev), jnp.float32)
    args = list(errs) + list(bufs)
    if prev is not None:
        args.append(prev)
    out, scratch = totals, []
    if final is not None:
        args += list(final)
        out = jax.ShapeDtypeStruct((rows, LANES), jnp.float32)
        scratch.append(pltpu.VMEM(totals.shape, totals.dtype))
    return pl.pallas_call(
        functools.partial(grad_kernel, n, tuple(slots), final is not None, prev is not None),
        out_shape=out,
        in_specs=[VMEM] * len(args),
        out_specs=VMEM,
        scratch_shapes=scratch,
        compiler_params=params(),
        cost_estimate=cost(2 * rows * lat_dev * sub * len(errs), 4 * lat_dev * sub * len(errs)),
        name="grad",
    )(*args)


def own_kernel(n, blocks, own, *refs):
    errs, out_ref = refs[:-1], refs[-1]
    fz, fy, fc = factors(n)
    _, y, c = place(n, lax.axis_index("lat"))
    group, sub = errs[0].shape
    row = lax.broadcasted_iota(jnp.int32, (own, group), 0) + (y * fc + c) * own
    want = lax.broadcasted_iota(jnp.int32, (own, group), 1)
    mine = jnp.where(row == want, 1.0, 0.0).astype(jnp.bfloat16)
    for err, (dc, dy, chunk, chunks) in zip(errs, blocks):
        block = ((c + dc) % fc) * fy + (y + fy - dy) % fy
        col = pl.multiple_of((block * chunks + chunk) * sub, sub)
        rows = jnp.dot(mine, err[...], preferred_element_type=jnp.float32)
        out_ref[:, pl.ds(col, sub)] = rows.astype(jnp.bfloat16)


def own_rows(n, blocks, own, width, errs):
    return pl.pallas_call(
        functools.partial(own_kernel, n, tuple(blocks), own),
        out_shape=jax.ShapeDtypeStruct((own, width), jnp.bfloat16),
        in_specs=[VMEM] * len(errs),
        out_specs=VMEM,
        compiler_params=params(),
        name="own_rows",
    )(*errs)


def local(codes, indices, decoder, targets):
    width = decoder.shape[1]
    rows, k_count = codes.shape
    n = lax.axis_size("lat")
    own = rows // n
    fz, fy, fc = factors(n)
    group = rows // fz
    chunks = CHUNKS
    sub = width // (fc * fy * chunks)
    z, _, _ = place(n, lax.axis_index("lat"))
    columns = [[at + i * fy * fc for i in range(fz)] for at in range(fy * fc)]

    def send(x, dy=0, dc=0):
        return lax.ppermute(x, "lat", shift(n, 0, dy, dc))

    def swap_z(x):
        return lax.all_to_all(x, "lat", 0, 0, axis_index_groups=columns, tiled=True)

    dense = None
    far, kept, bufs = {}, {}, {}
    for dc in list(range(1, fc)) + [0]:
        for p in range(chunks):
            part, bufs[dc, p], dense = decode(
                n, own, p, chunks, dc, sub, indices, codes, dense, decoder, targets
            )
            if dc:
                far[dc, p] = send(part, dc=dc)
            else:
                kept[p] = part

    diffs = []
    for p in range(chunks):
        summed = kept[p]
        for dc in range(1, fc):
            summed = summed + far[dc, p]
        mine = summed[:, (fy - 1) * sub :]
        got = [
            send(summed[:, o * sub : (o + 1) * sub], dy=o + 1) for o in range(fy - 1)
        ]
        for g in got:
            mine = mine + g
        diffs.append(jnp.sum(swap_z(mine).reshape(fz, group, sub), axis=0))

    loss = sum(jnp.sum(d * d, axis=1, keepdims=True) for d in diffs)

    near, near_at, other, other_at = [], [], [], []
    for p in range(chunks):
        err = diffs[p].astype(jnp.bfloat16)
        whole = swap_z(jnp.concatenate([err] * fz, axis=0))
        here = [whole] + [send(whole, dy=o) for o in range(1, fy)]
        for o, e in enumerate(here):
            near.append(e)
            near_at.append((0, o, p, chunks))
            for dc in range(1, fc):
                other.append(send(e, dc=dc))
                other_at.append((dc, o, p, chunks))

    def pieces(at):
        return [bufs[dc, p] for dc, _, p, _ in at], [(fy - 1 - dy) % fy for _, dy, _, _ in at]

    totals = None
    for e, at in zip(near, near_at):
        totals = grad(n, [e], *pieces([at]), totals)
    out = grad(n, other, *pieces(other_at), totals, (indices, loss))
    mine = [lax.dynamic_slice_in_dim(e, z * group, group, 0) for e in near + other]
    error = own_rows(n, near_at + other_at, own, width, mine)

    swapped = lax.all_to_all(out, "lat", 0, 0, tiled=True)
    back = jnp.sum(swapped.reshape(n, own, LANES), axis=0)
    return error, back[:, k_count] / width, back[:, :k_count]


def solution(mesh):
    in_specs = (P("groups", None), P("groups", None), P("lat", None), P(("groups", "lat"), None))
    out_specs = (P(("groups", "lat"), None), P(("groups", "lat")), P(("groups", "lat"), None))
    return jax.shard_map(local, mesh=mesh, in_specs=in_specs, out_specs=out_specs, check_vma=False)
```

```python
import functools

import jax
import jax.numpy as jnp
from jax import lax
from jax.experimental import pallas as pl
from jax.experimental.pallas import tpu as pltpu
from jax.sharding import PartitionSpec as P

CHUNKS = 2
ROW_STEP = 16
LANES = 128
PIECE = 512
VMEM = pl.BlockSpec(memory_space=pltpu.VMEM)
HBM = pl.BlockSpec(memory_space=pltpu.HBM)


def factors(n):
    c = 2 if n % 2 == 0 else 1
    m = n // c
    y = 1
    while 4 * y * y <= m and m % (2 * y) == 0:
        y *= 2
    return m // y, y, c


def place(n, index):
    _, y, c = factors(n)
    return index // (y * c), (index // c) % y, index % c


def partner(z, o, fz):
    return z ^ o if fz & (fz - 1) == 0 else (o - z) % fz


def shift(n, dz, dy, dc):
    fz, fy, fc = factors(n)
    pairs = []
    for i in range(n):
        z, y, c = place(n, i)
        to = (partner(z, dz, fz) * fy + (y + dy) % fy) * fc + (c + dc) % fc
        pairs.append((i, to))
    return pairs


def cost(flops, size):
    return pl.CostEstimate(flops=flops, bytes_accessed=size, transcendentals=0)


def params():
    return pltpu.CompilerParams(vmem_limit_bytes=24 * 1024 * 1024)


def in_hbm(x):
    return pltpu.with_memory_space_constraint(x, pltpu.HBM)


def column_copy(decoder_ref, buf, sem, slot, piece, col, width):
    at = piece * width
    return pltpu.make_async_copy(
        decoder_ref.at[:, pl.ds(pl.multiple_of(col + at, width), width)],
        buf.at[slot, :, pl.ds(at, width)],
        sem.at[slot, piece],
    )


def decode_kernel(n, own, chunk, chunks, dc, first, *refs):
    if first:
        ids_hbm, codes_hbm, decoder_ref, targets_hbm = refs[:4]
        out_ref, buf, dense_ref, sem, ids_ref, codes_ref, targets_ref, small = refs[4:]
    else:
        dense_ref, decoder_ref, targets_ref, out_ref, buf, sem = refs
    fz, fy, fc = factors(n)
    me = lax.axis_index("lat")
    _, y, c = place(n, me)
    lat_dev = decoder_ref.shape[0]
    sub = buf.shape[2]
    cols = []
    for o in range(fy):
        block = ((c + dc) % fc) * fy + (y + o + 1) % fy
        cols.append((block * chunks + chunk) * sub)
    if first:
        pairs = ((ids_hbm, ids_ref), (codes_hbm, codes_ref), (targets_hbm, targets_ref))
        smalls = [pltpu.make_async_copy(a, b, small.at[i]) for i, (a, b) in enumerate(pairs)]
        for copy in smalls:
            copy.start()
    width = min(sub, PIECE)
    for o in range(fy):
        for i in range(sub // width):
            column_copy(decoder_ref, buf, sem, o, i, cols[o], width).start()
    if first:
        for copy in smalls:
            copy.wait()
        rows, k_count = ids_ref.shape
        lanes = lax.broadcasted_iota(jnp.int32, (ROW_STEP, lat_dev), 1) + me * lat_dev

        def body(g, carry):
            at = pl.ds(pl.multiple_of(g * ROW_STEP, ROW_STEP), ROW_STEP)
            ids = ids_ref[at, :]
            codes = codes_ref[at, :].astype(jnp.float32)
            acc = jnp.zeros((ROW_STEP, lat_dev), jnp.float32)
            for k in range(k_count):
                acc = jnp.where(ids[:, k : k + 1] == lanes, codes[:, k : k + 1], acc)
            dense_ref[at, :] = acc.astype(jnp.bfloat16)
            return carry

        lax.fori_loop(0, rows // ROW_STEP, body, 0)
    rows = dense_ref.shape[0]
    row = lax.broadcasted_iota(jnp.int32, (rows, own), 0)
    want = lax.broadcasted_iota(jnp.int32, (rows, own), 1) + me * own
    mine = jnp.where(row == want, -1.0, 0.0).astype(jnp.bfloat16)
    for o in range(fy):
        for i in range(sub // width):
            column_copy(decoder_ref, buf, sem, o, i, cols[o], width).wait()
            at = i * width
            tgt = targets_ref[:, pl.ds(pl.multiple_of(cols[o] + at, width), width)]
            part = jnp.dot(
                dense_ref[...], buf[o, :, at : at + width], preferred_element_type=jnp.float32
            )
            part += jnp.dot(mine, tgt, preferred_element_type=jnp.float32)
            out_ref[:, o * sub + at : o * sub + at + width] = part


def decode(n, own, chunk, chunks, dc, sub, ids, codes, dense, decoder, targets):
    _, fy, _ = factors(n)
    lat_dev = decoder.shape[0]
    first = dense is None
    rows = ids.shape[0]
    out = [
        pltpu.VMEM((rows, fy * sub), jnp.float32),
        pltpu.VMEM((fy, lat_dev, sub), jnp.bfloat16),
    ]
    scratch = [pltpu.SemaphoreType.DMA((fy, sub // min(sub, PIECE)))]
    if first:
        out.append(pltpu.VMEM((rows, lat_dev), jnp.bfloat16))
        scratch += [pltpu.VMEM(x.shape, x.dtype) for x in (ids, codes, targets)]
        scratch.append(pltpu.SemaphoreType.DMA((3,)))
    decoder = in_hbm(decoder)
    if first:
        ids, codes, targets = in_hbm(ids), in_hbm(codes), in_hbm(targets)
    got = pl.pallas_call(
        functools.partial(decode_kernel, n, own, chunk, chunks, dc, first),
        out_shape=out,
        in_specs=[HBM, HBM, HBM, HBM] if first else [VMEM, HBM, VMEM],
        out_specs=[VMEM] * len(out),
        scratch_shapes=scratch,
        compiler_params=params(),
        cost_estimate=cost(2 * rows * lat_dev * fy * sub, 4 * lat_dev * fy * sub),
        name="decode",
    )(*((ids, codes, decoder, targets) if first else (dense, decoder, targets)))
    return got[0], got[1], got[2] if first else dense


def grad_kernel(n, slots, final, with_prev, *refs):
    refs = list(refs)
    errs = [refs.pop(0) for _ in slots]
    bufs = [refs.pop(0) for _ in slots]
    prev_ref = refs.pop(0) if with_prev else None
    fz, fy, fc = factors(n)
    me = lax.axis_index("lat")
    z, _, _ = place(n, me)
    total = prev_ref[...] if with_prev else None
    for err, buf, slot in zip(errs, bufs, slots):
        part = lax.dot_general(
            err[...], buf[slot], (((1,), (1,)), ((), ())), preferred_element_type=jnp.float32
        )
        total = part if total is None else total + part
    if not final:
        refs[0][...] = total
        return
    ids_ref, loss_ref, out_ref, totals_ref = refs
    totals_ref[...] = total
    rows, k_count = ids_ref.shape
    lat_dev = total.shape[1]
    group = rows // fz
    steps = group // ROW_STEP
    places = lax.broadcasted_iota(jnp.int32, (ROW_STEP, LANES), 1)
    pad = jnp.zeros((ROW_STEP, LANES - k_count), jnp.int32)

    def body(g, carry):
        here = pl.ds(pl.multiple_of(g * ROW_STEP, ROW_STEP), ROW_STEP)
        first = partner(z, g // steps, fz) * group + (g % steps) * ROW_STEP
        at = pl.ds(pl.multiple_of(first, ROW_STEP), ROW_STEP)
        ids = jnp.concatenate([ids_ref[at, :] - me * lat_dev, pad], axis=1)
        held = jnp.where(places < k_count, ids // LANES, -1)
        inside = ids % LANES
        loss = loss_ref[pl.ds(pl.multiple_of((g % steps) * ROW_STEP, ROW_STEP), ROW_STEP), :]
        acc = jnp.where((places == k_count) & (g // steps == 0), loss, 0.0)
        for t in range(lat_dev // LANES):
            values = totals_ref[here, t * LANES : (t + 1) * LANES]
            found = jnp.take_along_axis(values, inside, axis=1, mode="promise_in_bounds")
            acc = jnp.where(held == t, found, acc)
        out_ref[at, :] = acc
        return carry

    lax.fori_loop(0, rows // ROW_STEP, body, 0)


def grad(n, errs, bufs, slots, prev, final=None):
    lat_dev = bufs[0].shape[1]
    rows, sub = errs[0].shape
    totals = jax.ShapeDtypeStruct((rows, lat_dev), jnp.float32)
    args = list(errs) + list(bufs)
    if prev is not None:
        args.append(prev)
    out, scratch = totals, []
    if final is not None:
        args += list(final)
        out = jax.ShapeDtypeStruct((rows, LANES), jnp.float32)
        scratch.append(pltpu.VMEM(totals.shape, totals.dtype))
    return pl.pallas_call(
        functools.partial(grad_kernel, n, tuple(slots), final is not None, prev is not None),
        out_shape=out,
        in_specs=[VMEM] * len(args),
        out_specs=VMEM,
        scratch_shapes=scratch,
        compiler_params=params(),
        cost_estimate=cost(2 * rows * lat_dev * sub * len(errs), 4 * lat_dev * sub * len(errs)),
        name="grad",
    )(*args)


def own_kernel(n, blocks, own, *refs):
    errs, out_ref = refs[:-1], refs[-1]
    fz, fy, fc = factors(n)
    _, y, c = place(n, lax.axis_index("lat"))
    group, sub = errs[0].shape
    row = lax.broadcasted_iota(jnp.int32, (own, group), 0) + (y * fc + c) * own
    want = lax.broadcasted_iota(jnp.int32, (own, group), 1)
    mine = jnp.where(row == want, 1.0, 0.0).astype(jnp.bfloat16)
    for err, (dc, dy, chunk, chunks) in zip(errs, blocks):
        block = ((c + dc) % fc) * fy + (y + fy - dy) % fy
        col = pl.multiple_of((block * chunks + chunk) * sub, sub)
        rows = jnp.dot(mine, err[...], preferred_element_type=jnp.float32)
        out_ref[:, pl.ds(col, sub)] = rows.astype(jnp.bfloat16)


def own_rows(n, blocks, own, width, errs):
    return pl.pallas_call(
        functools.partial(own_kernel, n, tuple(blocks), own),
        out_shape=jax.ShapeDtypeStruct((own, width), jnp.bfloat16),
        in_specs=[VMEM] * len(errs),
        out_specs=VMEM,
        compiler_params=params(),
        name="own_rows",
    )(*errs)


def local(codes, indices, decoder, targets):
    width = decoder.shape[1]
    rows, k_count = codes.shape
    n = lax.axis_size("lat")
    own = rows // n
    fz, fy, fc = factors(n)
    group = rows // fz
    chunks = CHUNKS
    sub = width // (fc * fy * chunks)
    z, _, _ = place(n, lax.axis_index("lat"))
    zs = [z] + [partner(z, o, fz) for o in range(1, fz)]

    def send(x, dz=0, dy=0, dc=0):
        return lax.ppermute(x, "lat", shift(n, dz, dy, dc))

    def z_rows(x, o):
        return lax.dynamic_slice_in_dim(x, zs[o] * group, group, 0)

    dense = None
    bufs, summed = {}, []
    for p in range(chunks):
        parts = {}
        for dc in list(range(1, fc)) + [0]:
            parts[dc], bufs[dc, p], dense = decode(
                n, own, p, chunks, dc, sub, indices, codes, dense, decoder, targets
            )
            if dc:
                parts[dc] = send(parts[dc], dc=dc)
        total = sum(parts[dc] for dc in range(1, fc)) + parts[0] if fc > 1 else parts[0]
        mine = total[:, (fy - 1) * sub :]
        go = [total[:, o * sub : (o + 1) * sub] for o in range(fy - 1)]
        dense, go = lax.optimization_barrier((dense, go))
        for o in range(fy - 1):
            mine = mine + send(go[o], dy=o + 1)
        summed.append(mine)

    diffs = []
    for mine in summed:
        diff = z_rows(mine, 0)
        for o in range(1, fz):
            diff = diff + send(z_rows(mine, o), dz=o)
        diffs.append(diff)

    loss = sum(jnp.sum(d * d, axis=1, keepdims=True) for d in diffs)

    near, near_at, other, other_at = [], [], [], []
    for p in range(chunks):
        err = diffs[p].astype(jnp.bfloat16)
        whole = jnp.concatenate([err] + [send(err, dz=o) for o in range(1, fz)], axis=0)
        here = [whole] + [send(whole, dy=o) for o in range(1, fy)]
        for o, e in enumerate(here):
            near.append(e)
            near_at.append((0, o, p, chunks))
            for dc in range(1, fc):
                other.append(send(e, dc=dc))
                other_at.append((dc, o, p, chunks))

    def pieces(at):
        return [bufs[dc, p] for dc, _, p, _ in at], [(fy - 1 - dy) % fy for _, dy, _, _ in at]

    totals = None
    for e, at in zip(near, near_at):
        totals = grad(n, [e], *pieces([at]), totals)
    out = grad(n, other, *pieces(other_at), totals, (indices, loss))
    error = own_rows(n, near_at + other_at, own, width, [e[:group] for e in near + other])

    swapped = lax.all_to_all(out, "lat", 0, 0, tiled=True)
    back = jnp.sum(swapped.reshape(n, own, LANES), axis=0)
    return error, back[:, k_count] / width, back[:, :k_count]


def solution(mesh):
    in_specs = (P("groups", None), P("groups", None), P("lat", None), P(("groups", "lat"), None))
    out_specs = (P(("groups", "lat"), None), P(("groups", "lat")), P(("groups", "lat"), None))
    return jax.shard_map(local, mesh=mesh, in_specs=in_specs, out_specs=out_specs, check_vma=False)
```

```python
import functools

import jax
import jax.numpy as jnp
from jax import lax
from jax.experimental import pallas as pl
from jax.experimental.pallas import tpu as pltpu
from jax.sharding import PartitionSpec as P

CHUNKS = 2
ROW_STEP = 16
LANES = 128
VMEM = pl.BlockSpec(memory_space=pltpu.VMEM)
HBM = pl.BlockSpec(memory_space=pltpu.HBM)
ANY = pl.BlockSpec(memory_space=pl.ANY)


def factors(n):
    assert n & (n - 1) == 0
    c = min(n, 2)
    m = n // c
    y = 1
    while 4 * y * y <= m:
        y *= 2
    return m // y, y, c


def place(n, index):
    _, y, c = factors(n)
    return index // (y * c), (index // c) % y, index % c


def bits(size):
    return [1 << i for i in range(size.bit_length() - 1)]


def z_order(fz):
    order = [0]
    for b in reversed(bits(fz)):
        order += [j | b for j in order]
    return order


def pairs(n, dz, dy, dc):
    _, fy, fc = factors(n)
    out = []
    for i in range(n):
        z, y, c = place(n, i)
        out.append((i, ((z ^ dz) * fy + (y ^ dy)) * fc + (c ^ dc)))
    return out


def cost(flops, size):
    return pl.CostEstimate(flops=flops, bytes_accessed=size, transcendentals=0)


def params():
    return pltpu.CompilerParams(vmem_limit_bytes=24 * 1024 * 1024)


def in_hbm(x):
    return pltpu.with_memory_space_constraint(x, pltpu.HBM)


def column(n, chunk, chunks, sub, dy, dc):
    _, fy, fc = factors(n)
    _, y, c = place(n, lax.axis_index("lat"))
    return pl.multiple_of((((c ^ dc) * fy + (y ^ dy)) * chunks + chunk) * sub, sub)


def partial_sums(n, own, cols, dense_ref, targets_ref, buf, out_ref):
    rows = dense_ref.shape[0]
    sub = buf.shape[2]
    row = lax.broadcasted_iota(jnp.int32, (rows, own), 0)
    want = lax.broadcasted_iota(jnp.int32, (rows, own), 1) + lax.axis_index("lat") * own
    mine = jnp.where(row == want, -1.0, 0.0).astype(jnp.bfloat16)
    for o, col in enumerate(cols):
        part = jnp.dot(dense_ref[...], buf[o], preferred_element_type=jnp.float32)
        part += jnp.dot(
            mine, targets_ref[:, pl.ds(col, sub)], preferred_element_type=jnp.float32
        )
        out_ref[:, o * sub : (o + 1) * sub] = part


def first_kernel(n, own, chunks, order, *refs):
    fz, fy, fc = factors(n)
    ids_hbm, codes_hbm, decoder_hbm, targets_hbm = refs[:4]
    out_ref, dense_ref, targets_ref = refs[4:7]
    kept = len(order) - 1
    bufs = refs[7 : 7 + kept]
    buf, ids_ref, codes_ref, small, sem = refs[7 + kept :]
    bufs = (buf,) + tuple(bufs)
    me = lax.axis_index("lat")
    lat_dev = decoder_hbm.shape[0]
    sub = buf.shape[2]
    smalls = [
        pltpu.make_async_copy(a, b, small.at[i])
        for i, (a, b) in enumerate(
            ((ids_hbm, ids_ref), (codes_hbm, codes_ref), (targets_hbm, targets_ref))
        )
    ]
    for copy in smalls:
        copy.start()
    cols = [[column(n, p, chunks, sub, o, dc) for o in range(fy)] for p, dc in order]
    loads = [
        [
            pltpu.make_async_copy(
                decoder_hbm.at[:, pl.ds(cols[i][o], sub)], bufs[i].at[o], sem.at[i, o]
            )
            for o in range(fy)
        ]
        for i in range(len(order))
    ]
    for group in loads:
        for copy in group:
            copy.start()
    for copy in smalls:
        copy.wait()
    rows, k_count = ids_ref.shape
    lanes = lax.broadcasted_iota(jnp.int32, (ROW_STEP, lat_dev), 1) + me * lat_dev

    def body(g, carry):
        at = pl.ds(pl.multiple_of(g * ROW_STEP, ROW_STEP), ROW_STEP)
        ids = ids_ref[at, :]
        codes = codes_ref[at, :].astype(jnp.float32)
        acc = jnp.zeros((ROW_STEP, lat_dev), jnp.float32)
        for k in range(k_count):
            acc = jnp.where(ids[:, k : k + 1] == lanes, codes[:, k : k + 1], acc)
        dense_ref[at, :] = acc.astype(jnp.bfloat16)
        return carry

    lax.fori_loop(0, rows // ROW_STEP, body, 0)
    for copy in loads[0]:
        copy.wait()
    partial_sums(n, own, cols[0], dense_ref, targets_ref, buf, out_ref)
    for group in loads[1:]:
        for copy in group:
            copy.wait()


def first_decode(n, chunks, order, sub, ids, codes, decoder, targets):
    _, fy, _ = factors(n)
    lat_dev = decoder.shape[0]
    rows = ids.shape[0]
    columns = (fy, lat_dev, sub)
    args = (ids, codes, decoder, targets)
    return pl.pallas_call(
        functools.partial(first_kernel, n, rows // n, chunks, order),
        out_shape=[
            pltpu.VMEM((rows, fy * sub), jnp.float32),
            pltpu.VMEM((rows, lat_dev), jnp.bfloat16),
            pltpu.VMEM(targets.shape, targets.dtype),
        ]
        + [pltpu.VMEM(columns, jnp.bfloat16)] * (len(order) - 1),
        in_specs=[HBM] * 4,
        out_specs=[VMEM] * (2 + len(order)),
        scratch_shapes=[
            pltpu.VMEM(columns, jnp.bfloat16),
            pltpu.VMEM(ids.shape, ids.dtype),
            pltpu.VMEM(codes.shape, codes.dtype),
            pltpu.SemaphoreType.DMA((3,)),
            pltpu.SemaphoreType.DMA((len(order), fy)),
        ],
        compiler_params=params(),
        cost_estimate=cost(2 * rows * lat_dev * fy * sub, decoder.size * 2),
        name="first_decode",
    )(*[in_hbm(x) for x in args])


def decode_kernel(n, own, chunk, chunks, dc, dense_ref, targets_ref, buf, _, out_ref):
    sub = buf.shape[2]
    cols = [column(n, chunk, chunks, sub, o, dc) for o in range(buf.shape[0])]
    partial_sums(n, own, cols, dense_ref, targets_ref, buf, out_ref)


def decode(n, chunk, chunks, dc, dense, targets, buf, after):
    rows, lat_dev = dense.shape
    fy, _, sub = buf.shape
    return pl.pallas_call(
        functools.partial(decode_kernel, n, rows // n, chunk, chunks, dc),
        out_shape=pltpu.VMEM((rows, fy * sub), jnp.float32),
        in_specs=[VMEM, VMEM, VMEM, ANY],
        out_specs=VMEM,
        compiler_params=params(),
        cost_estimate=cost(2 * rows * lat_dev * fy * sub, 3 * lat_dev * fy * sub),
        name="decode",
    )(dense, targets, buf, after)


def grad_kernel(n, at, final, with_prev, *refs):
    refs = list(refs)
    err_ref, decoder_ref = refs.pop(0), refs.pop(0)
    prev_ref = refs.pop(0) if with_prev else None
    sub = err_ref.shape[1]
    dc, dy, chunk, chunks = at
    col = column(n, chunk, chunks, sub, dy, dc)
    total = lax.dot_general(
        err_ref[...],
        decoder_ref[:, pl.ds(col, sub)],
        (((1,), (1,)), ((), ())),
        preferred_element_type=jnp.float32,
    )
    if with_prev:
        total += prev_ref[...]
    if not final:
        refs[0][...] = total
        return
    ids_ref, loss_ref, out_ref, totals_ref = refs
    totals_ref[...] = total
    rows, k_count = ids_ref.shape
    lat_dev = total.shape[1]
    own = out_ref.shape[1]
    fz, fy, fc = factors(n)
    me = lax.axis_index("lat")
    z, y, c = place(n, me)
    group = rows // fz
    places = lax.broadcasted_iota(jnp.int32, (ROW_STEP, LANES), 1)
    pad = jnp.zeros((ROW_STEP, LANES - k_count), jnp.int32)
    for q, j in enumerate(z_order(fz)):
        for s in range(0, group, ROW_STEP):
            rows_at = pl.ds(pl.multiple_of((z ^ j) * group + s, ROW_STEP), ROW_STEP)
            ids = jnp.concatenate([ids_ref[rows_at, :] - me * lat_dev, pad], axis=1)
            held = jnp.where(places < k_count, ids // LANES, -1)
            inside = ids % LANES
            acc = jnp.zeros((ROW_STEP, LANES), jnp.float32)
            if q == 0:
                acc = jnp.where(places == k_count, loss_ref[s : s + ROW_STEP, :], acc)
            for t in range(lat_dev // LANES):
                values = totals_ref[q * group + s : q * group + s + ROW_STEP, t * LANES : (t + 1) * LANES]
                found = jnp.take_along_axis(values, inside, axis=1, mode="promise_in_bounds")
                acc = jnp.where(held == t, found, acc)
            for d in range(ROW_STEP // own):
                to = s // own + d
                index = ((c ^ (to % fc)) * fy + (y ^ (to // fc))) * fz + q
                out_ref[index] = acc[d * own : (d + 1) * own, :]


def grad(n, at, err, decoder, prev, final=None):
    lat_dev = decoder.shape[0]
    rows, sub = err.shape
    args = [err, decoder]
    if prev is not None:
        args.append(prev)
    out, scratch = jax.ShapeDtypeStruct((rows, lat_dev), jnp.float32), []
    if final is not None:
        args += list(final)
        scratch.append(pltpu.VMEM(out.shape, out.dtype))
        out = jax.ShapeDtypeStruct((n, rows // n, LANES), jnp.float32)
    return pl.pallas_call(
        functools.partial(grad_kernel, n, at, final is not None, prev is not None),
        out_shape=out,
        in_specs=[VMEM] * len(args),
        out_specs=VMEM,
        scratch_shapes=scratch,
        compiler_params=params(),
        cost_estimate=cost(2 * rows * lat_dev * sub, 3 * lat_dev * sub),
        name="grad",
    )(*args)


def own_kernel(n, blocks, own, *refs):
    errs, out_ref = refs[:-1], refs[-1]
    _, fy, fc = factors(n)
    _, y, c = place(n, lax.axis_index("lat"))
    group, sub = errs[0].shape
    row = lax.broadcasted_iota(jnp.int32, (own, group), 0) + (y * fc + c) * own
    want = lax.broadcasted_iota(jnp.int32, (own, group), 1)
    mine = jnp.where(row == want, 1.0, 0.0).astype(jnp.bfloat16)
    for err, (dc, dy, chunk, chunks) in zip(errs, blocks):
        rows = jnp.dot(mine, err[...], preferred_element_type=jnp.float32)
        out_ref[:, pl.ds(column(n, chunk, chunks, sub, dy, dc), sub)] = rows.astype(jnp.bfloat16)


def own_rows(n, blocks, own, width, errs):
    return pl.pallas_call(
        functools.partial(own_kernel, n, tuple(blocks), own),
        out_shape=jax.ShapeDtypeStruct((own, width), jnp.bfloat16),
        in_specs=[VMEM] * len(errs),
        out_specs=VMEM,
        compiler_params=params(),
        name="own_rows",
    )(*errs)


def local(codes, indices, decoder, targets):
    width = decoder.shape[1]
    rows, k_count = codes.shape
    n = lax.axis_size("lat")
    own = rows // n
    fz, fy, fc = factors(n)
    group = rows // fz
    chunks = CHUNKS
    sub = width // (fc * fy * chunks)
    z, _, _ = place(n, lax.axis_index("lat"))

    def swap(x, dz=0, dy=0, dc=0):
        return lax.ppermute(x, "lat", pairs(n, dz, dy, dc))

    def join(xs, axis):
        return xs[0] if len(xs) == 1 else jnp.concatenate(xs, axis=axis)

    order = tuple((p, dc) for p in range(chunks) for dc in reversed(range(fc)))
    part, dense, tgt, *bufs = first_decode(
        n, chunks, order, sub, indices, codes, decoder, targets
    )
    summed, after = [], part
    for p in range(chunks):
        total = None
        for dc in reversed(range(fc)):
            i = order.index((p, dc))
            if i:
                part = decode(n, p, chunks, dc, dense, tgt, bufs[i - 1], after)
                after = part
            got = swap(part, dc=dc) if dc else part
            total = got if total is None else total + got
        blocks = [total[:, o * sub : (o + 1) * sub] for o in range(fy)]
        for b in reversed(bits(fy)):
            go = join(blocks[b:], 1)
            after = go
            got = swap(go, dy=b)
            blocks = [blocks[o] + got[:, o * sub : (o + 1) * sub] for o in range(b)]
        summed.append(blocks[0])

    diffs = []
    for mine in summed:
        blocks = {
            j: lax.dynamic_slice_in_dim(mine, (z ^ j) * group, group, 0) for j in range(fz)
        }
        for b in bits(fz):
            going = [j for j in blocks if j & b]
            got = swap(join([blocks[j] for j in going], 0), dz=b)
            blocks = {
                j ^ b: blocks[j ^ b] + got[i * group : (i + 1) * group]
                for i, j in enumerate(going)
            }
        diffs.append(blocks[0])

    loss = sum(jnp.sum(d * d, axis=1, keepdims=True) for d in diffs)

    pieces = []
    for p in range(chunks):
        whole = diffs[p].astype(jnp.bfloat16)
        for b in reversed(bits(fz)):
            whole = join([whole, swap(whole, dz=b)], 0)
        here = [whole]
        for b in bits(fy):
            here += [swap(e, dy=b) for e in here]
        for dc in range(fc):
            for dy, e in enumerate(here):
                pieces.append(((dc, dy, p, chunks), swap(e, dc=dc) if dc else e))

    totals = None
    for at, e in pieces[:-1]:
        totals = grad(n, at, e, decoder, totals)
    back = grad(n, *pieces[-1], decoder, totals, (indices, loss))
    error = own_rows(n, [at for at, _ in pieces], own, width, [e[:group] for _, e in pieces])

    steps = [dict(dc=b) for b in reversed(bits(fc))] + [dict(dy=b) for b in reversed(bits(fy))]
    for step in steps + [dict(dz=b) for b in bits(fz)]:
        half = back.shape[0] // 2
        back = back[:half] + swap(back[half:], **step)
    back = back[0]
    return error, back[:, k_count] / width, back[:, :k_count]


def solution(mesh):
    in_specs = (P("groups", None), P("groups", None), P("lat", None), P(("groups", "lat"), None))
    out_specs = (P(("groups", "lat"), None), P(("groups", "lat")), P(("groups", "lat"), None))
    return jax.shard_map(local, mesh=mesh, in_specs=in_specs, out_specs=out_specs, check_vma=False)
```

```python
import functools

import jax
import jax.numpy as jnp
from jax import lax
from jax.experimental import pallas as pl
from jax.experimental.pallas import tpu as pltpu
from jax.sharding import PartitionSpec as P

CHUNKS = 2
ROW_STEP = 16
LANES = 128
VMEM = pl.BlockSpec(memory_space=pltpu.VMEM)
HBM = pl.BlockSpec(memory_space=pltpu.HBM)
ANY = pl.BlockSpec(memory_space=pl.ANY)


def factors(n):
    assert n & (n - 1) == 0
    c = min(n, 2)
    m = n // c
    y = 1
    while 4 * y * y <= m:
        y *= 2
    return m // y, y, c


def place(n, index):
    _, y, c = factors(n)
    return index // (y * c), (index // c) % y, index % c


def bits(size):
    return [1 << i for i in range(size.bit_length() - 1)]


def pairs(n, dz, dy, dc):
    _, fy, fc = factors(n)
    out = []
    for i in range(n):
        z, y, c = place(n, i)
        out.append((i, ((z ^ dz) * fy + (y ^ dy)) * fc + (c ^ dc)))
    return out


def cost(flops, size):
    return pl.CostEstimate(flops=flops, bytes_accessed=size, transcendentals=0)


def params():
    return pltpu.CompilerParams(vmem_limit_bytes=24 * 1024 * 1024)


def in_hbm(x):
    return pltpu.with_memory_space_constraint(x, pltpu.HBM)


def column(n, chunk, chunks, sub, dy, dc):
    _, fy, fc = factors(n)
    _, y, c = place(n, lax.axis_index("lat"))
    return pl.multiple_of((((c ^ dc) * fy + (y ^ dy)) * chunks + chunk) * sub, sub)


def hold(x, *after):
    return pl.pallas_call(
        lambda *refs: None,
        out_shape=jax.ShapeDtypeStruct(x.shape, x.dtype),
        in_specs=[ANY] * (1 + len(after)),
        out_specs=ANY,
        input_output_aliases={0: 0},
        name="hold",
    )(x, *after)


def load(decoder_hbm, col, buf, sem):
    return pltpu.make_async_copy(decoder_hbm.at[:, pl.ds(col, buf.shape[1])], buf, sem)


def decode_kernel(n, own, chunk, chunks, first, *refs):
    fz, fy, fc = factors(n)
    me = lax.axis_index("lat")
    if first:
        ids_hbm, codes_hbm, decoder_hbm, targets_hbm = refs[:4]
        outs, dense_ref = refs[4 : 4 + fc], refs[4 + fc]
        buf, sem, targets_ref, small, ids_ref, codes_ref = refs[5 + fc :]
        pairs_in = ((ids_hbm, ids_ref), (codes_hbm, codes_ref), (targets_hbm, targets_ref))
    else:
        dense_ref, decoder_hbm, targets_hbm, _ = refs[:4]
        outs = refs[4 : 4 + fc]
        buf, sem, targets_ref, small = refs[4 + fc :]
        pairs_in = ((targets_hbm, targets_ref),)
    sub = buf.shape[3]
    smalls = [pltpu.make_async_copy(a, b, small.at[i]) for i, (a, b) in enumerate(pairs_in)]
    for copy in smalls:
        copy.start()
    blocks = [(dc, o) for dc in reversed(range(fc)) for o in reversed(range(fy))]
    cols = {at: column(n, chunk, chunks, sub, at[1], at[0]) for at in blocks}
    loads = {at: load(decoder_hbm, cols[at], buf.at[at], sem.at[at]) for at in blocks}
    for at in blocks:
        loads[at].start()
    for copy in smalls:
        copy.wait()
    if first:
        rows, k_count = ids_ref.shape
        lat_dev = decoder_hbm.shape[0]
        lanes = lax.broadcasted_iota(jnp.int32, (ROW_STEP, lat_dev), 1) + me * lat_dev

        def body(g, carry):
            at = pl.ds(pl.multiple_of(g * ROW_STEP, ROW_STEP), ROW_STEP)
            ids = ids_ref[at, :]
            codes = codes_ref[at, :].astype(jnp.float32)
            acc = jnp.zeros((ROW_STEP, lat_dev), jnp.float32)
            for k in range(k_count):
                acc = jnp.where(ids[:, k : k + 1] == lanes, codes[:, k : k + 1], acc)
            dense_ref[at, :] = acc.astype(jnp.bfloat16)
            return carry

        lax.fori_loop(0, rows // ROW_STEP, body, 0)
    rows = dense_ref.shape[0]
    row = lax.broadcasted_iota(jnp.int32, (rows, own), 0)
    want = lax.broadcasted_iota(jnp.int32, (rows, own), 1) + me * own
    mine = jnp.where(row == want, -1.0, 0.0).astype(jnp.bfloat16)
    for dc, o in blocks:
        loads[dc, o].wait()
        part = jnp.dot(dense_ref[...], buf[dc, o], preferred_element_type=jnp.float32)
        part += jnp.dot(
            mine, targets_ref[:, pl.ds(cols[dc, o], sub)], preferred_element_type=jnp.float32
        )
        outs[dc][:, o * sub : (o + 1) * sub] = part


def decode(n, chunk, chunks, sub, ids, codes, dense, decoder, targets, after):
    _, fy, fc = factors(n)
    rows, lat_dev = ids.shape[0], decoder.shape[0]
    first = dense is None
    out = [pltpu.VMEM((rows, fy * sub), jnp.float32)] * fc
    scratch = [
        pltpu.VMEM((fc, fy, lat_dev, sub), jnp.bfloat16),
        pltpu.SemaphoreType.DMA((fc, fy)),
        pltpu.VMEM(targets.shape, targets.dtype),
        pltpu.SemaphoreType.DMA((3,)),
    ]
    if first:
        out.append(pltpu.VMEM((rows, lat_dev), jnp.bfloat16))
        scratch += [pltpu.VMEM(x.shape, x.dtype) for x in (ids, codes)]
        args, specs = [in_hbm(x) for x in (ids, codes, decoder, targets)], [HBM] * 4
    else:
        args = [dense, in_hbm(decoder), in_hbm(targets), after]
        specs = [VMEM, HBM, HBM, ANY]
    got = pl.pallas_call(
        functools.partial(decode_kernel, n, rows // n, chunk, chunks, first),
        out_shape=out,
        in_specs=specs,
        out_specs=[VMEM] * len(out),
        scratch_shapes=scratch,
        compiler_params=params(),
        cost_estimate=cost(2 * rows * lat_dev * fc * fy * sub, 4 * lat_dev * fc * fy * sub),
        name="decode",
    )(*args)
    return got[:fc], got[fc] if first else dense


def grad_kernel(n, blocks, after, final, with_prev, *refs):
    refs = list(refs)
    errs = [refs.pop(0) for _ in blocks]
    decoder_ref = refs.pop(0)
    prev_ref = refs.pop(0) if with_prev else None
    sub = errs[0].shape[1]
    total = prev_ref[...] if with_prev else None
    loads = []
    if not final:
        out_ref = refs.pop(0)
        next_ref = refs.pop(0) if after else None
        buf, sem = refs
        for i, (dc, dy, chunk, chunks) in enumerate(blocks):
            col = column(n, chunk, chunks, sub, dy, dc)
            loads.append(load(decoder_ref, col, buf.at[i], sem.at[i]))
        if after:
            dc, dy, chunk, chunks = after
            col = column(n, chunk, chunks, sub, dy, dc)
            loads.append(load(decoder_ref, col, next_ref, sem.at[len(blocks)]))
        for copy in loads:
            copy.start()
    for i, err in enumerate(errs):
        if not final:
            loads[i].wait()
        part = lax.dot_general(
            err[...],
            decoder_ref[...] if final else buf[i],
            (((1,), (1,)), ((), ())),
            preferred_element_type=jnp.float32,
        )
        total = part if total is None else total + part
    if not final:
        out_ref[...] = total
        if after:
            loads[-1].wait()
        return
    ids_ref, loss_ref, out_ref, totals_ref = refs
    totals_ref[...] = total
    rows, k_count = ids_ref.shape
    lat_dev = total.shape[1]
    own = out_ref.shape[1]
    fz, _, _ = factors(n)
    me = lax.axis_index("lat")
    z, _, _ = place(n, me)
    group = rows // fz
    places = lax.broadcasted_iota(jnp.int32, (ROW_STEP, LANES), 1)
    pad = jnp.zeros((ROW_STEP, LANES - k_count), jnp.int32)
    for j in range(fz):
        for s in range(0, group, ROW_STEP):
            first = (z ^ j) * group + s
            rows_at = pl.ds(pl.multiple_of(first, ROW_STEP), ROW_STEP)
            ids = jnp.concatenate([ids_ref[rows_at, :] - me * lat_dev, pad], axis=1)
            held = jnp.where(places < k_count, ids // LANES, -1)
            inside = ids % LANES
            acc = jnp.zeros((ROW_STEP, LANES), jnp.float32)
            if j == 0:
                acc = jnp.where(places == k_count, loss_ref[s : s + ROW_STEP, :], acc)
            here = slice(j * group + s, j * group + s + ROW_STEP)
            for t in range(lat_dev // LANES):
                values = totals_ref[here, t * LANES : (t + 1) * LANES]
                found = jnp.take_along_axis(values, inside, axis=1, mode="promise_in_bounds")
                acc = jnp.where(held == t, found, acc)
            for d in range(ROW_STEP // own):
                out_ref[first // own + d] = acc[d * own : (d + 1) * own, :]


def grad(n, blocks, errs, decoder, prev, after=None, final=None):
    rows, sub = errs[0].shape
    lat_dev = decoder.shape[0]
    count = len(errs)
    args = list(errs) + [decoder if final is not None else in_hbm(decoder)]
    specs = [VMEM] * count + [HBM if final is None else VMEM]
    if prev is not None:
        args.append(prev)
        specs.append(VMEM)
    totals = pltpu.VMEM((rows, lat_dev), jnp.float32)
    if final is None:
        out = [totals] + ([pltpu.VMEM((lat_dev, sub), jnp.bfloat16)] if after else [])
        scratch = [
            pltpu.VMEM((count, lat_dev, sub), jnp.bfloat16),
            pltpu.SemaphoreType.DMA((count + 1,)),
        ]
    else:
        args += list(final)
        specs += [VMEM] * len(final)
        out = [jax.ShapeDtypeStruct((n, rows // n, LANES), jnp.float32)]
        scratch = [totals]
    return pl.pallas_call(
        functools.partial(grad_kernel, n, tuple(blocks), after, final is not None, prev is not None),
        out_shape=out,
        in_specs=specs,
        out_specs=[VMEM] * len(out),
        scratch_shapes=scratch,
        compiler_params=params(),
        cost_estimate=cost(2 * rows * lat_dev * sub * count, 4 * lat_dev * sub * count),
        name="grad",
    )(*args)


def own_kernel(n, blocks, own, *refs):
    errs, out_ref = refs[:-1], refs[-1]
    _, fy, fc = factors(n)
    _, y, c = place(n, lax.axis_index("lat"))
    group, sub = errs[0].shape
    row = lax.broadcasted_iota(jnp.int32, (own, group), 0) + (y * fc + c) * own
    want = lax.broadcasted_iota(jnp.int32, (own, group), 1)
    mine = jnp.where(row == want, 1.0, 0.0).astype(jnp.bfloat16)
    for err, (dc, dy, chunk, chunks) in zip(errs, blocks):
        rows = jnp.dot(mine, err[...], preferred_element_type=jnp.float32)
        out_ref[:, pl.ds(column(n, chunk, chunks, sub, dy, dc), sub)] = rows.astype(jnp.bfloat16)


def own_rows(n, blocks, own, width, errs):
    return pl.pallas_call(
        functools.partial(own_kernel, n, tuple(blocks), own),
        out_shape=jax.ShapeDtypeStruct((own, width), jnp.bfloat16),
        in_specs=[VMEM] * len(errs),
        out_specs=VMEM,
        compiler_params=params(),
        name="own_rows",
    )(*errs)


def local(codes, indices, decoder, targets):
    width = decoder.shape[1]
    rows, k_count = codes.shape
    n = lax.axis_size("lat")
    own = rows // n
    fz, fy, fc = factors(n)
    group = rows // fz
    chunks = CHUNKS
    sub = width // (fc * fy * chunks)
    z, _, _ = place(n, lax.axis_index("lat"))

    def swap(x, dz=0, dy=0, dc=0):
        return lax.ppermute(x, "lat", pairs(n, dz, dy, dc))

    def join(xs, axis):
        return xs[0] if len(xs) == 1 else jnp.concatenate(xs, axis=axis)

    dense, after, summed = None, None, []
    for p in range(chunks):
        parts, dense = decode(
            n, p, chunks, sub, indices, codes, dense, decoder, targets, after
        )
        total = parts[0]
        for dc in range(1, fc):
            total = total + swap(parts[dc], dc=dc)
        blocks = [total[:, o * sub : (o + 1) * sub] for o in range(fy)]
        for b in reversed(bits(fy)):
            after = join(blocks[b:], 1)
            got = swap(after, dy=b)
            blocks = [blocks[o] + got[:, o * sub : (o + 1) * sub] for o in range(b)]
        summed.append(blocks[0])

    diffs = []
    for mine in summed:
        blocks = [
            lax.dynamic_slice_in_dim(mine, (z ^ j) * group, group, 0) for j in range(fz)
        ]
        diff = blocks[0]
        for j in range(1, fz):
            diff = diff + swap(blocks[j], dz=j)
        diffs.append(diff)

    loss = sum(jnp.sum(d * d, axis=1, keepdims=True) for d in diffs)

    pieces, totals = [], None

    def add(some, after=None):
        return grad(n, [at for at, _ in some], [e for _, e in some], decoder, totals, after)

    done = 0
    for p in range(chunks):
        err = diffs[p].astype(jnp.bfloat16)
        here = [join([err] + [swap(err, dz=j) for j in range(1, fz)], 0)]
        pieces.append(((0, 0, p, chunks), here[0]))
        for b in bits(fy):
            last = p == chunks - 1 and 2 * b >= fy
            if last:
                (totals,) = add(pieces[done:])
                done = len(pieces)
            got = [swap(e, dy=b) for e in here]
            if last:
                got = [hold(e, totals) for e in got]
            pieces += [((0, b | i, p, chunks), e) for i, e in enumerate(got)]
            here += got
        for dc in range(1, fc):
            pieces += [((dc, i, p, chunks), swap(e, dc=dc)) for i, e in enumerate(here)]
    totals, columns = add(pieces[done:-1], pieces[-1][0])
    at, e = pieces[-1]
    (back,) = grad(n, [at], [e], columns, totals, None, (indices, loss))
    error = own_rows(n, [at for at, _ in pieces], own, width, [e[:group] for _, e in pieces])

    back = jnp.sum(lax.all_to_all(back, "lat", 0, 0, tiled=True), axis=0)
    return error, back[:, k_count] / width, back[:, :k_count]


def solution(mesh):
    in_specs = (P("groups", None), P("groups", None), P("lat", None), P(("groups", "lat"), None))
    out_specs = (P(("groups", "lat"), None), P(("groups", "lat")), P(("groups", "lat"), None))
    return jax.shard_map(local, mesh=mesh, in_specs=in_specs, out_specs=out_specs, check_vma=False)
```

```python
import functools

import jax
import jax.numpy as jnp
from jax import lax
from jax.experimental import pallas as pl
from jax.experimental.pallas import tpu as pltpu
from jax.sharding import PartitionSpec as P

CHUNKS = 2
ROW_STEP = 16
LANES = 128
VMEM = pl.BlockSpec(memory_space=pltpu.VMEM)
HBM = pl.BlockSpec(memory_space=pltpu.HBM)


def factors(n):
    assert n & (n - 1) == 0
    c = min(n, 2)
    m = n // c
    y = 1
    while 4 * y * y <= m:
        y *= 2
    return m // y, y, c


def place(n, index):
    _, y, c = factors(n)
    return index // (y * c), (index // c) % y, index % c


def bits(size):
    return [1 << i for i in range(size.bit_length() - 1)]


def pairs(n, dz, dy, dc):
    _, fy, fc = factors(n)
    out = []
    for i in range(n):
        z, y, c = place(n, i)
        out.append((i, ((z ^ dz) * fy + (y ^ dy)) * fc + (c ^ dc)))
    return out


def cost(flops, size):
    return pl.CostEstimate(flops=flops, bytes_accessed=size, transcendentals=0)


def params():
    return pltpu.CompilerParams(vmem_limit_bytes=24 * 1024 * 1024)


def in_hbm(x):
    return pltpu.with_memory_space_constraint(x, pltpu.HBM)


def in_vmem(x):
    return pltpu.with_memory_space_constraint(x, pltpu.VMEM)


def column(n, chunk, chunks, sub, dy, dc):
    _, fy, fc = factors(n)
    _, y, c = place(n, lax.axis_index("lat"))
    return pl.multiple_of((((c ^ dc) * fy + (y ^ dy)) * chunks + chunk) * sub, sub)


def hold(x, *after):
    return pl.pallas_call(
        lambda *refs: None,
        out_shape=jax.ShapeDtypeStruct(x.shape, x.dtype),
        in_specs=[VMEM] * (1 + len(after)),
        out_specs=VMEM,
        input_output_aliases={0: 0},
        compiler_params=params(),
        name="hold",
    )(*[in_vmem(a) for a in (x, *after)])


def load(decoder_hbm, col, buf, sem):
    return pltpu.make_async_copy(decoder_hbm.at[:, pl.ds(col, buf.shape[1])], buf, sem)


def decode_kernel(n, own, chunks, parts, first, *refs):
    fz, fy, fc = factors(n)
    me = lax.axis_index("lat")
    if first:
        ids_hbm, codes_hbm, decoder_hbm, targets_hbm, out_ref, dense_ref = refs[:6]
        buf, sem, targets_ref, small, ids_ref, codes_ref = refs[6:]
        smalls_in = [(ids_hbm, ids_ref), (codes_hbm, codes_ref), (targets_hbm, targets_ref)]
    else:
        dense_ref, decoder_hbm, targets_hbm = refs[:3]
        out_ref, buf, sem, targets_ref, small = refs[-5:]
        smalls_in = [(targets_hbm, targets_ref)]
    smalls = [pltpu.make_async_copy(a, b, small.at[i]) for i, (a, b) in enumerate(smalls_in)]
    for copy in smalls:
        copy.start()
    lat_dev, sub = buf.shape[1:]
    cols = [column(n, p, chunks, sub, o, dc) for p, dc in parts for o in range(fy)]
    loads = [load(decoder_hbm, col, buf.at[i], sem.at[i]) for i, col in enumerate(cols)]
    for copy in loads:
        copy.start()
    for copy in smalls:
        copy.wait()
    if first:
        rows, k_count = ids_ref.shape
        lanes = lax.broadcasted_iota(jnp.int32, (ROW_STEP, lat_dev), 1) + me * lat_dev

        def body(g, carry):
            at = pl.ds(pl.multiple_of(g * ROW_STEP, ROW_STEP), ROW_STEP)
            ids = ids_ref[at, :]
            codes = codes_ref[at, :].astype(jnp.float32)
            acc = jnp.zeros((ROW_STEP, lat_dev), jnp.float32)
            for k in range(k_count):
                acc = jnp.where(ids[:, k : k + 1] == lanes, codes[:, k : k + 1], acc)
            dense_ref[at, :] = acc.astype(jnp.bfloat16)
            return carry

        lax.fori_loop(0, rows // ROW_STEP, body, 0)
    rows = dense_ref.shape[0]
    row = lax.broadcasted_iota(jnp.int32, (rows, own), 0)
    want = lax.broadcasted_iota(jnp.int32, (rows, own), 1) + me * own
    mine = jnp.where(row == want, -1.0, 0.0).astype(jnp.bfloat16)
    for i, col in enumerate(cols):
        loads[i].wait()
        part = jnp.dot(dense_ref[...], buf[i], preferred_element_type=jnp.float32)
        part += jnp.dot(
            mine, targets_ref[:, pl.ds(col, sub)], preferred_element_type=jnp.float32
        )
        out_ref[:, i * sub : (i + 1) * sub] = part


def decode(n, chunks, sub, parts, decoder, targets, start=None, dense=None, after=None):
    _, fy, _ = factors(n)
    first = start is not None
    rows = start[0].shape[0] if first else dense.shape[0]
    lat_dev = decoder.shape[0]
    count = len(parts) * fy
    out = [pltpu.VMEM((rows, count * sub), jnp.float32)]
    scratch = [
        pltpu.VMEM((count, lat_dev, sub), jnp.bfloat16),
        pltpu.SemaphoreType.DMA((count,)),
        pltpu.VMEM(targets.shape, targets.dtype),
        pltpu.SemaphoreType.DMA((3,)),
    ]
    if first:
        args = [in_hbm(x) for x in (*start, decoder, targets)]
        specs = [HBM] * 4
        out.append(pltpu.VMEM((rows, lat_dev), jnp.bfloat16))
        scratch += [pltpu.VMEM(x.shape, x.dtype) for x in start]
    else:
        args, specs = [dense, in_hbm(decoder), in_hbm(targets)], [VMEM, HBM, HBM]
        if after is not None:
            args.append(in_vmem(after))
            specs.append(VMEM)
    return pl.pallas_call(
        functools.partial(decode_kernel, n, rows // n, chunks, parts, first),
        out_shape=out,
        in_specs=specs,
        out_specs=[VMEM] * len(out),
        scratch_shapes=scratch,
        compiler_params=params(),
        cost_estimate=cost(2 * rows * lat_dev * count * sub, 4 * lat_dev * count * sub),
        name="decode",
    )(*args)


def grad_kernel(n, blocks, after, final, with_prev, loaded, *refs):
    refs = list(refs)
    errs = [refs.pop(0) for _ in blocks]
    decoder_ref = None if final else refs.pop(0)
    loaded_ref = refs.pop(0) if loaded else None
    prev_ref = refs.pop(0) if with_prev else None
    sub = errs[0].shape[1]
    total = prev_ref[...] if with_prev else None
    loads = []
    if not final:
        out_ref = refs.pop(0)
        next_ref = refs.pop(0) if after else None
        buf, sem = refs
        for i, (dc, dy, chunk, chunks) in enumerate(blocks):
            if loaded and i == 0:
                continue
            col = column(n, chunk, chunks, sub, dy, dc)
            loads.append(load(decoder_ref, col, buf.at[i], sem.at[i]))
        if after:
            dc, dy, chunk, chunks = after
            col = column(n, chunk, chunks, sub, dy, dc)
            loads.append(load(decoder_ref, col, next_ref, sem.at[len(blocks)]))
        for copy in loads:
            copy.start()
    for i, err in enumerate(errs):
        here = loaded and i == 0
        if not here:
            loads[i - loaded].wait()
        part = lax.dot_general(
            err[...],
            loaded_ref[...] if here else buf[i],
            (((1,), (1,)), ((), ())),
            preferred_element_type=jnp.float32,
        )
        total = part if total is None else total + part
    if not final:
        out_ref[...] = total
        if after:
            loads[-1].wait()
        return
    ids_ref, loss_ref, out_ref, totals_ref = refs
    totals_ref[...] = total
    rows, k_count = ids_ref.shape
    lat_dev = total.shape[1]
    own = out_ref.shape[1]
    fz, _, _ = factors(n)
    me = lax.axis_index("lat")
    z, _, _ = place(n, me)
    group = rows // fz
    places = lax.broadcasted_iota(jnp.int32, (ROW_STEP, LANES), 1)
    pad = jnp.zeros((ROW_STEP, LANES - k_count), jnp.int32)
    for j in range(fz):
        for s in range(0, group, ROW_STEP):
            first = (z ^ j) * group + s
            rows_at = pl.ds(pl.multiple_of(first, ROW_STEP), ROW_STEP)
            ids = jnp.concatenate([ids_ref[rows_at, :] - me * lat_dev, pad], axis=1)
            held = jnp.where(places < k_count, ids // LANES, -1)
            inside = ids % LANES
            acc = jnp.zeros((ROW_STEP, LANES), jnp.float32)
            if j == 0:
                acc = jnp.where(places == k_count, loss_ref[s : s + ROW_STEP, :], acc)
            here = slice(j * group + s, j * group + s + ROW_STEP)
            for t in range(lat_dev // LANES):
                values = totals_ref[here, t * LANES : (t + 1) * LANES]
                found = jnp.take_along_axis(values, inside, axis=1, mode="promise_in_bounds")
                acc = jnp.where(held == t, found, acc)
            for d in range(ROW_STEP // own):
                out_ref[first // own + d] = acc[d * own : (d + 1) * own, :]


def grad(n, blocks, errs, decoder, prev, columns=None, after=None, final=None):
    rows, sub = errs[0].shape
    lat_dev = decoder.shape[0]
    count = len(errs)
    args, specs = list(errs), [VMEM] * count
    if final is None:
        args.append(in_hbm(decoder))
        specs.append(HBM)
    for x in (columns, prev):
        if x is not None:
            args.append(in_vmem(x))
            specs.append(VMEM)
    totals = pltpu.VMEM((rows, lat_dev), jnp.float32)
    if final is None:
        out = [totals] + ([pltpu.VMEM((lat_dev, sub), jnp.bfloat16)] if after else [])
        scratch = [
            pltpu.VMEM((count, lat_dev, sub), jnp.bfloat16),
            pltpu.SemaphoreType.DMA((count + 1,)),
        ]
    else:
        args += list(final)
        specs += [VMEM] * len(final)
        out = [jax.ShapeDtypeStruct((n, rows // n, LANES), jnp.float32)]
        scratch = [totals]
    return pl.pallas_call(
        functools.partial(
            grad_kernel, n, tuple(blocks), after, final is not None, prev is not None, columns is not None
        ),
        out_shape=out,
        in_specs=specs,
        out_specs=[VMEM] * len(out),
        scratch_shapes=scratch,
        compiler_params=params(),
        cost_estimate=cost(2 * rows * lat_dev * sub * count, 4 * lat_dev * sub * count),
        name="grad",
    )(*args)


def own_kernel(n, blocks, own, *refs):
    errs, out_ref = refs[:-1], refs[-1]
    _, fy, fc = factors(n)
    _, y, c = place(n, lax.axis_index("lat"))
    group, sub = errs[0].shape
    row = lax.broadcasted_iota(jnp.int32, (own, group), 0) + (y * fc + c) * own
    want = lax.broadcasted_iota(jnp.int32, (own, group), 1)
    mine = jnp.where(row == want, 1.0, 0.0).astype(jnp.bfloat16)
    for err, (dc, dy, chunk, chunks) in zip(errs, blocks):
        rows = jnp.dot(mine, err[...], preferred_element_type=jnp.float32)
        out_ref[:, pl.ds(column(n, chunk, chunks, sub, dy, dc), sub)] = rows.astype(jnp.bfloat16)


def own_rows(n, blocks, own, width, errs):
    return pl.pallas_call(
        functools.partial(own_kernel, n, tuple(blocks), own),
        out_shape=jax.ShapeDtypeStruct((own, width), jnp.bfloat16),
        in_specs=[VMEM] * len(errs),
        out_specs=VMEM,
        compiler_params=params(),
        name="own_rows",
    )(*errs)


def local(codes, indices, decoder, targets):
    width = decoder.shape[1]
    rows, k_count = codes.shape
    n = lax.axis_size("lat")
    own = rows // n
    fz, fy, fc = factors(n)
    group = rows // fz
    chunks = CHUNKS
    sub = width // (fc * fy * chunks)
    z, _, _ = place(n, lax.axis_index("lat"))

    def swap(x, dz=0, dy=0, dc=0):
        return lax.ppermute(x, "lat", pairs(n, dz, dy, dc))

    def join(xs, axis):
        return xs[0] if len(xs) == 1 else jnp.concatenate(xs, axis=axis)

    wide = fy * sub
    others = tuple((p, dc) for dc in range(1, fc) for p in range(chunks))
    part, dense = decode(n, chunks, sub, others, decoder, targets, (indices, codes))
    came = swap(part, dc=1)
    summed, leaving, after = [], [], None
    for p in range(chunks):
        (part,) = decode(n, chunks, sub, ((p, 0),), decoder, targets, dense=dense, after=after)
        total = part + came[:, p * wide : (p + 1) * wide]
        blocks = [total[:, o * sub : (o + 1) * sub] for o in range(fy)]
        got = None
        for b in reversed(bits(fy)):
            if got is not None:
                blocks = [blocks[o] + got[:, o * sub : (o + 1) * sub] for o in range(2 * b)]
            after = join(blocks[b:], 1)
            got = swap(after, dy=b)
        leaving.append(after)
        summed.append((blocks[0], got))

    sums, moved = [], []
    for p, (x, y) in enumerate(summed):
        x = x + (hold(y, leaving[p + 1]) if p + 1 < chunks else y)
        blocks = [
            lax.dynamic_slice_in_dim(x, (z ^ j) * group, group, 0) for j in range(fz)
        ]
        sums.append(blocks[0])
        moved.append([swap(e, dz=j) for j, e in enumerate(blocks) if j])
    errs, gathered, loss = [], [], 0.0
    for p in range(chunks):
        if p + 1 < chunks:
            moved[p][-1] = hold(moved[p][-1], sums[p + 1])
        if p:
            moved[p][0] = hold(moved[p][0], errs[p - 1])
        diff = sum(moved[p], sums[p])
        loss = loss + jnp.sum(diff * diff, axis=1, keepdims=True)
        errs.append(diff.astype(jnp.bfloat16))
        gathered.append([swap(errs[p], dz=j) for j in range(1, fz)])

    pieces, columns, totals, wholes = [], None, None, []
    for p in range(chunks):
        if p + 1 < chunks:
            gathered[p][-1] = hold(gathered[p][-1], errs[p + 1])
        if p:
            gathered[p][0] = hold(gathered[p][0], wholes[p - 1])
        wholes.append(join([errs[p]] + gathered[p], 0))
    first = [((0, 0, p, chunks), e) for p, e in enumerate(wholes)]
    done = None
    for p in range(chunks):
        here = [wholes[p]]
        for b in bits(fy):
            got = [swap(e, dy=b) for e in here]
            if p == chunks - 1 and 2 * b >= fy:
                (totals,) = grad(n, [at for at, _ in first], [e for _, e in first], decoder, None)
                if pieces:
                    totals, columns = grad(
                        n, [at for at, _ in pieces], [e for _, e in pieces], decoder, totals, None, (0, b, p, chunks)
                    )
                done = len(pieces)
                got = [hold(got[0], totals)] + got[1:]
            pieces += [((0, b | i, p, chunks), e) for i, e in enumerate(got)]
            here += got
        for dc in range(1, fc):
            pieces += [((dc, i, p, chunks), swap(e, dc=dc)) for i, e in enumerate(here)]
    some, last = pieces[done:-1], pieces[-1]
    totals, columns = grad(
        n, [at for at, _ in some], [e for _, e in some], decoder, totals, columns, last[0]
    )
    (back,) = grad(n, [last[0]], [last[1]], decoder, totals, columns, None, (indices, loss))
    pieces = first + pieces
    error = own_rows(n, [at for at, _ in pieces], own, width, [e[:group] for _, e in pieces])

    back = jnp.sum(lax.all_to_all(back, "lat", 0, 0, tiled=True), axis=0)
    return error, back[:, k_count] / width, back[:, :k_count]


def solution(mesh):
    in_specs = (P("groups", None), P("groups", None), P("lat", None), P(("groups", "lat"), None))
    out_specs = (P(("groups", "lat"), None), P(("groups", "lat")), P(("groups", "lat"), None))
    return jax.shard_map(local, mesh=mesh, in_specs=in_specs, out_specs=out_specs, check_vma=False)
```

```python
import functools

import jax
import jax.numpy as jnp
from jax import lax
from jax.experimental import pallas as pl
from jax.experimental.pallas import tpu as pltpu
from jax.sharding import PartitionSpec as P

CHUNKS = 2
ROW_STEP = 16
LANES = 128
SUBLANES = 8
FETCHES = 8
VMEM = pl.BlockSpec(memory_space=pltpu.VMEM)
HBM = pl.BlockSpec(memory_space=pltpu.HBM)


def factors(n):
    assert n > 1 and n & (n - 1) == 0
    c = 2
    m = n // c
    y = 1
    while 4 * y * y <= m:
        y *= 2
    return m // y, y, c


def place(n, index):
    _, y, c = factors(n)
    return index // (y * c), (index // c) % y, index % c


def bits(size):
    return [1 << i for i in range(size.bit_length() - 1)]


def pairs(n, dz, dy, dc):
    _, fy, fc = factors(n)
    out = []
    for i in range(n):
        z, y, c = place(n, i)
        out.append((i, ((z ^ dz) * fy + (y ^ dy)) * fc + (c ^ dc)))
    return out


def cost(flops, size):
    return pl.CostEstimate(flops=flops, bytes_accessed=size, transcendentals=0)


def params():
    return pltpu.CompilerParams(vmem_limit_bytes=24 * 1024 * 1024)


def in_hbm(x):
    return pltpu.with_memory_space_constraint(x, pltpu.HBM)


def in_vmem(x):
    return pltpu.with_memory_space_constraint(x, pltpu.VMEM)


def column(n, chunk, chunks, sub, dy, dc):
    _, fy, fc = factors(n)
    _, y, c = place(n, lax.axis_index("lat"))
    return pl.multiple_of((((c ^ dc) * fy + (y ^ dy)) * chunks + chunk) * sub, sub)


def hold(x, *after):
    return pl.pallas_call(
        lambda *refs: None,
        out_shape=jax.ShapeDtypeStruct(x.shape, x.dtype),
        in_specs=[VMEM] * (1 + len(after)),
        out_specs=VMEM,
        input_output_aliases={0: 0},
        compiler_params=params(),
        name="hold",
    )(*[in_vmem(a) for a in (x, *after)])


def load(decoder_hbm, col, buf, sem):
    return pltpu.make_async_copy(decoder_hbm.at[:, pl.ds(col, buf.shape[1])], buf, sem)


def decode_kernel(n, own, chunks, parts, first, *refs):
    fz, fy, fc = factors(n)
    me = lax.axis_index("lat")
    if first:
        ids_hbm, codes_hbm, decoder_hbm, targets_hbm, out_ref, dense_ref = refs[:6]
        buf, sem, targets_ref, small, ids_ref, codes_ref = refs[6:]
        smalls_in = [(ids_hbm, ids_ref), (codes_hbm, codes_ref), (targets_hbm, targets_ref)]
    else:
        dense_ref, decoder_hbm, targets_hbm = refs[:3]
        out_ref, buf, sem, targets_ref, small = refs[-5:]
        smalls_in = [(targets_hbm, targets_ref)]
    smalls = [pltpu.make_async_copy(a, b, small.at[i]) for i, (a, b) in enumerate(smalls_in)]
    for copy in smalls:
        copy.start()
    lat_dev, sub = buf.shape[1:]
    cols = [column(n, p, chunks, sub, o, dc) for p, dc in parts for o in range(fy)]
    loads = [load(decoder_hbm, col, buf.at[i], sem.at[i]) for i, col in enumerate(cols)]
    for copy in loads:
        copy.start()
    for copy in smalls:
        copy.wait()
    if first:
        rows, k_count = ids_ref.shape
        lanes = lax.broadcasted_iota(jnp.int32, (ROW_STEP, lat_dev), 1) + me * lat_dev

        def body(g, carry):
            at = pl.ds(pl.multiple_of(g * ROW_STEP, ROW_STEP), ROW_STEP)
            ids = ids_ref[at, :]
            codes = codes_ref[at, :].astype(jnp.float32)
            acc = jnp.zeros((ROW_STEP, lat_dev), jnp.float32)
            for k in range(k_count):
                acc = jnp.where(ids[:, k : k + 1] == lanes, codes[:, k : k + 1], acc)
            dense_ref[at, :] = acc.astype(jnp.bfloat16)
            return carry

        lax.fori_loop(0, rows // ROW_STEP, body, 0)
    per = SUBLANES // own
    tile = pl.ds(pl.multiple_of(me // per * SUBLANES, SUBLANES), SUBLANES)
    mine = lax.broadcasted_iota(jnp.int32, (SUBLANES, sub), 0) // own == me % per
    for i, col in enumerate(cols):
        loads[i].wait()
        here = slice(i * sub, (i + 1) * sub)
        out_ref[:, here] = jnp.dot(dense_ref[...], buf[i], preferred_element_type=jnp.float32)
        target = targets_ref[:, pl.ds(col, sub)].astype(jnp.float32)
        target = jnp.concatenate([target] * per, axis=0)
        out_ref[tile, here] -= jnp.where(mine, target, 0.0)


def decode(n, chunks, sub, parts, decoder, targets, start=None, dense=None, after=None):
    _, fy, _ = factors(n)
    first = start is not None
    rows = start[0].shape[0] if first else dense.shape[0]
    lat_dev = decoder.shape[0]
    count = len(parts) * fy
    out = [pltpu.VMEM((rows, count * sub), jnp.float32)]
    scratch = [
        pltpu.VMEM((count, lat_dev, sub), jnp.bfloat16),
        pltpu.SemaphoreType.DMA((count,)),
        pltpu.VMEM(targets.shape, targets.dtype),
        pltpu.SemaphoreType.DMA((3,)),
    ]
    if first:
        args = [in_hbm(x) for x in (*start, decoder, targets)]
        specs = [HBM] * 4
        out.append(pltpu.VMEM((rows, lat_dev), jnp.bfloat16))
        scratch += [pltpu.VMEM(x.shape, x.dtype) for x in start]
    else:
        args, specs = [dense, in_hbm(decoder), in_hbm(targets)], [VMEM, HBM, HBM]
        if after is not None:
            args.append(in_vmem(after))
            specs.append(VMEM)
    return pl.pallas_call(
        functools.partial(decode_kernel, n, rows // n, chunks, parts, first),
        out_shape=out,
        in_specs=specs,
        out_specs=[VMEM] * len(out),
        scratch_shapes=scratch,
        compiler_params=params(),
        cost_estimate=cost(2 * rows * lat_dev * count * sub, 4 * lat_dev * count * sub),
        name="decode",
    )(*args)


def fetch_kernel(decoder_hbm, _, out_ref, sem):
    step = out_ref.shape[0] // FETCHES
    parts = [pl.ds(i * step, step) for i in range(FETCHES)]
    copies = [
        pltpu.make_async_copy(decoder_hbm.at[at], out_ref.at[at], sem.at[i])
        for i, at in enumerate(parts)
    ]
    for copy in copies:
        copy.start()
    for copy in copies:
        copy.wait()


def fetch(decoder, after):
    return pl.pallas_call(
        fetch_kernel,
        out_shape=pltpu.VMEM(decoder.shape, decoder.dtype),
        in_specs=[HBM, VMEM],
        out_specs=VMEM,
        scratch_shapes=[pltpu.SemaphoreType.DMA((FETCHES,))],
        compiler_params=params(),
        cost_estimate=cost(0, decoder.size * 2),
        name="fetch",
    )(in_hbm(decoder), in_vmem(after))


def grad_kernel(n, places, counts, final, with_prev, *refs):
    refs = list(refs)
    errs = [[refs.pop(0) for _ in range(count)] for count in counts]
    decoder_ref = refs.pop(0)
    total = refs.pop(0)[...] if with_prev else None
    for parts, (dc, dy) in zip(errs, places):
        err = parts[0][...] if len(parts) == 1 else jnp.concatenate([e[...] for e in parts], axis=0)
        width = err.shape[1]
        part = lax.dot_general(
            err,
            decoder_ref[:, pl.ds(column(n, 0, 1, width, dy, dc), width)],
            (((1,), (1,)), ((), ())),
            preferred_element_type=jnp.float32,
        )
        total = part if total is None else total + part
    if not final:
        refs[0][...] = total
        return
    ids_ref, loss_ref, out_ref, totals_ref = refs
    totals_ref[...] = total
    rows, k_count = ids_ref.shape
    lat_dev = total.shape[1]
    own = out_ref.shape[1]
    fz, _, _ = factors(n)
    me = lax.axis_index("lat")
    z, _, _ = place(n, me)
    group = rows // fz
    places = lax.broadcasted_iota(jnp.int32, (ROW_STEP, LANES), 1)
    pad = jnp.zeros((ROW_STEP, LANES - k_count), jnp.int32)
    for j in range(fz):
        for s in range(0, group, ROW_STEP):
            first = (z ^ j) * group + s
            rows_at = pl.ds(pl.multiple_of(first, ROW_STEP), ROW_STEP)
            ids = jnp.concatenate([ids_ref[rows_at, :] - me * lat_dev, pad], axis=1)
            held = jnp.where(places < k_count, ids // LANES, -1)
            inside = ids % LANES
            acc = jnp.zeros((ROW_STEP, LANES), jnp.float32)
            if j == 0:
                acc = jnp.where(places == k_count, loss_ref[s : s + ROW_STEP, :], acc)
            here = slice(j * group + s, j * group + s + ROW_STEP)
            for t in range(lat_dev // LANES):
                values = totals_ref[here, t * LANES : (t + 1) * LANES]
                found = jnp.take_along_axis(values, inside, axis=1, mode="promise_in_bounds")
                acc = jnp.where(held == t, found, acc)
            for d in range(ROW_STEP // own):
                out_ref[first // own + d] = acc[d * own : (d + 1) * own, :]


def grad(n, rows, pieces, decoder, prev, final=None):
    lat_dev = decoder.shape[0]
    places = tuple(at for at, _ in pieces)
    counts = tuple(len(e) for _, e in pieces)
    args = [x for _, e in pieces for x in e] + [in_vmem(decoder)]
    if prev is not None:
        args.append(in_vmem(prev))
    if final is not None:
        args += list(final)
    totals = pltpu.VMEM((rows, lat_dev), jnp.float32)
    size = pieces[0][1][0].shape[1] * len(pieces)
    return pl.pallas_call(
        functools.partial(grad_kernel, n, places, counts, final is not None, prev is not None),
        out_shape=totals if final is None else jax.ShapeDtypeStruct((n, rows // n, LANES), jnp.float32),
        in_specs=[VMEM] * len(args),
        out_specs=VMEM,
        scratch_shapes=[] if final is None else [totals],
        compiler_params=params(),
        cost_estimate=cost(2 * rows * lat_dev * size, 4 * lat_dev * size),
        name="grad",
    )(*args)


def own_kernel(n, blocks, own, *refs):
    errs, out_ref = refs[:-1], refs[-1]
    _, fy, fc = factors(n)
    _, y, c = place(n, lax.axis_index("lat"))
    group, sub = errs[0].shape
    row = lax.broadcasted_iota(jnp.int32, (own, group), 0) + (y * fc + c) * own
    want = lax.broadcasted_iota(jnp.int32, (own, group), 1)
    mine = jnp.where(row == want, 1.0, 0.0).astype(jnp.bfloat16)
    for err, (dc, dy) in zip(errs, blocks):
        rows = jnp.dot(mine, err[...], preferred_element_type=jnp.float32)
        out_ref[:, pl.ds(column(n, 0, 1, sub, dy, dc), sub)] = rows.astype(jnp.bfloat16)


def own_rows(n, blocks, own, width, errs):
    return pl.pallas_call(
        functools.partial(own_kernel, n, tuple(blocks), own),
        out_shape=jax.ShapeDtypeStruct((own, width), jnp.bfloat16),
        in_specs=[VMEM] * len(errs),
        out_specs=VMEM,
        compiler_params=params(),
        name="own_rows",
    )(*errs)


def local(codes, indices, decoder, targets):
    width = decoder.shape[1]
    rows, k_count = codes.shape
    n = lax.axis_size("lat")
    own = rows // n
    fz, fy, fc = factors(n)
    group = rows // fz
    chunks = CHUNKS
    sub = width // (fc * fy * chunks)
    z, _, _ = place(n, lax.axis_index("lat"))

    def swap(x, dz=0, dy=0, dc=0):
        return lax.ppermute(x, "lat", pairs(n, dz, dy, dc))

    def join(xs, axis):
        return xs[0] if len(xs) == 1 else jnp.concatenate(xs, axis=axis)

    wide = fy * sub
    others = tuple((p, dc) for dc in range(1, fc) for p in range(chunks))
    part, dense = decode(n, chunks, sub, others, decoder, targets, (indices, codes))
    came = swap(part, dc=1)
    summed, leaving, after = [], [], None
    for p in range(chunks):
        (part,) = decode(n, chunks, sub, ((p, 0),), decoder, targets, dense=dense, after=after)
        total = part + came[:, p * wide : (p + 1) * wide]
        blocks = [total[:, o * sub : (o + 1) * sub] for o in range(fy)]
        got = None
        for b in reversed(bits(fy)):
            if got is not None:
                blocks = [blocks[o] + got[:, o * sub : (o + 1) * sub] for o in range(2 * b)]
            after = join(blocks[b:], 1)
            got = swap(after, dy=b)
        leaving.append(after)
        summed.append((blocks[0], got))

    fetched = fetch(decoder, leaving[-1])
    sums, moved = [], []
    for p, (x, y) in enumerate(summed):
        x = x + (hold(y, fetched) if p == 0 else y)
        blocks = [
            lax.dynamic_slice_in_dim(x, (z ^ j) * group, group, 0) for j in range(fz)
        ]
        sums.append(blocks[0])
        moved.append([swap(e, dz=j) for j, e in enumerate(blocks) if j])
    errs, loss = [], 0.0
    for p in range(chunks):
        if p + 1 < chunks:
            moved[p][-1] = hold(moved[p][-1], sums[p + 1])
        if p:
            moved[p][0] = hold(moved[p][0], errs[p - 1])
        diff = sum(moved[p], sums[p])
        loss = loss + jnp.sum(diff * diff, axis=1, keepdims=True)
        errs.append(diff.astype(jnp.bfloat16))

    err = join(errs, 1)
    come = [err] + [swap(err, dz=j) for j in range(1, fz)]
    half = fz // 2
    near = [((0, 0), [join(come[:half], 0), join(come[half:], 0)])]
    for b in bits(fy):
        last = [((0, b | at[1]), [swap(e, dy=b) for e in parts]) for at, parts in near]
        near += last
    near = near[: -len(last)]

    def to_core(pieces):
        sent = swap(join([e for _, parts in pieces for e in parts], 0), dc=1)
        return [((1, at[1]), [sent[i * rows : (i + 1) * rows]]) for i, (at, _) in enumerate(pieces)]

    far = to_core(near)
    totals = grad(n, rows, near, fetched, None)
    totals = grad(n, rows, far, fetched, totals)
    last[-1][1][0] = hold(last[-1][1][0], totals)
    far_last = to_core(last)
    totals = grad(n, rows, last, fetched, totals)
    back = grad(n, rows, far_last, fetched, totals, (indices, loss))
    pieces = near + far + last + far_last
    error = own_rows(n, [at for at, _ in pieces], own, width, [e[0][:group] for _, e in pieces])

    back = jnp.sum(lax.all_to_all(back, "lat", 0, 0, tiled=True), axis=0)
    return error, back[:, k_count] / width, back[:, :k_count]


def solution(mesh):
    in_specs = (P("groups", None), P("groups", None), P("lat", None), P(("groups", "lat"), None))
    out_specs = (P(("groups", "lat"), None), P(("groups", "lat")), P(("groups", "lat"), None))
    return jax.shard_map(local, mesh=mesh, in_specs=in_specs, out_specs=out_specs, check_vma=False)
```

```python
import functools

import jax
import jax.numpy as jnp
from jax import lax
from jax.experimental import pallas as pl
from jax.experimental.pallas import tpu as pltpu
from jax.sharding import PartitionSpec as P

CHUNKS = 2
ROW_STEP = 16
LANES = 128
SUBLANES = 8
FETCHES = 4
VMEM = pl.BlockSpec(memory_space=pltpu.VMEM)
HBM = pl.BlockSpec(memory_space=pltpu.HBM)


def factors(n):
    assert n > 1 and n & (n - 1) == 0
    c = 2
    m = n // c
    y = 1
    while 4 * y * y <= m:
        y *= 2
    return m // y, y, c


def place(n, index):
    _, y, c = factors(n)
    return index // (y * c), (index // c) % y, index % c


def bits(size):
    return [1 << i for i in range(size.bit_length() - 1)]


def z_order(fz):
    return ([fz - 1] if fz > 1 else []) + list(range(1, fz - 1))


def pairs(n, dz, dy, dc):
    _, fy, fc = factors(n)
    out = []
    for i in range(n):
        z, y, c = place(n, i)
        out.append((i, ((z ^ dz) * fy + (y ^ dy)) * fc + (c ^ dc)))
    return out


def cost(flops, size):
    return pl.CostEstimate(flops=flops, bytes_accessed=size, transcendentals=0)


def params():
    return pltpu.CompilerParams(vmem_limit_bytes=24 * 1024 * 1024)


def in_hbm(x):
    return pltpu.with_memory_space_constraint(x, pltpu.HBM)


def in_vmem(x):
    return pltpu.with_memory_space_constraint(x, pltpu.VMEM)


def column(n, chunk, chunks, sub, dy, dc):
    _, fy, fc = factors(n)
    _, y, c = place(n, lax.axis_index("lat"))
    return pl.multiple_of((((c ^ dc) * fy + (y ^ dy)) * chunks + chunk) * sub, sub)


def hold(x, *after):
    return pl.pallas_call(
        lambda *refs: None,
        out_shape=jax.ShapeDtypeStruct(x.shape, x.dtype),
        in_specs=[VMEM] * (1 + len(after)),
        out_specs=VMEM,
        input_output_aliases={0: 0},
        compiler_params=params(),
        name="hold",
    )(*[in_vmem(a) for a in (x, *after)])


def load(decoder_hbm, col, buf, sem):
    return pltpu.make_async_copy(decoder_hbm.at[:, pl.ds(col, buf.shape[1])], buf, sem)


def decode_kernel(n, own, chunks, parts, first, loaded, keep, *refs):
    fz, fy, fc = factors(n)
    me = lax.axis_index("lat")
    refs = list(refs)
    if first:
        ids_hbm, codes_hbm = refs.pop(0), refs.pop(0)
    else:
        dense_ref = refs.pop(0)
    decoder_ref, targets_hbm = refs.pop(0), refs.pop(0)
    if not first and not loaded:
        refs.pop(0)
    outs = [refs.pop(0) for _ in parts]
    if first:
        dense_ref, kept_ref = refs.pop(0), refs.pop(0)
    targets_ref, small = refs.pop(0), refs.pop(0)
    smalls_in = [(targets_hbm, targets_ref)]
    if first:
        smalls_in = [(ids_hbm, refs[0]), (codes_hbm, refs[1])] + smalls_in
        ids_ref, codes_ref = refs.pop(0), refs.pop(0)
    smalls = [pltpu.make_async_copy(a, b, small.at[i]) for i, (a, b) in enumerate(smalls_in)]
    for copy in smalls:
        copy.start()
    rows, lat_dev = dense_ref.shape
    sub = outs[0].shape[1] // fy
    cols = [column(n, p, chunks, sub, o, dc) for p, dc in parts for o in range(fy)]
    loads, later, buf = [], [], decoder_ref
    if not loaded:
        buf, sem = refs
        loads = [load(decoder_ref, col, buf.at[i], sem.at[i]) for i, col in enumerate(cols)]
        for i, (p, dc, o) in enumerate((p, dc, o) for p, dc in keep for o in range(fy)):
            col = column(n, p, chunks, sub, o, dc)
            later.append(load(decoder_ref, col, kept_ref.at[i], sem.at[len(cols) + i]))
    for copy in loads + later:
        copy.start()
    for copy in smalls:
        copy.wait()
    if first:
        k_count = ids_ref.shape[1]
        lanes = lax.broadcasted_iota(jnp.int32, (ROW_STEP, lat_dev), 1) + me * lat_dev

        def body(g, carry):
            at = pl.ds(pl.multiple_of(g * ROW_STEP, ROW_STEP), ROW_STEP)
            ids = ids_ref[at, :]
            codes = codes_ref[at, :].astype(jnp.float32)
            acc = jnp.zeros((ROW_STEP, lat_dev), jnp.float32)
            for k in range(k_count):
                acc = jnp.where(ids[:, k : k + 1] == lanes, codes[:, k : k + 1], acc)
            dense_ref[at, :] = acc.astype(jnp.bfloat16)
            return carry

        lax.fori_loop(0, rows // ROW_STEP, body, 0)
    per = SUBLANES // own
    tile = pl.ds(pl.multiple_of(me // per * SUBLANES, SUBLANES), SUBLANES)
    mine = lax.broadcasted_iota(jnp.int32, (SUBLANES, sub), 0) // own == me % per
    for i, col in enumerate(cols):
        if loads:
            loads[i].wait()
        out_ref = outs[i // fy]
        here = slice(i % fy * sub, (i % fy + 1) * sub)
        out_ref[:, here] = jnp.dot(dense_ref[...], buf[i], preferred_element_type=jnp.float32)
        target = targets_ref[:, pl.ds(col, sub)].astype(jnp.float32)
        target = jnp.concatenate([target] * per, axis=0)
        out_ref[tile, here] -= jnp.where(mine, target, 0.0)
    for copy in later:
        copy.wait()


def decode(n, chunks, sub, parts, decoder, targets, start=None, keep=(), dense=None, after=None):
    _, fy, _ = factors(n)
    first, loaded = start is not None, decoder.ndim == 3
    rows = start[0].shape[0] if first else dense.shape[0]
    lat_dev = decoder.shape[-2]
    count = len(parts) * fy
    out = [pltpu.VMEM((rows, fy * sub), jnp.float32)] * len(parts)
    scratch = [pltpu.VMEM(targets.shape, targets.dtype), pltpu.SemaphoreType.DMA((3,))]
    if first:
        args = [in_hbm(x) for x in (*start, decoder, targets)]
        specs = [HBM] * 4
        out += [
            pltpu.VMEM((rows, lat_dev), jnp.bfloat16),
            pltpu.VMEM((len(keep) * fy, lat_dev, sub), jnp.bfloat16),
        ]
        scratch += [pltpu.VMEM(x.shape, x.dtype) for x in start]
    elif loaded:
        args, specs = [dense, in_vmem(decoder), in_hbm(targets)], [VMEM, VMEM, HBM]
    else:
        args = [dense, in_hbm(decoder), in_hbm(targets), in_vmem(after)]
        specs = [VMEM, HBM, HBM, VMEM]
    if not loaded:
        scratch += [
            pltpu.VMEM((count, lat_dev, sub), jnp.bfloat16),
            pltpu.SemaphoreType.DMA((count + len(keep) * fy,)),
        ]
    return pl.pallas_call(
        functools.partial(decode_kernel, n, rows // n, chunks, parts, first, loaded, keep),
        out_shape=out,
        in_specs=specs,
        out_specs=[VMEM] * len(out),
        scratch_shapes=scratch,
        compiler_params=params(),
        cost_estimate=cost(2 * rows * lat_dev * count * sub, 4 * lat_dev * count * sub),
        name="decode",
    )(*args)


def fetch_kernel(n, dys, decoder_hbm, _, out_ref, sem):
    _, lat_dev, width = out_ref.shape
    step = lat_dev // FETCHES
    copies = []
    for slot, (dc, dy) in enumerate((dc, dy) for dc in range(2) for dy in dys):
        col = column(n, 0, 1, width, dy, dc)
        for i in range(FETCHES):
            at = pl.ds(i * step, step)
            copies.append(
                pltpu.make_async_copy(
                    decoder_hbm.at[at, pl.ds(col, width)], out_ref.at[slot, at], sem.at[slot, i]
                )
            )
    for copy in copies:
        copy.start()
    for copy in copies:
        copy.wait()


def fetch(n, width, dys, decoder, after):
    count = 2 * len(dys)
    return pl.pallas_call(
        functools.partial(fetch_kernel, n, dys),
        out_shape=pltpu.VMEM((count, decoder.shape[0], width), decoder.dtype),
        in_specs=[HBM, VMEM],
        out_specs=VMEM,
        scratch_shapes=[pltpu.SemaphoreType.DMA((count, FETCHES))],
        compiler_params=params(),
        cost_estimate=cost(0, decoder.shape[0] * count * width * 2),
        name="fetch",
    )(in_hbm(decoder), in_vmem(after))


def grad_kernel(n, slots, counts, final, with_prev, *refs):
    refs = list(refs)
    errs = [[refs.pop(0) for _ in range(count)] for count in counts]
    decoder_ref = refs.pop(0)
    total = refs.pop(0)[...] if with_prev else None
    for parts, slot in zip(errs, slots):
        err = parts[0][...] if len(parts) == 1 else jnp.concatenate([e[...] for e in parts], axis=0)
        part = lax.dot_general(
            err,
            decoder_ref[slot],
            (((1,), (1,)), ((), ())),
            preferred_element_type=jnp.float32,
        )
        total = part if total is None else total + part
    if not final:
        refs[0][...] = total
        return
    ids_ref, loss_ref, out_ref, totals_ref = refs
    totals_ref[...] = total
    rows, k_count = ids_ref.shape
    lat_dev = total.shape[1]
    own = out_ref.shape[1]
    fz, _, _ = factors(n)
    me = lax.axis_index("lat")
    z, _, _ = place(n, me)
    group = rows // fz
    places = lax.broadcasted_iota(jnp.int32, (ROW_STEP, LANES), 1)
    pad = jnp.zeros((ROW_STEP, LANES - k_count), jnp.int32)
    for q, j in enumerate([0] + z_order(fz)):
        for s in range(0, group, ROW_STEP):
            first = (z ^ j) * group + s
            rows_at = pl.ds(pl.multiple_of(first, ROW_STEP), ROW_STEP)
            ids = jnp.concatenate([ids_ref[rows_at, :] - me * lat_dev, pad], axis=1)
            held = jnp.where(places < k_count, ids // LANES, -1)
            inside = ids % LANES
            acc = jnp.zeros((ROW_STEP, LANES), jnp.float32)
            if q == 0:
                acc = jnp.where(places == k_count, loss_ref[s : s + ROW_STEP, :], acc)
            here = slice(q * group + s, q * group + s + ROW_STEP)
            for t in range(lat_dev // LANES):
                values = totals_ref[here, t * LANES : (t + 1) * LANES]
                found = jnp.take_along_axis(values, inside, axis=1, mode="promise_in_bounds")
                acc = jnp.where(held == t, found, acc)
            for d in range(ROW_STEP // own):
                out_ref[first // own + d] = acc[d * own : (d + 1) * own, :]


def grad(n, rows, pieces, decoder, prev, final=None):
    count, lat_dev, _ = decoder.shape
    slots = tuple(dc * (count // 2) + dy % (count // 2) for (dc, dy), _ in pieces)
    counts = tuple(len(e) for _, e in pieces)
    args = [x for _, e in pieces for x in e] + [in_vmem(decoder)]
    if prev is not None:
        args.append(in_vmem(prev))
    if final is not None:
        args += list(final)
    totals = pltpu.VMEM((rows, lat_dev), jnp.float32)
    size = pieces[0][1][0].shape[1] * len(pieces)
    return pl.pallas_call(
        functools.partial(grad_kernel, n, slots, counts, final is not None, prev is not None),
        out_shape=totals if final is None else jax.ShapeDtypeStruct((n, rows // n, LANES), jnp.float32),
        in_specs=[VMEM] * len(args),
        out_specs=VMEM,
        scratch_shapes=[] if final is None else [totals],
        compiler_params=params(),
        cost_estimate=cost(2 * rows * lat_dev * size, 4 * lat_dev * size),
        name="grad",
    )(*args)


def own_kernel(n, blocks, own, *refs):
    errs, out_ref = refs[:-1], refs[-1]
    _, fy, fc = factors(n)
    _, y, c = place(n, lax.axis_index("lat"))
    group, sub = errs[0].shape
    row = lax.broadcasted_iota(jnp.int32, (own, group), 0) + (y * fc + c) * own
    want = lax.broadcasted_iota(jnp.int32, (own, group), 1)
    mine = jnp.where(row == want, 1.0, 0.0).astype(jnp.bfloat16)
    for err, (dc, dy) in zip(errs, blocks):
        rows = jnp.dot(mine, err[...], preferred_element_type=jnp.float32)
        out_ref[:, pl.ds(column(n, 0, 1, sub, dy, dc), sub)] = rows.astype(jnp.bfloat16)


def own_rows(n, blocks, own, width, errs):
    return pl.pallas_call(
        functools.partial(own_kernel, n, tuple(blocks), own),
        out_shape=jax.ShapeDtypeStruct((own, width), jnp.bfloat16),
        in_specs=[VMEM] * len(errs),
        out_specs=VMEM,
        compiler_params=params(),
        name="own_rows",
    )(*errs)


def local(codes, indices, decoder, targets):
    width = decoder.shape[1]
    rows, k_count = codes.shape
    n = lax.axis_size("lat")
    own = rows // n
    fz, fy, fc = factors(n)
    group = rows // fz
    chunks = CHUNKS
    sub = width // (fc * fy * chunks)
    z, _, _ = place(n, lax.axis_index("lat"))

    def swap(x, dz=0, dy=0, dc=0):
        return lax.ppermute(x, "lat", pairs(n, dz, dy, dc))

    def join(xs, axis):
        return xs[0] if len(xs) == 1 else jnp.concatenate(xs, axis=axis)

    def in_order(xs, after=None):
        for i, x in enumerate(xs):
            if after is not None:
                xs[i] = hold(x, after)
            after = xs[i]
        return xs

    others = tuple((p, 1) for p in range(chunks))
    *parts, dense, columns = decode(
        n, chunks, sub, others, decoder, targets, (indices, codes), ((0, 0),)
    )
    came = [swap(part, dc=1) for part in parts]
    summed, leaving, after = [], [], None
    for p in range(chunks):
        (part,) = decode(
            n, chunks, sub, ((p, 0),), decoder if p else columns, targets, dense=dense, after=after
        )
        total = part + came[p]
        blocks = [total[:, o * sub : (o + 1) * sub] for o in range(fy)]
        got = None
        for b in reversed(bits(fy)):
            if got is not None:
                blocks = [blocks[o] + got[:, o * sub : (o + 1) * sub] for o in range(2 * b)]
            after = join(blocks[b:], 1)
            got = swap(after, dy=b)
        leaving.append(after)
        summed.append((blocks[0], got))

    wide = chunks * sub
    half = fy // 2
    near_columns = fetch(n, wide, tuple(range(half)), decoder, leaving[-1])
    sums, moved = [], []
    for p, (x, y) in enumerate(summed):
        x = x + (hold(y, near_columns) if p == 0 else y)
        sums.append(lax.dynamic_slice_in_dim(x, z * group, group, 0))
        moved.append(
            [
                swap(lax.dynamic_slice_in_dim(x, (z ^ j) * group, group, 0), dz=j)
                for j in z_order(fz)
            ]
        )
    errs, loss, after = [], 0.0, sums[-1]
    for p in range(chunks):
        diff = sum(in_order(moved[p], after), sums[p])
        loss = loss + jnp.sum(diff * diff, axis=1, keepdims=True)
        errs.append(diff.astype(jnp.bfloat16))
        after = errs[p]

    err = join(errs, 1)
    come = [swap(err, dz=j) for j in z_order(fz)]
    far_columns = fetch(n, wide, tuple(range(half, fy)), decoder, err)
    own_part = swap(err, dy=1)
    come = in_order(come[:-1], far_columns) + come[-1:]
    own_part = hold(own_part, come[-2])
    come[-1] = hold(come[-1], own_part)
    near = [((0, 0), [err, join(come[:-1], 0), come[-1]])]
    for b in bits(fy):
        last = [
            ((0, b | at[1]), in_order([own_part if e is err else swap(e, dy=b) for e in parts]))
            for at, parts in near
        ]
        near += last
    near = near[: -len(last)]

    def to_core(pieces):
        sent = swap(join([e for _, parts in pieces for e in parts], 0), dc=1)
        return [((1, at[1]), [sent[i * rows : (i + 1) * rows]]) for i, (at, _) in enumerate(pieces)]

    far = to_core(near)
    totals = grad(n, rows, near, near_columns, None)
    totals = grad(n, rows, far, near_columns, totals)
    last[-1][1][-1] = hold(last[-1][1][-1], totals)
    far_last = to_core(last)
    totals = grad(n, rows, last, far_columns, totals)
    back = grad(n, rows, far_last, far_columns, totals, (indices, loss))
    pieces = near + far + last + far_last
    error = own_rows(n, [at for at, _ in pieces], own, width, [e[0][:group] for _, e in pieces])

    back = jnp.sum(lax.all_to_all(back, "lat", 0, 0, tiled=True), axis=0)
    return error, back[:, k_count] / width, back[:, :k_count]


def solution(mesh):
    in_specs = (P("groups", None), P("groups", None), P("lat", None), P(("groups", "lat"), None))
    out_specs = (P(("groups", "lat"), None), P(("groups", "lat")), P(("groups", "lat"), None))
    return jax.shard_map(local, mesh=mesh, in_specs=in_specs, out_specs=out_specs, check_vma=False)
```

```python
import functools

import jax
import jax.numpy as jnp
from jax import lax
from jax.experimental import pallas as pl
from jax.experimental.pallas import tpu as pltpu
from jax.sharding import PartitionSpec as P

CHUNKS = 2
ROW_STEP = 16
LANES = 128
SUBLANES = 8
LOADS = 8
VMEM = pl.BlockSpec(memory_space=pltpu.VMEM)
HBM = pl.BlockSpec(memory_space=pltpu.HBM)


def factors(n):
    assert n > 1 and n & (n - 1) == 0
    c = 2
    m = n // c
    y = 1
    while 4 * y * y <= m:
        y *= 2
    return m // y, y, c


def place(n, index):
    _, y, c = factors(n)
    return index // (y * c), (index // c) % y, index % c


def bits(size):
    return [1 << i for i in range(size.bit_length() - 1)]


def z_order(fz):
    return ([fz - 1] if fz > 1 else []) + list(range(1, fz - 1))


def pairs(n, dz, dy, dc):
    _, fy, fc = factors(n)
    out = []
    for i in range(n):
        z, y, c = place(n, i)
        out.append((i, ((z ^ dz) * fy + (y ^ dy)) * fc + (c ^ dc)))
    return out


def cost(flops, size):
    return pl.CostEstimate(flops=flops, bytes_accessed=size, transcendentals=0)


def params():
    return pltpu.CompilerParams(vmem_limit_bytes=24 * 1024 * 1024)


def in_hbm(x):
    return pltpu.with_memory_space_constraint(x, pltpu.HBM)


def in_vmem(x):
    return pltpu.with_memory_space_constraint(x, pltpu.VMEM)


def column(n, chunk, chunks, sub, dy, dc):
    _, fy, fc = factors(n)
    _, y, c = place(n, lax.axis_index("lat"))
    return pl.multiple_of((((c ^ dc) * fy + (y ^ dy)) * chunks + chunk) * sub, sub)


def hold(x, *after):
    return pl.pallas_call(
        lambda *refs: None,
        out_shape=jax.ShapeDtypeStruct(x.shape, x.dtype),
        in_specs=[VMEM] * (1 + len(after)),
        out_specs=VMEM,
        input_output_aliases={0: 0},
        compiler_params=params(),
        name="hold",
    )(*[in_vmem(a) for a in (x, *after)])


def loads_of(decoder_hbm, col, buf, sem):
    count = sem.shape[0]
    step = buf.shape[0] // count
    return [
        pltpu.make_async_copy(
            decoder_hbm.at[pl.ds(i * step, step), pl.ds(col, buf.shape[1])],
            buf.at[pl.ds(i * step, step)],
            sem.at[i],
        )
        for i in range(count)
    ]


def decode_kernel(n, own, chunks, parts, first, *refs):
    fz, fy, fc = factors(n)
    me = lax.axis_index("lat")
    refs = list(refs)
    if first:
        ids_hbm, codes_hbm = refs.pop(0), refs.pop(0)
    else:
        dense_ref = refs.pop(0)
    decoder_hbm, targets_hbm = refs.pop(0), refs.pop(0)
    if len(refs) > 4 + len(parts) and not first:
        refs.pop(0)
    outs = [refs.pop(0) for _ in parts]
    if first:
        dense_ref = refs.pop(0)
    buf, sem, targets_ref, small = refs[:4]
    smalls_in = [(targets_hbm, targets_ref)]
    if first:
        ids_ref, codes_ref = refs[4:]
        smalls_in = [(ids_hbm, ids_ref), (codes_hbm, codes_ref)] + smalls_in
    smalls = [pltpu.make_async_copy(a, b, small.at[i]) for i, (a, b) in enumerate(smalls_in)]
    for copy in smalls:
        copy.start()
    rows, lat_dev = dense_ref.shape
    sub = outs[0].shape[1] // fy
    cols = [column(n, p, chunks, sub, o, dc) for p, dc in parts for o in range(fy)]
    if first:
        _, _, c = place(n, me)
        slab = pl.multiple_of((c ^ 1) * buf.shape[2], buf.shape[2])
        loads = [loads_of(decoder_hbm, slab, buf.at[0], sem.at[0])]
    else:
        loads = [loads_of(decoder_hbm, col, buf.at[i], sem.at[i]) for i, col in enumerate(cols)]
    for copies in loads:
        for copy in copies:
            copy.start()
    for copy in smalls:
        copy.wait()
    if first:
        k_count = ids_ref.shape[1]
        lanes = lax.broadcasted_iota(jnp.int32, (ROW_STEP, lat_dev), 1) + me * lat_dev

        def body(g, carry):
            at = pl.ds(pl.multiple_of(g * ROW_STEP, ROW_STEP), ROW_STEP)
            ids = ids_ref[at, :]
            codes = codes_ref[at, :].astype(jnp.float32)
            acc = jnp.zeros((ROW_STEP, lat_dev), jnp.float32)
            for k in range(k_count):
                acc = jnp.where(ids[:, k : k + 1] == lanes, codes[:, k : k + 1], acc)
            dense_ref[at, :] = acc.astype(jnp.bfloat16)
            return carry

        lax.fori_loop(0, rows // ROW_STEP, body, 0)
        for copy in loads[0]:
            copy.wait()
    per = SUBLANES // own
    tile = pl.ds(pl.multiple_of(me // per * SUBLANES, SUBLANES), SUBLANES)
    mine = lax.broadcasted_iota(jnp.int32, (SUBLANES, sub), 0) // own == me % per
    for i, col in enumerate(cols):
        if first:
            columns = buf[0, :, pl.ds(pl.multiple_of(col - slab, sub), sub)]
        else:
            for copy in loads[i]:
                copy.wait()
            columns = buf[i]
        out_ref = outs[i // fy]
        here = slice(i % fy * sub, (i % fy + 1) * sub)
        out_ref[:, here] = jnp.dot(dense_ref[...], columns, preferred_element_type=jnp.float32)
        target = targets_ref[:, pl.ds(col, sub)].astype(jnp.float32)
        target = jnp.concatenate([target] * per, axis=0)
        out_ref[tile, here] -= jnp.where(mine, target, 0.0)


def decode(n, chunks, sub, parts, decoder, targets, start=None, dense=None, after=None):
    _, fy, _ = factors(n)
    first = start is not None
    rows = start[0].shape[0] if first else dense.shape[0]
    lat_dev = decoder.shape[0]
    out = [pltpu.VMEM((rows, fy * sub), jnp.float32)] * len(parts)
    count = len(parts) * fy
    blocks = (1, lat_dev, count * sub) if first else (count, lat_dev, sub)
    scratch = [
        pltpu.VMEM(blocks, jnp.bfloat16),
        pltpu.SemaphoreType.DMA((blocks[0], LOADS if first else 2)),
        pltpu.VMEM(targets.shape, targets.dtype),
        pltpu.SemaphoreType.DMA((3,)),
    ]
    if first:
        args = [in_hbm(x) for x in (*start, decoder, targets)]
        specs = [HBM] * 4
        out.append(pltpu.VMEM((rows, lat_dev), jnp.bfloat16))
        scratch += [pltpu.VMEM(x.shape, x.dtype) for x in start]
    else:
        args, specs = [dense, in_hbm(decoder), in_hbm(targets)], [VMEM, HBM, HBM]
        if after is not None:
            args.append(in_vmem(after))
            specs.append(VMEM)
    return pl.pallas_call(
        functools.partial(decode_kernel, n, rows // n, chunks, parts, first),
        out_shape=out,
        in_specs=specs,
        out_specs=[VMEM] * len(out),
        scratch_shapes=scratch,
        compiler_params=params(),
        cost_estimate=cost(2 * rows * lat_dev * count * sub, 4 * lat_dev * count * sub),
        name="decode",
    )(*args)


def grad_kernel(n, counts, here, then, final, *refs):
    refs = list(refs)
    errs = [[refs.pop(0) for _ in range(count)] for count in counts]
    decoder_hbm = None if final else refs.pop(0)
    if here:
        total, columns_ref = None, refs[-2]
    else:
        columns_ref, total = refs.pop(0), refs.pop(0)[...]
    loads, later = [], []
    if not final:
        out_ref, next_ref, sem = refs[0], refs[1], refs[-1]
        wide = next_ref.shape[2]
        for i, (dc, dy) in enumerate(here):
            col = column(n, 0, 1, wide, dy, dc)
            loads.append(loads_of(decoder_hbm, col, columns_ref.at[i], sem.at[len(then) + i]))
        for i, (dc, dy) in enumerate(then):
            later += loads_of(decoder_hbm, column(n, 0, 1, wide, dy, dc), next_ref.at[i], sem.at[i])
        for copy in sum(loads, []) + later:
            copy.start()
    for i, parts in enumerate(errs):
        if loads:
            for copy in loads[i]:
                copy.wait()
        err = parts[0][...] if len(parts) == 1 else jnp.concatenate([e[...] for e in parts], axis=0)
        part = lax.dot_general(
            err,
            columns_ref[i],
            (((1,), (1,)), ((), ())),
            preferred_element_type=jnp.float32,
        )
        total = part if total is None else total + part
    if not final:
        out_ref[...] = total
        for copy in later:
            copy.wait()
        return
    ids_ref, loss_ref, out_ref, totals_ref = refs
    totals_ref[...] = total
    rows, k_count = ids_ref.shape
    lat_dev = total.shape[1]
    own = out_ref.shape[1]
    fz, _, _ = factors(n)
    me = lax.axis_index("lat")
    z, _, _ = place(n, me)
    group = rows // fz
    places = lax.broadcasted_iota(jnp.int32, (ROW_STEP, LANES), 1)
    pad = jnp.zeros((ROW_STEP, LANES - k_count), jnp.int32)
    for q, j in enumerate([0] + z_order(fz)):
        for s in range(0, group, ROW_STEP):
            first = (z ^ j) * group + s
            rows_at = pl.ds(pl.multiple_of(first, ROW_STEP), ROW_STEP)
            ids = jnp.concatenate([ids_ref[rows_at, :] - me * lat_dev, pad], axis=1)
            held = jnp.where(places < k_count, ids // LANES, -1)
            inside = ids % LANES
            acc = jnp.zeros((ROW_STEP, LANES), jnp.float32)
            if q == 0:
                acc = jnp.where(places == k_count, loss_ref[s : s + ROW_STEP, :], acc)
            here = slice(q * group + s, q * group + s + ROW_STEP)
            for t in range(lat_dev // LANES):
                values = totals_ref[here, t * LANES : (t + 1) * LANES]
                found = jnp.take_along_axis(values, inside, axis=1, mode="promise_in_bounds")
                acc = jnp.where(held == t, found, acc)
            for d in range(ROW_STEP // own):
                out_ref[first // own + d] = acc[d * own : (d + 1) * own, :]


def grad(n, rows, pieces, decoder, prev, then=(), final=None):
    lat_dev = decoder.shape[0]
    wide = pieces[0][1][0].shape[1]
    counts = tuple(len(e) for _, e in pieces)
    here = tuple(at for at, _ in pieces) if prev is None else ()
    args, specs = [x for _, e in pieces for x in e], []
    specs = [VMEM] * len(args)
    if final is None:
        args.append(in_hbm(decoder))
        specs.append(HBM)
    for x in reversed(prev or ()):
        args.append(in_vmem(x))
        specs.append(VMEM)
    totals = pltpu.VMEM((rows, lat_dev), jnp.float32)
    if final is None:
        out = [totals, pltpu.VMEM((len(then), lat_dev, wide), jnp.bfloat16)]
        scratch = [pltpu.VMEM((len(here), lat_dev, wide), jnp.bfloat16)] if here else []
        scratch.append(pltpu.SemaphoreType.DMA((len(then) + len(here), LOADS // 2)))
    else:
        args += list(final)
        specs += [VMEM] * len(final)
        out = jax.ShapeDtypeStruct((n, rows // n, LANES), jnp.float32)
        scratch = [totals]
    size = wide * len(pieces)
    return pl.pallas_call(
        functools.partial(grad_kernel, n, counts, here, then, final is not None),
        out_shape=out,
        in_specs=specs,
        out_specs=VMEM if final is not None else [VMEM, VMEM],
        scratch_shapes=scratch,
        compiler_params=params(),
        cost_estimate=cost(2 * rows * lat_dev * size, 4 * lat_dev * size),
        name="grad",
    )(*args)


def own_kernel(n, blocks, own, *refs):
    errs, out_ref = refs[:-1], refs[-1]
    _, fy, fc = factors(n)
    _, y, c = place(n, lax.axis_index("lat"))
    group, sub = errs[0].shape
    row = lax.broadcasted_iota(jnp.int32, (own, group), 0) + (y * fc + c) * own
    want = lax.broadcasted_iota(jnp.int32, (own, group), 1)
    mine = jnp.where(row == want, 1.0, 0.0).astype(jnp.bfloat16)
    for err, (dc, dy) in zip(errs, blocks):
        rows = jnp.dot(mine, err[...], preferred_element_type=jnp.float32)
        out_ref[:, pl.ds(column(n, 0, 1, sub, dy, dc), sub)] = rows.astype(jnp.bfloat16)


def own_rows(n, blocks, own, width, errs):
    return pl.pallas_call(
        functools.partial(own_kernel, n, tuple(blocks), own),
        out_shape=jax.ShapeDtypeStruct((own, width), jnp.bfloat16),
        in_specs=[VMEM] * len(errs),
        out_specs=VMEM,
        compiler_params=params(),
        name="own_rows",
    )(*errs)


def local(codes, indices, decoder, targets):
    width = decoder.shape[1]
    rows, k_count = codes.shape
    n = lax.axis_size("lat")
    own = rows // n
    fz, fy, fc = factors(n)
    group = rows // fz
    chunks = CHUNKS
    sub = width // (fc * fy * chunks)
    z, _, _ = place(n, lax.axis_index("lat"))

    def swap(x, dz=0, dy=0, dc=0):
        return lax.ppermute(x, "lat", pairs(n, dz, dy, dc))

    def join(xs, axis):
        return xs[0] if len(xs) == 1 else jnp.concatenate(xs, axis=axis)

    def in_order(xs, after=None):
        for i, x in enumerate(xs):
            if after is not None:
                xs[i] = hold(x, after)
            after = xs[i]
        return xs

    others = tuple((p, 1) for p in range(chunks))
    *parts, dense = decode(n, chunks, sub, others, decoder, targets, (indices, codes))
    came = [swap(part, dc=1) for part in parts]
    summed, leaving, after = [], [], None
    for p in range(chunks):
        (part,) = decode(n, chunks, sub, ((p, 0),), decoder, targets, dense=dense, after=after)
        total = part + came[p]
        blocks = [total[:, o * sub : (o + 1) * sub] for o in range(fy)]
        got = None
        for b in reversed(bits(fy)):
            if got is not None:
                blocks = [blocks[o] + got[:, o * sub : (o + 1) * sub] for o in range(2 * b)]
            after = join(blocks[b:], 1)
            got = swap(after, dy=b)
        leaving.append(after)
        summed.append((blocks[0], got))

    sums, moved = [], []
    for p, (x, y) in enumerate(summed):
        x = x + (hold(y, leaving[-1]) if p == 0 else y)
        sums.append(lax.dynamic_slice_in_dim(x, z * group, group, 0))
        moved.append(
            [
                swap(lax.dynamic_slice_in_dim(x, (z ^ j) * group, group, 0), dz=j)
                for j in z_order(fz)
            ]
        )
    errs, loss, after = [], 0.0, sums[-1]
    for p in range(chunks):
        diff = sum(in_order(moved[p], after), sums[p])
        loss = loss + jnp.sum(diff * diff, axis=1, keepdims=True)
        errs.append(diff.astype(jnp.bfloat16))
        after = errs[p]

    err = join(errs, 1)
    come = [swap(err, dz=j) for j in z_order(fz)]
    own_part = swap(err, dy=1)
    come = in_order(come[:-1] + [own_part] + come[-1:])
    own_part = come.pop(-2)
    near = [((0, 0), [err, join(come, 0)])]
    for b in bits(fy):
        last = [
            ((0, b | at[1]), in_order([own_part if e is err else swap(e, dy=b) for e in parts]))
            for at, parts in near
        ]
        near += last
    near = near[: -len(last)]
    half = rows // 2

    def halves(parts):
        whole = join(parts, 0)
        return [whole[:group], whole[group : group + half], whole[group + half :]]

    far = [((1, at[1]), [swap(e, dc=1) for e in halves(parts)]) for at, parts in near]
    far_last = [(1, at[1]) for at, _ in last]
    sums = grad(n, rows, near, decoder, None, tuple(at for at, _ in far))
    sums = grad(n, rows, far, decoder, sums, tuple(at for at, _ in last))
    last[-1][1][-1] = hold(last[-1][1][-1], sums[0])
    far_last = [
        (at, [swap(join(parts, 0), dc=1)]) for at, (_, parts) in zip(far_last, last)
    ]
    sums = grad(n, rows, last, decoder, sums, tuple(at for at, _ in far_last))
    back = grad(n, rows, far_last, decoder, sums, (), (indices, loss))
    pieces = near + far + last + far_last
    error = own_rows(n, [at for at, _ in pieces], own, width, [e[0][:group] for _, e in pieces])

    back = jnp.sum(lax.all_to_all(back, "lat", 0, 0, tiled=True), axis=0)
    return error, back[:, k_count] / width, back[:, :k_count]


def solution(mesh):
    in_specs = (P("groups", None), P("groups", None), P("lat", None), P(("groups", "lat"), None))
    out_specs = (P(("groups", "lat"), None), P(("groups", "lat")), P(("groups", "lat"), None))
    return jax.shard_map(local, mesh=mesh, in_specs=in_specs, out_specs=out_specs, check_vma=False)
```

```python
import functools

import jax
import jax.numpy as jnp
from jax import lax
from jax.experimental import pallas as pl
from jax.experimental.pallas import tpu as pltpu
from jax.sharding import PartitionSpec as P

CHUNKS = 2
ROW_STEP = 16
LANES = 128
SUBLANES = 8
LOADS = 4
VMEM = pl.BlockSpec(memory_space=pltpu.VMEM)
HBM = pl.BlockSpec(memory_space=pltpu.HBM)


def factors(n):
    assert n > 1 and n & (n - 1) == 0
    c = 2
    m = n // c
    y = 1
    while 4 * y * y <= m:
        y *= 2
    return m // y, y, c


def place(n, index):
    _, y, c = factors(n)
    return index // (y * c), (index // c) % y, index % c


def bits(size):
    return [1 << i for i in range(size.bit_length() - 1)]


def z_order(fz):
    return ([fz - 1] if fz > 1 else []) + list(range(1, fz - 1))


def pairs(n, dz, dy, dc):
    _, fy, fc = factors(n)
    out = []
    for i in range(n):
        z, y, c = place(n, i)
        out.append((i, ((z ^ dz) * fy + (y ^ dy)) * fc + (c ^ dc)))
    return out


def cost(flops, size):
    return pl.CostEstimate(flops=flops, bytes_accessed=size, transcendentals=0)


def params():
    return pltpu.CompilerParams(vmem_limit_bytes=24 * 1024 * 1024)


def in_hbm(x):
    return pltpu.with_memory_space_constraint(x, pltpu.HBM)


def in_vmem(x):
    return pltpu.with_memory_space_constraint(x, pltpu.VMEM)


def column(n, chunk, chunks, sub, dy, dc):
    _, fy, fc = factors(n)
    _, y, c = place(n, lax.axis_index("lat"))
    return pl.multiple_of((((c ^ dc) * fy + (y ^ dy)) * chunks + chunk) * sub, sub)


def hold(x, *after):
    return pl.pallas_call(
        lambda *refs: None,
        out_shape=jax.ShapeDtypeStruct(x.shape, x.dtype),
        in_specs=[VMEM] * (1 + len(after)),
        out_specs=VMEM,
        input_output_aliases={0: 0},
        compiler_params=params(),
        name="hold",
    )(*[in_vmem(a) for a in (x, *after)])


def loads_of(decoder_hbm, col, buf, sem):
    count = sem.shape[0]
    step = buf.shape[0] // count
    return [
        pltpu.make_async_copy(
            decoder_hbm.at[pl.ds(i * step, step), pl.ds(col, buf.shape[1])],
            buf.at[pl.ds(i * step, step)],
            sem.at[i],
        )
        for i in range(count)
    ]


def decode_kernel(n, own, chunks, parts, first, *refs):
    fz, fy, fc = factors(n)
    me = lax.axis_index("lat")
    refs = list(refs)
    if first:
        ids_hbm, codes_hbm = refs.pop(0), refs.pop(0)
    else:
        dense_ref = refs.pop(0)
    decoder_hbm, targets_hbm = refs.pop(0), refs.pop(0)
    if len(refs) > 4 + len(parts) and not first:
        refs.pop(0)
    outs = [refs.pop(0) for _ in parts]
    if first:
        dense_ref = refs.pop(0)
    buf, sem, targets_ref, small = refs[:4]
    smalls_in = [(targets_hbm, targets_ref)]
    if first:
        ids_ref, codes_ref = refs[4:]
        smalls_in = [(ids_hbm, ids_ref), (codes_hbm, codes_ref)] + smalls_in
    smalls = [pltpu.make_async_copy(a, b, small.at[i]) for i, (a, b) in enumerate(smalls_in)]
    for copy in smalls:
        copy.start()
    rows, lat_dev = dense_ref.shape
    sub = outs[0].shape[1] // fy
    cols = [column(n, p, chunks, sub, o, dc) for p, dc in parts for o in range(fy)]
    loads = [loads_of(decoder_hbm, col, buf.at[i], sem.at[i]) for i, col in enumerate(cols)]
    for copies in loads:
        for copy in copies:
            copy.start()
    for copy in smalls:
        copy.wait()
    if first:
        k_count = ids_ref.shape[1]
        lanes = lax.broadcasted_iota(jnp.int32, (ROW_STEP, lat_dev), 1) + me * lat_dev

        def body(g, carry):
            at = pl.ds(pl.multiple_of(g * ROW_STEP, ROW_STEP), ROW_STEP)
            ids = ids_ref[at, :]
            codes = codes_ref[at, :].astype(jnp.float32)
            acc = jnp.zeros((ROW_STEP, lat_dev), jnp.float32)
            for k in range(k_count):
                acc = jnp.where(ids[:, k : k + 1] == lanes, codes[:, k : k + 1], acc)
            dense_ref[at, :] = acc.astype(jnp.bfloat16)
            return carry

        lax.fori_loop(0, rows // ROW_STEP, body, 0)
    per = SUBLANES // own
    tile = pl.ds(pl.multiple_of(me // per * SUBLANES, SUBLANES), SUBLANES)
    mine = lax.broadcasted_iota(jnp.int32, (SUBLANES, sub), 0) // own == me % per
    for i, col in enumerate(cols):
        for copy in loads[i]:
            copy.wait()
        out_ref = outs[i // fy]
        here = slice(i % fy * sub, (i % fy + 1) * sub)
        out_ref[:, here] = jnp.dot(dense_ref[...], buf[i], preferred_element_type=jnp.float32)
        target = targets_ref[:, pl.ds(col, sub)].astype(jnp.float32)
        target = jnp.concatenate([target] * per, axis=0)
        out_ref[tile, here] -= jnp.where(mine, target, 0.0)


def decode(n, chunks, sub, parts, decoder, targets, start=None, dense=None, after=None):
    _, fy, _ = factors(n)
    first = start is not None
    rows = start[0].shape[0] if first else dense.shape[0]
    lat_dev = decoder.shape[0]
    out = [pltpu.VMEM((rows, fy * sub), jnp.float32)] * len(parts)
    count = len(parts) * fy
    scratch = [
        pltpu.VMEM((count, lat_dev, sub), jnp.bfloat16),
        pltpu.SemaphoreType.DMA((count, 1)),
        pltpu.VMEM(targets.shape, targets.dtype),
        pltpu.SemaphoreType.DMA((3,)),
    ]
    if first:
        args = [in_hbm(x) for x in (*start, decoder, targets)]
        specs = [HBM] * 4
        out.append(pltpu.VMEM((rows, lat_dev), jnp.bfloat16))
        scratch += [pltpu.VMEM(x.shape, x.dtype) for x in start]
    else:
        args, specs = [dense, in_hbm(decoder), in_hbm(targets)], [VMEM, HBM, HBM]
        if after is not None:
            args.append(in_vmem(after))
            specs.append(VMEM)
    return pl.pallas_call(
        functools.partial(decode_kernel, n, rows // n, chunks, parts, first),
        out_shape=out,
        in_specs=specs,
        out_specs=[VMEM] * len(out),
        scratch_shapes=scratch,
        compiler_params=params(),
        cost_estimate=cost(2 * rows * lat_dev * count * sub, 4 * lat_dev * count * sub),
        name="decode",
    )(*args)


def fetch_kernel(n, places, decoder_hbm, _, *refs):
    outs, token_ref, sem = refs[:-2], refs[-2], refs[-1]
    copies = []
    for i, (dc, dy) in enumerate(places):
        col = column(n, 0, 1, outs[i].shape[1], dy, dc)
        copies += loads_of(decoder_hbm, col, outs[i], sem.at[i])
    for copy in copies:
        copy.start()
    token_ref[...] = jnp.zeros_like(token_ref)
    for copy in copies:
        copy.wait()


def fetch(n, width, places, decoder, after):
    block = pltpu.VMEM((decoder.shape[0], width), decoder.dtype)
    return pl.pallas_call(
        functools.partial(fetch_kernel, n, places),
        out_shape=[block] * len(places) + [pltpu.VMEM((SUBLANES, LANES), jnp.float32)],
        in_specs=[HBM, VMEM],
        out_specs=[VMEM] * (1 + len(places)),
        scratch_shapes=[pltpu.SemaphoreType.DMA((len(places), LOADS))],
        compiler_params=params(),
        cost_estimate=cost(0, decoder.shape[0] * len(places) * width * 2),
        name="fetch",
    )(in_hbm(decoder), in_vmem(after))


def grad_kernel(n, counts, with_prev, final, *refs):
    refs = list(refs)
    errs = [[refs.pop(0) for _ in range(count)] for count in counts]
    columns = [refs.pop(0) for _ in counts]
    total = refs.pop(0)[...] if with_prev else None
    for parts, columns_ref in zip(errs, columns):
        err = parts[0][...] if len(parts) == 1 else jnp.concatenate([e[...] for e in parts], axis=0)
        part = lax.dot_general(
            err,
            columns_ref[...],
            (((1,), (1,)), ((), ())),
            preferred_element_type=jnp.float32,
        )
        total = part if total is None else total + part
    if not final:
        refs[0][...] = total
        return
    ids_ref, loss_ref, out_ref, totals_ref = refs
    totals_ref[...] = total
    rows, k_count = ids_ref.shape
    lat_dev = total.shape[1]
    own = out_ref.shape[1]
    fz, _, _ = factors(n)
    me = lax.axis_index("lat")
    z, _, _ = place(n, me)
    group = rows // fz
    places = lax.broadcasted_iota(jnp.int32, (ROW_STEP, LANES), 1)
    pad = jnp.zeros((ROW_STEP, LANES - k_count), jnp.int32)
    for q, j in enumerate([0] + z_order(fz)):
        for s in range(0, group, ROW_STEP):
            first = (z ^ j) * group + s
            rows_at = pl.ds(pl.multiple_of(first, ROW_STEP), ROW_STEP)
            ids = jnp.concatenate([ids_ref[rows_at, :] - me * lat_dev, pad], axis=1)
            held = jnp.where(places < k_count, ids // LANES, -1)
            inside = ids % LANES
            acc = jnp.zeros((ROW_STEP, LANES), jnp.float32)
            if q == 0:
                acc = jnp.where(places == k_count, loss_ref[s : s + ROW_STEP, :], acc)
            here = slice(q * group + s, q * group + s + ROW_STEP)
            for t in range(lat_dev // LANES):
                values = totals_ref[here, t * LANES : (t + 1) * LANES]
                found = jnp.take_along_axis(values, inside, axis=1, mode="promise_in_bounds")
                acc = jnp.where(held == t, found, acc)
            for d in range(ROW_STEP // own):
                out_ref[first // own + d] = acc[d * own : (d + 1) * own, :]


def grad(n, rows, pieces, columns, prev, final=None):
    lat_dev, wide = columns[pieces[0][0]].shape
    counts = tuple(len(e) for _, e in pieces)
    args = [x for _, e in pieces for x in e] + [in_vmem(columns[at]) for at, _ in pieces]
    if prev is not None:
        args.append(in_vmem(prev))
    if final is not None:
        args += list(final)
    totals = pltpu.VMEM((rows, lat_dev), jnp.float32)
    size = wide * len(pieces)
    return pl.pallas_call(
        functools.partial(grad_kernel, n, counts, prev is not None, final is not None),
        out_shape=totals if final is None else jax.ShapeDtypeStruct((n, rows // n, LANES), jnp.float32),
        in_specs=[VMEM] * len(args),
        out_specs=VMEM,
        scratch_shapes=[] if final is None else [totals],
        compiler_params=params(),
        cost_estimate=cost(2 * rows * lat_dev * size, 4 * lat_dev * size),
        name="grad",
    )(*args)


def own_kernel(n, blocks, own, *refs):
    errs, out_ref = refs[:-1], refs[-1]
    _, fy, fc = factors(n)
    _, y, c = place(n, lax.axis_index("lat"))
    group, sub = errs[0].shape
    row = lax.broadcasted_iota(jnp.int32, (own, group), 0) + (y * fc + c) * own
    want = lax.broadcasted_iota(jnp.int32, (own, group), 1)
    mine = jnp.where(row == want, 1.0, 0.0).astype(jnp.bfloat16)
    for err, (dc, dy) in zip(errs, blocks):
        rows = jnp.dot(mine, err[...], preferred_element_type=jnp.float32)
        out_ref[:, pl.ds(column(n, 0, 1, sub, dy, dc), sub)] = rows.astype(jnp.bfloat16)


def own_rows(n, blocks, own, width, errs):
    return pl.pallas_call(
        functools.partial(own_kernel, n, tuple(blocks), own),
        out_shape=jax.ShapeDtypeStruct((own, width), jnp.bfloat16),
        in_specs=[VMEM] * len(errs),
        out_specs=VMEM,
        compiler_params=params(),
        name="own_rows",
    )(*errs)


def local(codes, indices, decoder, targets):
    width = decoder.shape[1]
    rows, k_count = codes.shape
    n = lax.axis_size("lat")
    own = rows // n
    fz, fy, fc = factors(n)
    group = rows // fz
    chunks = CHUNKS
    sub = width // (fc * fy * chunks)
    z, _, _ = place(n, lax.axis_index("lat"))

    def swap(x, dz=0, dy=0, dc=0):
        return lax.ppermute(x, "lat", pairs(n, dz, dy, dc))

    def join(xs, axis):
        return xs[0] if len(xs) == 1 else jnp.concatenate(xs, axis=axis)

    def in_order(xs, after=None):
        for i, x in enumerate(xs):
            if after is not None:
                xs[i] = hold(x, after)
            after = xs[i]
        return xs

    others = tuple((p, 1) for p in range(chunks))
    *parts, dense = decode(n, chunks, sub, others, decoder, targets, (indices, codes))
    came = [swap(part, dc=1) for part in parts]
    summed, leaving, after = [], [], None
    for p in range(chunks):
        (part,) = decode(n, chunks, sub, ((p, 0),), decoder, targets, dense=dense, after=after)
        total = part + came[p]
        blocks = [total[:, o * sub : (o + 1) * sub] for o in range(fy)]
        got = None
        for b in reversed(bits(fy)):
            if got is not None:
                blocks = [blocks[o] + got[:, o * sub : (o + 1) * sub] for o in range(2 * b)]
            after = join(blocks[b:], 1)
            got = swap(after, dy=b)
        leaving.append(after)
        summed.append((blocks[0], got))

    places = tuple((dc, dy) for dy in range(fy) for dc in range(fc))
    *columns, token = fetch(n, chunks * sub, places, decoder, leaving[-1])
    columns = dict(zip(places, columns))
    sums, moved = [], []
    for p, (x, y) in enumerate(summed):
        x = x + (hold(y, token) if p == 0 else y)
        sums.append(lax.dynamic_slice_in_dim(x, z * group, group, 0))
        moved.append(
            [
                swap(lax.dynamic_slice_in_dim(x, (z ^ j) * group, group, 0), dz=j)
                for j in z_order(fz)
            ]
        )
    errs, loss, after = [], 0.0, sums[-1]
    for p in range(chunks):
        diff = sum(in_order(moved[p], after), sums[p])
        loss = loss + jnp.sum(diff * diff, axis=1, keepdims=True)
        errs.append(diff.astype(jnp.bfloat16))
        after = errs[p]

    err = join(errs, 1)
    come = [swap(err, dz=j) for j in z_order(fz)]
    own_part = swap(err, dy=1)
    come = in_order(come[:-1] + [own_part] + come[-1:])
    own_part = come.pop(-2)
    near = [((0, 0), [err, join(come, 0)])]
    for b in bits(fy):
        last = [
            ((0, b | at[1]), in_order([own_part if e is err else swap(e, dy=b) for e in parts]))
            for at, parts in near
        ]
        near += last
    near = near[: -len(last)]
    half = rows // 2

    def halves(parts):
        whole = join(parts, 0)
        return [whole[:group], whole[group : group + half], whole[group + half :]]

    far = [((1, at[1]), [swap(e, dc=1) for e in halves(parts)]) for at, parts in near]
    totals = grad(n, rows, near, columns, None)
    totals = grad(n, rows, far, columns, totals)
    last[-1][1][-1] = hold(last[-1][1][-1], totals)
    far_last = [((1, at[1]), [swap(join(parts, 0), dc=1)]) for at, parts in last]
    totals = grad(n, rows, last, columns, totals)
    back = grad(n, rows, far_last, columns, totals, (indices, loss))
    pieces = near + far + last + far_last
    error = own_rows(n, [at for at, _ in pieces], own, width, [e[0][:group] for _, e in pieces])

    back = jnp.sum(lax.all_to_all(back, "lat", 0, 0, tiled=True), axis=0)
    return error, back[:, k_count] / width, back[:, :k_count]


def solution(mesh):
    in_specs = (P("groups", None), P("groups", None), P("lat", None), P(("groups", "lat"), None))
    out_specs = (P(("groups", "lat"), None), P(("groups", "lat")), P(("groups", "lat"), None))
    return jax.shard_map(local, mesh=mesh, in_specs=in_specs, out_specs=out_specs, check_vma=False)
```

```python
import functools

import jax
import jax.numpy as jnp
from jax import lax
from jax.experimental import pallas as pl
from jax.experimental.pallas import tpu as pltpu
from jax.sharding import PartitionSpec as P

CHUNKS = 2
ROW_STEP = 16
LANES = 128
SUBLANES = 8
LOADS = 4
VMEM = pl.BlockSpec(memory_space=pltpu.VMEM)
HBM = pl.BlockSpec(memory_space=pltpu.HBM)


def factors(n):
    assert n > 1 and n & (n - 1) == 0
    c = 2
    m = n // c
    y = 1
    while 4 * y * y <= m:
        y *= 2
    return m // y, y, c


def place(n, index):
    _, y, c = factors(n)
    return index // (y * c), (index // c) % y, index % c


def bits(size):
    return [1 << i for i in range(size.bit_length() - 1)]


def z_order(fz):
    return ([fz - 1] if fz > 1 else []) + list(range(1, fz - 1))


def pairs(n, dz, dy, dc):
    _, fy, fc = factors(n)
    out = []
    for i in range(n):
        z, y, c = place(n, i)
        out.append((i, ((z ^ dz) * fy + (y ^ dy)) * fc + (c ^ dc)))
    return out


def cost(flops, size):
    return pl.CostEstimate(flops=flops, bytes_accessed=size, transcendentals=0)


def params():
    return pltpu.CompilerParams(vmem_limit_bytes=24 * 1024 * 1024)


def in_hbm(x):
    return pltpu.with_memory_space_constraint(x, pltpu.HBM)


def in_vmem(x):
    return pltpu.with_memory_space_constraint(x, pltpu.VMEM)


def column(n, chunk, chunks, sub, dy, dc):
    _, fy, fc = factors(n)
    _, y, c = place(n, lax.axis_index("lat"))
    return pl.multiple_of((((c ^ dc) * fy + (y ^ dy)) * chunks + chunk) * sub, sub)


def hold(x, *after):
    def kernel(x_ref, *refs):
        refs[-1][...] = x_ref[...]

    return pl.pallas_call(
        kernel,
        out_shape=jax.ShapeDtypeStruct(x.shape, x.dtype),
        in_specs=[VMEM] * (1 + len(after)),
        out_specs=VMEM,
        input_output_aliases={0: 0},
        compiler_params=params(),
        name="hold",
    )(*[in_vmem(a) for a in (x, *after)])


def loads_of(decoder_hbm, col, buf, sem):
    count = sem.shape[0]
    step = buf.shape[0] // count
    return [
        pltpu.make_async_copy(
            decoder_hbm.at[pl.ds(i * step, step), pl.ds(col, buf.shape[1])],
            buf.at[pl.ds(i * step, step)],
            sem.at[i],
        )
        for i in range(count)
    ]


def add_targets(n, own, col, targets_ref, out_ref, here):
    me = lax.axis_index("lat")
    width = here.stop - here.start
    per = SUBLANES // own
    tile = pl.ds(pl.multiple_of(me // per * SUBLANES, SUBLANES), SUBLANES)
    mine = lax.broadcasted_iota(jnp.int32, (SUBLANES, width), 0) // own == me % per
    target = targets_ref[:, pl.ds(col, width)].astype(jnp.float32)
    target = jnp.concatenate([target] * per, axis=0)
    out_ref[tile, here] -= jnp.where(mine, target, 0.0)


def first_kernel(n, own, chunks, *refs):
    ids_hbm, codes_hbm, decoder_hbm, targets_hbm = refs[:4]
    outs = refs[4 : 4 + chunks]
    dense_ref, kept_ref, buf, sem, kept_sem, targets_ref, small, ids_ref, codes_ref = refs[4 + chunks :]
    _, fy, _ = factors(n)
    me = lax.axis_index("lat")
    smalls_in = [(ids_hbm, ids_ref), (codes_hbm, codes_ref), (targets_hbm, targets_ref)]
    smalls = [pltpu.make_async_copy(a, b, small.at[i]) for i, (a, b) in enumerate(smalls_in)]
    for copy in smalls:
        copy.start()
    rows, lat_dev = dense_ref.shape
    wide = buf.shape[2]
    sub = wide // chunks
    cols = [column(n, 0, 1, wide, o, 1) for o in range(fy)]
    loads = [loads_of(decoder_hbm, col, buf.at[i], sem.at[i]) for i, col in enumerate(cols)]
    later = []
    for o in range(fy):
        col = column(n, 0, chunks, sub, o, 0)
        later += loads_of(decoder_hbm, col, kept_ref.at[o], kept_sem.at[o])
    for copy in sum(loads, []) + later:
        copy.start()
    for copy in smalls:
        copy.wait()
    k_count = ids_ref.shape[1]
    lanes = lax.broadcasted_iota(jnp.int32, (ROW_STEP, lat_dev), 1) + me * lat_dev

    def body(g, carry):
        at = pl.ds(pl.multiple_of(g * ROW_STEP, ROW_STEP), ROW_STEP)
        ids = ids_ref[at, :]
        codes = codes_ref[at, :].astype(jnp.float32)
        acc = jnp.zeros((ROW_STEP, lat_dev), jnp.float32)
        for k in range(k_count):
            acc = jnp.where(ids[:, k : k + 1] == lanes, codes[:, k : k + 1], acc)
        dense_ref[at, :] = acc.astype(jnp.bfloat16)
        return carry

    lax.fori_loop(0, rows // ROW_STEP, body, 0)
    for o in range(fy):
        for copy in loads[o]:
            copy.wait()
        for p in range(chunks):
            here = slice(o * sub, (o + 1) * sub)
            outs[p][:, here] = jnp.dot(
                dense_ref[...], buf[o, :, p * sub : (p + 1) * sub], preferred_element_type=jnp.float32
            )
            add_targets(n, own, pl.multiple_of(cols[o] + p * sub, sub), targets_ref, outs[p], here)
    for copy in later:
        copy.wait()


def first_decode(n, chunks, sub, ids, codes, decoder, targets):
    _, fy, _ = factors(n)
    rows, lat_dev = ids.shape[0], decoder.shape[0]
    return pl.pallas_call(
        functools.partial(first_kernel, n, rows // n, chunks),
        out_shape=[pltpu.VMEM((rows, fy * sub), jnp.float32)] * chunks
        + [pltpu.VMEM((rows, lat_dev), jnp.bfloat16), pltpu.VMEM((fy, lat_dev, sub), jnp.bfloat16)],
        in_specs=[HBM] * 4,
        out_specs=[VMEM] * (chunks + 2),
        scratch_shapes=[
            pltpu.VMEM((fy, lat_dev, chunks * sub), jnp.bfloat16),
            pltpu.SemaphoreType.DMA((fy, LOADS)),
            pltpu.SemaphoreType.DMA((fy, LOADS)),
            pltpu.VMEM(targets.shape, targets.dtype),
            pltpu.SemaphoreType.DMA((3,)),
            pltpu.VMEM(ids.shape, ids.dtype),
            pltpu.VMEM(codes.shape, codes.dtype),
        ],
        compiler_params=params(),
        cost_estimate=cost(2 * rows * lat_dev * chunks * fy * sub, 4 * lat_dev * chunks * fy * sub),
        name="first_decode",
    )(*[in_hbm(x) for x in (ids, codes, decoder, targets)])


def decode_kernel(n, own, chunk, chunks, loaded, dense_ref, columns_ref, targets_hbm, *refs):
    _, fy, _ = factors(n)
    out_ref, targets_ref, small = refs[0 if loaded else 1 :][:3]
    copy_targets = pltpu.make_async_copy(targets_hbm, targets_ref, small)
    copy_targets.start()
    sub = out_ref.shape[1] // fy
    cols = [column(n, chunk, chunks, sub, o, 0) for o in range(fy)]
    loads, buf = [[]] * fy, columns_ref
    if not loaded:
        buf, sem = refs[4:]
        loads = [loads_of(columns_ref, col, buf.at[i], sem.at[i]) for i, col in enumerate(cols)]
        for copy in sum(loads, []):
            copy.start()
    for o, col in enumerate(cols):
        for copy in loads[o]:
            copy.wait()
        here = slice(o * sub, (o + 1) * sub)
        out_ref[:, here] = jnp.dot(dense_ref[...], buf[o], preferred_element_type=jnp.float32)
    copy_targets.wait()
    for o, col in enumerate(cols):
        add_targets(n, own, col, targets_ref, out_ref, slice(o * sub, (o + 1) * sub))


def decode(n, chunk, chunks, sub, dense, columns, targets, after=None):
    _, fy, _ = factors(n)
    loaded = columns.ndim == 3
    rows, lat_dev = dense.shape
    scratch = [pltpu.VMEM(targets.shape, targets.dtype), pltpu.SemaphoreType.DMA]
    if loaded:
        args, specs = [dense, in_vmem(columns), in_hbm(targets)], [VMEM, VMEM, HBM]
    else:
        args, specs = [dense, in_hbm(columns), in_hbm(targets), in_vmem(after)], [VMEM, HBM, HBM, VMEM]
        scratch += [
            pltpu.VMEM((fy, lat_dev, sub), jnp.bfloat16),
            pltpu.SemaphoreType.DMA((fy, LOADS)),
        ]
    return pl.pallas_call(
        functools.partial(decode_kernel, n, rows // n, chunk, chunks, loaded),
        out_shape=pltpu.VMEM((rows, fy * sub), jnp.float32),
        in_specs=specs,
        out_specs=VMEM,
        scratch_shapes=scratch,
        compiler_params=params(),
        cost_estimate=cost(2 * rows * lat_dev * fy * sub, 4 * lat_dev * fy * sub),
        name="decode",
    )(*args)


def fetch_kernel(n, places, decoder_hbm, ids_hbm, _, *refs):
    outs = refs[: len(places)]
    ids_ref, token_ref, sem, ids_sem = refs[len(places) :]
    copies = [pltpu.make_async_copy(ids_hbm, ids_ref, ids_sem)]
    for i, (dc, dy) in enumerate(places):
        col = column(n, 0, 1, outs[i].shape[1], dy, dc)
        copies += loads_of(decoder_hbm, col, outs[i], sem.at[i])
    for copy in copies:
        copy.start()
    token_ref[...] = jnp.zeros_like(token_ref)
    for copy in copies:
        copy.wait()


def fetch(n, width, places, decoder, ids, after):
    block = pltpu.VMEM((decoder.shape[0], width), decoder.dtype)
    return pl.pallas_call(
        functools.partial(fetch_kernel, n, places),
        out_shape=[block] * len(places)
        + [pltpu.VMEM(ids.shape, ids.dtype), pltpu.VMEM((SUBLANES, LANES), jnp.float32)],
        in_specs=[HBM, HBM, VMEM],
        out_specs=[VMEM] * (2 + len(places)),
        scratch_shapes=[pltpu.SemaphoreType.DMA((len(places), LOADS)), pltpu.SemaphoreType.DMA],
        compiler_params=params(),
        cost_estimate=cost(0, decoder.shape[0] * len(places) * width * 2),
        name="fetch",
    )(in_hbm(decoder), in_hbm(ids), in_vmem(after))


def grad_kernel(n, count, with_prev, final, *refs):
    refs = list(refs)
    errs = [refs.pop(0) for _ in range(count)]
    columns = [(refs.pop(0), refs.pop(0)) for _ in errs]
    prev_ref = refs.pop(0) if with_prev else None
    totals_ref, token_ref = (refs[-1], None) if final else refs
    for i, err in enumerate(errs):
        for core in range(2):
            part = lax.dot_general(
                err[...],
                columns[i][core][...],
                (((1,), (1,)), ((), ())),
                preferred_element_type=jnp.float32,
            )
            if i:
                part += totals_ref[core]
            elif with_prev:
                part += prev_ref[core]
            totals_ref[core] = part
    if not final:
        token_ref[...] = jnp.zeros_like(token_ref)
        return
    ids_ref, loss_ref, out_ref = refs[:3]
    rows, k_count = ids_ref.shape
    lat_dev = totals_ref.shape[2]
    own = out_ref.shape[1]
    fz, _, _ = factors(n)
    me = lax.axis_index("lat")
    z, _, _ = place(n, me)
    group = rows // fz
    places = lax.broadcasted_iota(jnp.int32, (ROW_STEP, LANES), 1)
    pad = jnp.zeros((ROW_STEP, LANES - k_count), jnp.int32)
    for q, j in enumerate([0] + z_order(fz)):
        for s in range(0, group, ROW_STEP):
            first = (z ^ j) * group + s
            rows_at = pl.ds(pl.multiple_of(first, ROW_STEP), ROW_STEP)
            ids = jnp.concatenate([ids_ref[rows_at, :], pad], axis=1)
            acc = jnp.zeros((ROW_STEP, LANES), jnp.float32)
            if q == 0:
                acc = jnp.where(places == k_count, loss_ref[s : s + ROW_STEP, :], acc)
            here = slice(q * group + s, q * group + s + ROW_STEP)
            for core in range(2):
                local_ids = ids - (me ^ core) * lat_dev
                held = jnp.where(places < k_count, local_ids // LANES, -1)
                inside = local_ids % LANES
                for t in range(lat_dev // LANES):
                    values = totals_ref[core, here, t * LANES : (t + 1) * LANES]
                    found = jnp.take_along_axis(values, inside, axis=1, mode="promise_in_bounds")
                    acc = jnp.where(held == t, found, acc)
            for d in range(ROW_STEP // own):
                out_ref[first // own + d] = acc[d * own : (d + 1) * own, :]


def grad(n, rows, pieces, columns, prev, final=None):
    lat_dev, wide = columns[pieces[0][0]][0].shape
    args = [e for _, e in pieces]
    args += [in_vmem(x) for at, _ in pieces for x in columns[at]]
    if prev is not None:
        args.append(in_vmem(prev))
    if final is not None:
        args += list(final)
    totals = pltpu.VMEM((2, rows, lat_dev), jnp.float32)
    size = 2 * wide * len(pieces)
    return pl.pallas_call(
        functools.partial(grad_kernel, n, len(pieces), prev is not None, final is not None),
        out_shape=[totals, pltpu.VMEM((SUBLANES, LANES), jnp.float32)]
        if final is None
        else jax.ShapeDtypeStruct((n, rows // n, LANES), jnp.float32),
        in_specs=[VMEM] * len(args),
        out_specs=[VMEM] * 2 if final is None else VMEM,
        scratch_shapes=[] if final is None else [totals],
        compiler_params=params(),
        cost_estimate=cost(2 * rows * lat_dev * size, 4 * lat_dev * size),
        name="grad",
    )(*args)


def own_kernel(n, places, *refs):
    parts, out_ref = refs[:-1], refs[-1]
    for part, (dc, dy) in zip(parts, places):
        width = part.shape[1]
        out_ref[:, pl.ds(column(n, 0, 1, width, dy, dc), width)] = part[...]


def own_rows(n, places, width, parts):
    return pl.pallas_call(
        functools.partial(own_kernel, n, places),
        out_shape=jax.ShapeDtypeStruct((parts[0].shape[0], width), jnp.bfloat16),
        in_specs=[VMEM] * len(parts),
        out_specs=VMEM,
        compiler_params=params(),
        name="own_rows",
    )(*parts)


def local(codes, indices, decoder, targets):
    width = decoder.shape[1]
    rows, k_count = codes.shape
    n = lax.axis_size("lat")
    own = rows // n
    fz, fy, fc = factors(n)
    group = rows // fz
    chunks = CHUNKS
    wide = width // (fc * fy)
    sub = wide // chunks
    z, y_at, core_at = place(n, lax.axis_index("lat"))

    def swap(x, dz=0, dy=0, dc=0):
        return lax.ppermute(x, "lat", pairs(n, dz, dy, dc))

    def join(xs, axis):
        return xs[0] if len(xs) == 1 else jnp.concatenate(xs, axis=axis)

    def in_order(xs, after=None):
        for i, x in enumerate(xs):
            if after is not None:
                xs[i] = hold(x, after)
            after = xs[i]
        return xs

    *parts, dense, columns = first_decode(n, chunks, sub, indices, codes, decoder, targets)
    came = [swap(part, dc=1) for part in parts]
    summed, leaving, after = [], [], None
    for p in range(chunks):
        part = decode(n, p, chunks, sub, dense, decoder if p else columns, targets, after)
        total = part + came[p]
        blocks = [total[:, o * sub : (o + 1) * sub] for o in range(fy)]
        got = None
        for b in reversed(bits(fy)):
            if got is not None:
                blocks = [blocks[o] + got[:, o * sub : (o + 1) * sub] for o in range(2 * b)]
            after = join(blocks[b:], 1)
            got = swap(after, dy=b)
        leaving.append(after)
        summed.append((blocks[0], got))

    places = tuple((dc, dy) for dc in range(fc) for dy in range(fy))
    *kept, ids, token = fetch(n, wide, places, decoder, indices, leaving[-1])

    sums, moved = [], []
    for p, (x, y) in enumerate(summed):
        if p == 0:
            y = hold(y, token)
            columns = [(kept[dy], swap(hold(kept[fy + dy], y), dc=1)) for dy in range(fy)]
        x = x + y
        sums.append(lax.dynamic_slice_in_dim(x, z * group, group, 0))
        moved.append(
            [
                swap(lax.dynamic_slice_in_dim(x, (z ^ j) * group, group, 0), dz=j)
                for j in z_order(fz)
            ]
        )
    errs, loss, after = [], 0.0, sums[-1]
    for p in range(chunks):
        diff = sum(in_order(moved[p], after), sums[p])
        loss = loss + jnp.sum(diff * diff, axis=1, keepdims=True)
        errs.append(diff.astype(jnp.bfloat16))
        after = errs[p]

    err = join(errs, 1)
    near = [(0, join([err] + [swap(err, dz=j) for j in z_order(fz)], 0))]
    for b in bits(fy):
        last = [(b | dy, swap(e, dy=b)) for dy, e in near]
        near += last
    pieces, near = near, near[: -len(last)]
    totals, token = grad(n, rows, near, columns, None)

    def rows_of(core):
        first = (y_at * fc + core) * own
        return [lax.dynamic_slice_in_dim(e, first, own, 0) for _, e in pieces]

    other = swap(hold(join(rows_of(1 - core_at), 0), token), dc=1)
    last[-1] = (last[-1][0], hold(last[-1][1], other))
    back = grad(n, rows, last, columns, totals, (ids, loss))
    own_places = tuple((dc, dy) for dc in range(fc) for dy, _ in pieces)
    error = own_rows(
        n, own_places, width, rows_of(core_at) + [other[i * own : (i + 1) * own] for i in range(fy)]
    )

    back = jnp.sum(lax.all_to_all(back, "lat", 0, 0, tiled=True), axis=0)
    return error, back[:, k_count] / width, back[:, :k_count]


def solution(mesh):
    in_specs = (P("groups", None), P("groups", None), P("lat", None), P(("groups", "lat"), None))
    out_specs = (P(("groups", "lat"), None), P(("groups", "lat")), P(("groups", "lat"), None))
    return jax.shard_map(local, mesh=mesh, in_specs=in_specs, out_specs=out_specs, check_vma=False)
```

```python
import functools

import jax
import jax.numpy as jnp
from jax import lax
from jax.experimental import pallas as pl
from jax.experimental.pallas import tpu as pltpu
from jax.sharding import PartitionSpec as P

CHUNKS = 2
ROW_STEP = 16
LANES = 128
SUBLANES = 8
LOADS = 4
VMEM = pl.BlockSpec(memory_space=pltpu.VMEM)
HBM = pl.BlockSpec(memory_space=pltpu.HBM)


def factors(n):
    assert n > 1 and n & (n - 1) == 0
    c = 2
    m = n // c
    y = 1
    while 4 * y * y <= m:
        y *= 2
    return m // y, y, c


def place(n, index):
    _, y, c = factors(n)
    return index // (y * c), (index // c) % y, index % c


def bits(size):
    return [1 << i for i in range(size.bit_length() - 1)]


def z_order(fz):
    return ([fz - 1] if fz > 1 else []) + list(range(1, fz - 1))


def pairs(n, dz, dy, dc):
    _, fy, fc = factors(n)
    out = []
    for i in range(n):
        z, y, c = place(n, i)
        out.append((i, ((z ^ dz) * fy + (y ^ dy)) * fc + (c ^ dc)))
    return out


def cost(flops, size):
    return pl.CostEstimate(flops=flops, bytes_accessed=size, transcendentals=0)


def params():
    return pltpu.CompilerParams(vmem_limit_bytes=24 * 1024 * 1024)


def in_hbm(x):
    return pltpu.with_memory_space_constraint(x, pltpu.HBM)


def in_vmem(x):
    return pltpu.with_memory_space_constraint(x, pltpu.VMEM)


def column(n, chunk, chunks, sub, dy, dc):
    _, fy, fc = factors(n)
    _, y, c = place(n, lax.axis_index("lat"))
    return pl.multiple_of((((c ^ dc) * fy + (y ^ dy)) * chunks + chunk) * sub, sub)


def hold(x, *after):
    def kernel(x_ref, *refs):
        refs[-1][...] = x_ref[...]

    return pl.pallas_call(
        kernel,
        out_shape=jax.ShapeDtypeStruct(x.shape, x.dtype),
        in_specs=[VMEM] * (1 + len(after)),
        out_specs=VMEM,
        input_output_aliases={0: 0},
        compiler_params=params(),
        name="hold",
    )(*[in_vmem(a) for a in (x, *after)])


def loads_of(decoder_hbm, col, buf, sem):
    count = sem.shape[0]
    step = buf.shape[0] // count
    return [
        pltpu.make_async_copy(
            decoder_hbm.at[pl.ds(i * step, step), pl.ds(col, buf.shape[1])],
            buf.at[pl.ds(i * step, step)],
            sem.at[i],
        )
        for i in range(count)
    ]


def decode_kernel(n, own, chunks, parts, first, *refs):
    fz, fy, fc = factors(n)
    me = lax.axis_index("lat")
    refs = list(refs)
    if first:
        ids_hbm, codes_hbm = refs.pop(0), refs.pop(0)
    else:
        dense_ref = refs.pop(0)
    decoder_hbm, targets_hbm = refs.pop(0), refs.pop(0)
    if len(refs) > 4 + len(parts) and not first:
        refs.pop(0)
    outs = [refs.pop(0) for _ in parts]
    if first:
        dense_ref = refs.pop(0)
    buf, sem, targets_ref, small = refs[:4]
    smalls_in = [(targets_hbm, targets_ref)]
    if first:
        ids_ref, codes_ref = refs[4:]
        smalls_in = [(ids_hbm, ids_ref), (codes_hbm, codes_ref)] + smalls_in
    smalls = [pltpu.make_async_copy(a, b, small.at[i]) for i, (a, b) in enumerate(smalls_in)]
    for copy in smalls:
        copy.start()
    rows, lat_dev = dense_ref.shape
    sub = outs[0].shape[1] // fy
    cols = [column(n, p, chunks, sub, o, dc) for p, dc in parts for o in range(fy)]
    loads = [loads_of(decoder_hbm, col, buf.at[i], sem.at[i]) for i, col in enumerate(cols)]
    for copies in loads:
        for copy in copies:
            copy.start()
    for copy in smalls:
        copy.wait()
    if first:
        k_count = ids_ref.shape[1]
        assert lat_dev <= 512
        half = lat_dev // 2
        lanes = (lax.broadcasted_iota(jnp.int32, (ROW_STEP, lat_dev), 1) - half).astype(jnp.bfloat16)

        def body(g, carry):
            at = pl.ds(pl.multiple_of(g * ROW_STEP, ROW_STEP), ROW_STEP)
            ids = ids_ref[at, :] - (me * lat_dev + half)
            ids = jnp.where((ids >= -half) & (ids < half), ids, half + 44).astype(jnp.bfloat16)
            codes = codes_ref[at, :]
            acc = jnp.zeros((ROW_STEP, lat_dev), jnp.bfloat16)
            for k in range(k_count):
                acc = jnp.where(ids[:, k : k + 1] == lanes, codes[:, k : k + 1], acc)
            dense_ref[at, :] = acc
            return carry

        lax.fori_loop(0, rows // ROW_STEP, body, 0)
    per = SUBLANES // own
    tile = pl.ds(pl.multiple_of(me // per * SUBLANES, SUBLANES), SUBLANES)
    mine = lax.broadcasted_iota(jnp.int32, (SUBLANES, sub), 0) // own == me % per
    for i, col in enumerate(cols):
        for copy in loads[i]:
            copy.wait()
        out_ref = outs[i // fy]
        here = slice(i % fy * sub, (i % fy + 1) * sub)
        out_ref[:, here] = jnp.dot(dense_ref[...], buf[i], preferred_element_type=jnp.float32)
        target = targets_ref[:, pl.ds(col, sub)].astype(jnp.float32)
        target = jnp.concatenate([target] * per, axis=0)
        out_ref[tile, here] -= jnp.where(mine, target, 0.0)


def decode(n, chunks, sub, parts, decoder, targets, start=None, dense=None, after=None):
    _, fy, _ = factors(n)
    first = start is not None
    rows = start[0].shape[0] if first else dense.shape[0]
    lat_dev = decoder.shape[0]
    out = [pltpu.VMEM((rows, fy * sub), jnp.float32)] * len(parts)
    count = len(parts) * fy
    scratch = [
        pltpu.VMEM((count, lat_dev, sub), jnp.bfloat16),
        pltpu.SemaphoreType.DMA((count, 1)),
        pltpu.VMEM(targets.shape, targets.dtype),
        pltpu.SemaphoreType.DMA((3,)),
    ]
    if first:
        args = [in_hbm(x) for x in (*start, decoder, targets)]
        specs = [HBM] * 4
        out.append(pltpu.VMEM((rows, lat_dev), jnp.bfloat16))
        scratch += [pltpu.VMEM(x.shape, x.dtype) for x in start]
    else:
        args, specs = [dense, in_hbm(decoder), in_hbm(targets)], [VMEM, HBM, HBM]
        if after is not None:
            args.append(in_vmem(after))
            specs.append(VMEM)
    return pl.pallas_call(
        functools.partial(decode_kernel, n, rows // n, chunks, parts, first),
        out_shape=out,
        in_specs=specs,
        out_specs=[VMEM] * len(out),
        scratch_shapes=scratch,
        compiler_params=params(),
        cost_estimate=cost(2 * rows * lat_dev * count * sub, 4 * lat_dev * count * sub),
        name="decode",
    )(*args)


def fetch_kernel(n, places, decoder_hbm, ids_hbm, _, *refs):
    outs = refs[: len(places)]
    ids_ref, token_ref, sem, ids_sem = refs[len(places) :]
    copies = [pltpu.make_async_copy(ids_hbm, ids_ref, ids_sem)]
    for i, (dc, dy) in enumerate(places):
        col = column(n, 0, 1, outs[i].shape[1], dy, dc)
        copies += loads_of(decoder_hbm, col, outs[i], sem.at[i])
    for copy in copies:
        copy.start()
    token_ref[...] = jnp.zeros_like(token_ref)
    for copy in copies:
        copy.wait()


def fetch(n, width, places, decoder, ids, after):
    block = pltpu.VMEM((decoder.shape[0], width), decoder.dtype)
    return pl.pallas_call(
        functools.partial(fetch_kernel, n, places),
        out_shape=[block] * len(places)
        + [pltpu.VMEM(ids.shape, ids.dtype), pltpu.VMEM((SUBLANES, LANES), jnp.float32)],
        in_specs=[HBM, HBM, VMEM],
        out_specs=[VMEM] * (2 + len(places)),
        scratch_shapes=[pltpu.SemaphoreType.DMA((len(places), LOADS)), pltpu.SemaphoreType.DMA],
        compiler_params=params(),
        cost_estimate=cost(0, decoder.shape[0] * len(places) * width * 2),
        name="fetch",
    )(in_hbm(decoder), in_hbm(ids), in_vmem(after))


def grad_kernel(n, counts, with_prev, final, *refs):
    refs = list(refs)
    errs = [[refs.pop(0) for _ in range(count)] for count in counts]
    columns = [refs.pop(0) for _ in counts]
    total = refs.pop(0)[...] if with_prev else None
    for parts, columns_ref in zip(errs, columns):
        err = parts[0][...] if len(parts) == 1 else jnp.concatenate([e[...] for e in parts], axis=0)
        part = lax.dot_general(
            err,
            columns_ref[...],
            (((1,), (1,)), ((), ())),
            preferred_element_type=jnp.float32,
        )
        total = part if total is None else total + part
    if not final:
        refs[0][...] = total
        return
    ids_ref, loss_ref, out_ref, totals_ref = refs
    totals_ref[...] = total
    rows, k_count = ids_ref.shape
    lat_dev = total.shape[1]
    own = out_ref.shape[1]
    fz, _, _ = factors(n)
    me = lax.axis_index("lat")
    z, _, _ = place(n, me)
    group = rows // fz
    places = lax.broadcasted_iota(jnp.int32, (ROW_STEP, LANES), 1)
    pad = jnp.zeros((ROW_STEP, LANES - k_count), jnp.int32)
    for q, j in enumerate([0] + z_order(fz)):
        for s in range(0, group, ROW_STEP):
            first = (z ^ j) * group + s
            rows_at = pl.ds(pl.multiple_of(first, ROW_STEP), ROW_STEP)
            ids = jnp.concatenate([ids_ref[rows_at, :] - me * lat_dev, pad], axis=1)
            held = jnp.where(places < k_count, ids // LANES, -1)
            inside = ids % LANES
            acc = jnp.zeros((ROW_STEP, LANES), jnp.float32)
            if q == 0:
                acc = jnp.where(places == k_count, loss_ref[s : s + ROW_STEP, :], acc)
            here = slice(q * group + s, q * group + s + ROW_STEP)
            for t in range(lat_dev // LANES):
                values = totals_ref[here, t * LANES : (t + 1) * LANES]
                found = jnp.take_along_axis(values, inside, axis=1, mode="promise_in_bounds")
                acc = jnp.where(held == t, found, acc)
            for d in range(ROW_STEP // own):
                out_ref[first // own + d] = acc[d * own : (d + 1) * own, :]


def grad(n, rows, pieces, columns, prev, final=None):
    lat_dev, wide = columns[pieces[0][0]].shape
    counts = tuple(len(e) for _, e in pieces)
    args = [x for _, e in pieces for x in e] + [in_vmem(columns[at]) for at, _ in pieces]
    if prev is not None:
        args.append(in_vmem(prev))
    if final is not None:
        args += list(final)
    totals = pltpu.VMEM((rows, lat_dev), jnp.float32)
    size = wide * len(pieces)
    return pl.pallas_call(
        functools.partial(grad_kernel, n, counts, prev is not None, final is not None),
        out_shape=totals if final is None else jax.ShapeDtypeStruct((n, rows // n, LANES), jnp.float32),
        in_specs=[VMEM] * len(args),
        out_specs=VMEM,
        scratch_shapes=[] if final is None else [totals],
        compiler_params=params(),
        cost_estimate=cost(2 * rows * lat_dev * size, 4 * lat_dev * size),
        name="grad",
    )(*args)


def own_kernel(n, blocks, own, *refs):
    errs, out_ref = refs[:-1], refs[-1]
    _, fy, fc = factors(n)
    _, y, c = place(n, lax.axis_index("lat"))
    group, sub = errs[0].shape
    row = lax.broadcasted_iota(jnp.int32, (own, group), 0) + (y * fc + c) * own
    want = lax.broadcasted_iota(jnp.int32, (own, group), 1)
    mine = jnp.where(row == want, 1.0, 0.0).astype(jnp.bfloat16)
    for err, (dc, dy) in zip(errs, blocks):
        rows = jnp.dot(mine, err[...], preferred_element_type=jnp.float32)
        out_ref[:, pl.ds(column(n, 0, 1, sub, dy, dc), sub)] = rows.astype(jnp.bfloat16)


def own_rows(n, blocks, own, width, errs):
    return pl.pallas_call(
        functools.partial(own_kernel, n, tuple(blocks), own),
        out_shape=jax.ShapeDtypeStruct((own, width), jnp.bfloat16),
        in_specs=[VMEM] * len(errs),
        out_specs=VMEM,
        compiler_params=params(),
        name="own_rows",
    )(*errs)


def local(codes, indices, decoder, targets):
    width = decoder.shape[1]
    rows, k_count = codes.shape
    n = lax.axis_size("lat")
    own = rows // n
    fz, fy, fc = factors(n)
    group = rows // fz
    chunks = CHUNKS
    sub = width // (fc * fy * chunks)
    z, _, _ = place(n, lax.axis_index("lat"))

    def swap(x, dz=0, dy=0, dc=0):
        return lax.ppermute(x, "lat", pairs(n, dz, dy, dc))

    def join(xs, axis):
        return xs[0] if len(xs) == 1 else jnp.concatenate(xs, axis=axis)

    def in_order(xs, after=None):
        for i, x in enumerate(xs):
            if after is not None:
                xs[i] = hold(x, after)
            after = xs[i]
        return xs

    others = tuple((p, 1) for p in range(chunks))
    *parts, dense = decode(n, chunks, sub, others, decoder, targets, (indices, codes))
    came = [swap(part, dc=1) for part in parts]
    summed, leaving, after = [], [], None
    for p in range(chunks):
        (part,) = decode(n, chunks, sub, ((p, 0),), decoder, targets, dense=dense, after=after)
        total = part + came[p]
        blocks = [total[:, o * sub : (o + 1) * sub] for o in range(fy)]
        got = None
        for b in reversed(bits(fy)):
            if got is not None:
                blocks = [blocks[o] + got[:, o * sub : (o + 1) * sub] for o in range(2 * b)]
            after = join(blocks[b:], 1)
            got = swap(after, dy=b)
        leaving.append(after)
        summed.append((blocks[0], got))

    places = tuple((dc, dy) for dy in range(fy) for dc in range(fc))
    *columns, ids, token = fetch(n, chunks * sub, places, decoder, indices, leaving[-1])
    columns = dict(zip(places, columns))
    sums, moved = [], []
    for p, (x, y) in enumerate(summed):
        x = x + (hold(y, token) if p == 0 else y)
        sums.append(lax.dynamic_slice_in_dim(x, z * group, group, 0))
        moved.append(
            [
                swap(lax.dynamic_slice_in_dim(x, (z ^ j) * group, group, 0), dz=j)
                for j in z_order(fz)
            ]
        )
    errs, loss, after = [], 0.0, sums[-1]
    for p in range(chunks):
        diff = sum(in_order(moved[p], after), sums[p])
        loss = loss + jnp.sum(diff * diff, axis=1, keepdims=True)
        errs.append(diff.astype(jnp.bfloat16))
        after = errs[p]

    err = join(errs, 1)
    near = [((0, 0), [join([err] + [swap(err, dz=j) for j in z_order(fz)], 0)])]
    for b in bits(fy):
        last = [((0, b | at[1]), [swap(e, dy=b) for e in parts]) for at, parts in near]
        near += last
    near = near[: -len(last)]
    half = rows // 2

    def halves(parts):
        whole = join(parts, 0)
        return [whole[:group], whole[group : group + half], whole[group + half :]]

    far = [((1, at[1]), [swap(e, dc=1) for e in halves(parts)]) for at, parts in near]
    totals = grad(n, rows, near, columns, None)
    totals = grad(n, rows, far, columns, totals)
    last[-1][1][-1] = hold(last[-1][1][-1], totals)
    far_last = [((1, at[1]), [swap(join(parts, 0), dc=1)]) for at, parts in last]
    totals = grad(n, rows, last, columns, totals)
    back = grad(n, rows, far_last, columns, totals, (in_vmem(ids), loss))
    pieces = near + far + last + far_last
    error = own_rows(n, [at for at, _ in pieces], own, width, [e[0][:group] for _, e in pieces])

    back = jnp.sum(lax.all_to_all(back, "lat", 0, 0, tiled=True), axis=0)
    return error, back[:, k_count] / width, back[:, :k_count]


def solution(mesh):
    in_specs = (P("groups", None), P("groups", None), P("lat", None), P(("groups", "lat"), None))
    out_specs = (P(("groups", "lat"), None), P(("groups", "lat")), P(("groups", "lat"), None))
    return jax.shard_map(local, mesh=mesh, in_specs=in_specs, out_specs=out_specs, check_vma=False)
```

```python
import functools

import jax
import jax.numpy as jnp
from jax import lax
from jax.experimental import pallas as pl
from jax.experimental.pallas import tpu as pltpu
from jax.sharding import PartitionSpec as P

CHUNKS = 2
ROW_STEP = 16
LANES = 128
SUBLANES = 8
LOADS = 4
VMEM = pl.BlockSpec(memory_space=pltpu.VMEM)
HBM = pl.BlockSpec(memory_space=pltpu.HBM)


def factors(n):
    assert n > 1 and n & (n - 1) == 0
    c = 2
    m = n // c
    y = 1
    while 4 * y * y <= m:
        y *= 2
    return m // y, y, c


def place(n, index):
    _, y, c = factors(n)
    return index // (y * c), (index // c) % y, index % c


def bits(size):
    return [1 << i for i in range(size.bit_length() - 1)]


def z_order(fz):
    return ([fz - 1] if fz > 1 else []) + list(range(1, fz - 1))


def pairs(n, dz, dy, dc):
    _, fy, fc = factors(n)
    out = []
    for i in range(n):
        z, y, c = place(n, i)
        out.append((i, ((z ^ dz) * fy + (y ^ dy)) * fc + (c ^ dc)))
    return out


def cost(flops, size):
    return pl.CostEstimate(flops=flops, bytes_accessed=size, transcendentals=0)


def params():
    return pltpu.CompilerParams(vmem_limit_bytes=24 * 1024 * 1024)


def in_hbm(x):
    return pltpu.with_memory_space_constraint(x, pltpu.HBM)


def in_vmem(x):
    return pltpu.with_memory_space_constraint(x, pltpu.VMEM)


def column(n, chunk, chunks, sub, dy, dc):
    _, fy, fc = factors(n)
    _, y, c = place(n, lax.axis_index("lat"))
    return pl.multiple_of((((c ^ dc) * fy + (y ^ dy)) * chunks + chunk) * sub, sub)


def hold(x, *after):
    def kernel(x_ref, *refs):
        refs[-1][...] = x_ref[...]

    return pl.pallas_call(
        kernel,
        out_shape=jax.ShapeDtypeStruct(x.shape, x.dtype),
        in_specs=[VMEM] * (1 + len(after)),
        out_specs=VMEM,
        input_output_aliases={0: 0},
        compiler_params=params(),
        name="hold",
    )(*[in_vmem(a) for a in (x, *after)])


def loads_of(decoder_hbm, col, buf, sem):
    count = sem.shape[0]
    step = buf.shape[0] // count
    return [
        pltpu.make_async_copy(
            decoder_hbm.at[pl.ds(i * step, step), pl.ds(col, buf.shape[1])],
            buf.at[pl.ds(i * step, step)],
            sem.at[i],
        )
        for i in range(count)
    ]


def decode_kernel(n, own, chunks, parts, first, *refs):
    fz, fy, fc = factors(n)
    me = lax.axis_index("lat")
    refs = list(refs)
    if first:
        ids_hbm, codes_hbm = refs.pop(0), refs.pop(0)
    else:
        dense_ref = refs.pop(0)
    decoder_hbm, targets_hbm = refs.pop(0), refs.pop(0)
    if len(refs) > 4 + len(parts) and not first:
        refs.pop(0)
    outs = [refs.pop(0) for _ in parts]
    if first:
        dense_ref = refs.pop(0)
    buf, sem, targets_ref, small = refs[:4]
    smalls_in = [(targets_hbm, targets_ref)]
    if first:
        ids_ref, codes_ref = refs[4:]
        smalls_in = [(ids_hbm, ids_ref), (codes_hbm, codes_ref)] + smalls_in
    smalls = [pltpu.make_async_copy(a, b, small.at[i]) for i, (a, b) in enumerate(smalls_in)]
    for copy in smalls:
        copy.start()
    rows, lat_dev = dense_ref.shape
    sub = outs[0].shape[1] // fy
    cols = [column(n, p, chunks, sub, o, dc) for p, dc in parts for o in range(fy)]
    loads = [loads_of(decoder_hbm, col, buf.at[i], sem.at[i]) for i, col in enumerate(cols)]
    for copies in loads:
        for copy in copies:
            copy.start()
    for copy in smalls:
        copy.wait()
    if first:
        k_count = ids_ref.shape[1]
        assert lat_dev <= 512
        half = lat_dev // 2
        lanes = (lax.broadcasted_iota(jnp.int32, (ROW_STEP, lat_dev), 1) - half).astype(jnp.bfloat16)

        def body(g, carry):
            at = pl.ds(pl.multiple_of(g * ROW_STEP, ROW_STEP), ROW_STEP)
            ids = ids_ref[at, :] - (me * lat_dev + half)
            ids = jnp.where((ids >= -half) & (ids < half), ids, half + 44).astype(jnp.bfloat16)
            codes = codes_ref[at, :]
            acc = jnp.zeros((ROW_STEP, lat_dev), jnp.bfloat16)
            for k in range(k_count):
                acc = jnp.where(ids[:, k : k + 1] == lanes, codes[:, k : k + 1], acc)
            dense_ref[at, :] = acc
            return carry

        lax.fori_loop(0, rows // ROW_STEP, body, 0)
    per = SUBLANES // own
    tile = pl.ds(pl.multiple_of(me // per * SUBLANES, SUBLANES), SUBLANES)
    mine = lax.broadcasted_iota(jnp.int32, (SUBLANES, sub), 0) // own == me % per
    for i, col in enumerate(cols):
        for copy in loads[i]:
            copy.wait()
        out_ref = outs[i // fy]
        here = slice(i % fy * sub, (i % fy + 1) * sub)
        out_ref[:, here] = jnp.dot(dense_ref[...], buf[i], preferred_element_type=jnp.float32)
        target = targets_ref[:, pl.ds(col, sub)].astype(jnp.float32)
        target = jnp.concatenate([target] * per, axis=0)
        out_ref[tile, here] -= jnp.where(mine, target, 0.0)


def decode(n, chunks, sub, parts, decoder, targets, start=None, dense=None, after=None):
    _, fy, _ = factors(n)
    first = start is not None
    rows = start[0].shape[0] if first else dense.shape[0]
    lat_dev = decoder.shape[0]
    out = [pltpu.VMEM((rows, fy * sub), jnp.float32)] * len(parts)
    count = len(parts) * fy
    scratch = [
        pltpu.VMEM((count, lat_dev, sub), jnp.bfloat16),
        pltpu.SemaphoreType.DMA((count, 1)),
        pltpu.VMEM(targets.shape, targets.dtype),
        pltpu.SemaphoreType.DMA((3,)),
    ]
    if first:
        args = [in_hbm(x) for x in (*start, decoder, targets)]
        specs = [HBM] * 4
        out.append(pltpu.VMEM((rows, lat_dev), jnp.bfloat16))
        scratch += [pltpu.VMEM(x.shape, x.dtype) for x in start]
    else:
        args, specs = [dense, in_hbm(decoder), in_hbm(targets)], [VMEM, HBM, HBM]
        if after is not None:
            args.append(in_vmem(after))
            specs.append(VMEM)
    return pl.pallas_call(
        functools.partial(decode_kernel, n, rows // n, chunks, parts, first),
        out_shape=out,
        in_specs=specs,
        out_specs=[VMEM] * len(out),
        scratch_shapes=scratch,
        compiler_params=params(),
        cost_estimate=cost(2 * rows * lat_dev * count * sub, 4 * lat_dev * count * sub),
        name="decode",
    )(*args)


def fetch_kernel(n, places, decoder_hbm, ids_hbm, _, *refs):
    outs = refs[: len(places)]
    ids_ref, token_ref, sem, ids_sem = refs[len(places) :]
    copies = [pltpu.make_async_copy(ids_hbm, ids_ref, ids_sem)]
    for i, (dc, dy) in enumerate(places):
        col = column(n, 0, 1, outs[i].shape[1], dy, dc)
        copies += loads_of(decoder_hbm, col, outs[i], sem.at[i])
    for copy in copies:
        copy.start()
    token_ref[...] = jnp.zeros_like(token_ref)
    for copy in copies:
        copy.wait()


def fetch(n, width, places, decoder, ids, after):
    block = pltpu.VMEM((decoder.shape[0], width), decoder.dtype)
    return pl.pallas_call(
        functools.partial(fetch_kernel, n, places),
        out_shape=[block] * len(places)
        + [pltpu.VMEM(ids.shape, ids.dtype), pltpu.VMEM((SUBLANES, LANES), jnp.float32)],
        in_specs=[HBM, HBM, VMEM],
        out_specs=[VMEM] * (2 + len(places)),
        scratch_shapes=[pltpu.SemaphoreType.DMA((len(places), LOADS)), pltpu.SemaphoreType.DMA],
        compiler_params=params(),
        cost_estimate=cost(0, decoder.shape[0] * len(places) * width * 2),
        name="fetch",
    )(in_hbm(decoder), in_hbm(ids), in_vmem(after))


def grad_kernel(n, counts, with_prev, final, *refs):
    refs = list(refs)
    errs = [[refs.pop(0) for _ in range(count)] for count in counts]
    columns = [refs.pop(0) for _ in counts]
    total = refs.pop(0)[...] if with_prev else None
    for parts, columns_ref in zip(errs, columns):
        err = parts[0][...] if len(parts) == 1 else jnp.concatenate([e[...] for e in parts], axis=0)
        part = lax.dot_general(
            err,
            columns_ref[...],
            (((1,), (1,)), ((), ())),
            preferred_element_type=jnp.float32,
        )
        total = part if total is None else total + part
    if not final:
        refs[0][...] = total
        return
    ids_ref, loss_ref, out_ref, totals_ref = refs
    totals_ref[...] = total
    rows, k_count = ids_ref.shape
    lat_dev = total.shape[1]
    own = out_ref.shape[1]
    fz, _, _ = factors(n)
    me = lax.axis_index("lat")
    z, _, _ = place(n, me)
    group = rows // fz
    places = lax.broadcasted_iota(jnp.int32, (ROW_STEP, LANES), 1)
    pad = jnp.zeros((ROW_STEP, LANES - k_count), jnp.int32)
    for q, j in enumerate([0] + z_order(fz)):
        for s in range(0, group, ROW_STEP):
            first = (z ^ j) * group + s
            rows_at = pl.ds(pl.multiple_of(first, ROW_STEP), ROW_STEP)
            ids = jnp.concatenate([ids_ref[rows_at, :] - me * lat_dev, pad], axis=1)
            held = jnp.where(places < k_count, ids // LANES, -1)
            inside = ids % LANES
            acc = jnp.zeros((ROW_STEP, LANES), jnp.float32)
            if q == 0:
                acc = jnp.where(places == k_count, loss_ref[s : s + ROW_STEP, :], acc)
            here = slice(q * group + s, q * group + s + ROW_STEP)
            for t in range(lat_dev // LANES):
                values = totals_ref[here, t * LANES : (t + 1) * LANES]
                found = jnp.take_along_axis(values, inside, axis=1, mode="promise_in_bounds")
                acc = jnp.where(held == t, found, acc)
            for d in range(ROW_STEP // own):
                out_ref[first // own + d] = acc[d * own : (d + 1) * own, :]


def grad(n, rows, pieces, columns, prev, final=None):
    lat_dev, wide = columns[pieces[0][0]].shape
    counts = tuple(len(e) for _, e in pieces)
    args = [x for _, e in pieces for x in e] + [in_vmem(columns[at]) for at, _ in pieces]
    if prev is not None:
        args.append(in_vmem(prev))
    if final is not None:
        args += list(final)
    totals = pltpu.VMEM((rows, lat_dev), jnp.float32)
    size = wide * len(pieces)
    return pl.pallas_call(
        functools.partial(grad_kernel, n, counts, prev is not None, final is not None),
        out_shape=totals if final is None else pltpu.VMEM((n, rows // n, LANES), jnp.float32),
        in_specs=[VMEM] * len(args),
        out_specs=VMEM,
        scratch_shapes=[] if final is None else [totals],
        compiler_params=params(),
        cost_estimate=cost(2 * rows * lat_dev * size, 4 * lat_dev * size),
        name="grad",
    )(*args)


def own_kernel(n, blocks, own, *refs):
    errs, out_ref = refs[:-1], refs[-1]
    _, fy, fc = factors(n)
    _, y, c = place(n, lax.axis_index("lat"))
    group, sub = errs[0].shape
    row = lax.broadcasted_iota(jnp.int32, (own, group), 0) + (y * fc + c) * own
    want = lax.broadcasted_iota(jnp.int32, (own, group), 1)
    mine = jnp.where(row == want, 1.0, 0.0).astype(jnp.bfloat16)
    for err, (dc, dy) in zip(errs, blocks):
        rows = jnp.dot(mine, err[...], preferred_element_type=jnp.float32)
        out_ref[:, pl.ds(column(n, 0, 1, sub, dy, dc), sub)] = rows.astype(jnp.bfloat16)


def own_rows(n, blocks, own, width, errs):
    return pl.pallas_call(
        functools.partial(own_kernel, n, tuple(blocks), own),
        out_shape=jax.ShapeDtypeStruct((own, width), jnp.bfloat16),
        in_specs=[VMEM] * len(errs),
        out_specs=VMEM,
        compiler_params=params(),
        name="own_rows",
    )(*errs)


def local(codes, indices, decoder, targets):
    width = decoder.shape[1]
    rows, k_count = codes.shape
    n = lax.axis_size("lat")
    own = rows // n
    fz, fy, fc = factors(n)
    group = rows // fz
    chunks = CHUNKS
    sub = width // (fc * fy * chunks)
    z, _, _ = place(n, lax.axis_index("lat"))

    def swap(x, dz=0, dy=0, dc=0):
        return lax.ppermute(x, "lat", pairs(n, dz, dy, dc))

    def join(xs, axis):
        return xs[0] if len(xs) == 1 else jnp.concatenate(xs, axis=axis)

    def in_order(xs, after=None):
        for i, x in enumerate(xs):
            if after is not None:
                xs[i] = hold(x, after)
            after = xs[i]
        return xs

    others = tuple((p, 1) for p in range(chunks))
    *parts, dense = decode(n, chunks, sub, others, decoder, targets, (indices, codes))
    came = [swap(part, dc=1) for part in parts]
    summed, leaving, after = [], [], None
    for p in range(chunks):
        (part,) = decode(n, chunks, sub, ((p, 0),), decoder, targets, dense=dense, after=after)
        total = part + came[p]
        blocks = [total[:, o * sub : (o + 1) * sub] for o in range(fy)]
        got = None
        for b in reversed(bits(fy)):
            if got is not None:
                blocks = [blocks[o] + got[:, o * sub : (o + 1) * sub] for o in range(2 * b)]
            after = join(blocks[b:], 1)
            got = swap(after, dy=b)
        leaving.append(after)
        summed.append((blocks[0], got))

    places = tuple((dc, dy) for dy in range(fy) for dc in range(fc))
    *columns, ids, token = fetch(n, chunks * sub, places, decoder, indices, leaving[-1])
    columns = dict(zip(places, columns))
    sums, moved = [], []
    for p, (x, y) in enumerate(summed):
        x = x + (hold(y, token) if p == 0 else y)
        sums.append(lax.dynamic_slice_in_dim(x, z * group, group, 0))
        moved.append(
            [
                swap(lax.dynamic_slice_in_dim(x, (z ^ j) * group, group, 0), dz=j)
                for j in z_order(fz)
            ]
        )
    errs, loss, after = [], 0.0, sums[-1]
    for p in range(chunks):
        diff = sum(in_order(moved[p], after), sums[p])
        loss = loss + jnp.sum(diff * diff, axis=1, keepdims=True)
        errs.append(diff.astype(jnp.bfloat16))
        after = errs[p]

    err = join(errs, 1)
    come = [swap(err, dz=j) for j in z_order(fz)]
    near = [((0, 0), [join([err] + come[:-1], 0), come[-1]])]
    for b in bits(fy):
        last = [((0, b | at[1]), in_order([swap(e, dy=b) for e in parts])) for at, parts in near]
        near += last
    near = near[: -len(last)]
    half = rows // 2

    def halves(parts):
        whole = join(parts, 0)
        return [whole[:group], whole[group : group + half], whole[group + half :]]

    far = [((1, at[1]), [swap(e, dc=1) for e in halves(parts)]) for at, parts in near]
    totals = grad(n, rows, near, columns, None)
    totals = grad(n, rows, far, columns, totals)
    last[-1][1][-1] = hold(last[-1][1][-1], totals)
    far_last = [((1, at[1]), [swap(join(parts, 0), dc=1)]) for at, parts in last]
    totals = grad(n, rows, last, columns, totals)
    back = grad(n, rows, far_last, columns, totals, (in_vmem(ids), loss))
    pieces = near + far + last + far_last
    error = own_rows(n, [at for at, _ in pieces], own, width, [e[0][:group] for _, e in pieces])

    back = jnp.sum(lax.all_to_all(back, "lat", 0, 0, tiled=True), axis=0)
    return error, back[:, k_count] / width, back[:, :k_count]


def solution(mesh):
    in_specs = (P("groups", None), P("groups", None), P("lat", None), P(("groups", "lat"), None))
    out_specs = (P(("groups", "lat"), None), P(("groups", "lat")), P(("groups", "lat"), None))
    return jax.shard_map(local, mesh=mesh, in_specs=in_specs, out_specs=out_specs, check_vma=False)
```

```python
import functools

import jax
import jax.numpy as jnp
from jax import lax
from jax.experimental import pallas as pl
from jax.experimental.pallas import tpu as pltpu
from jax.sharding import PartitionSpec as P

CHUNKS = 2
ROW_STEP = 16
LANES = 128
SUBLANES = 8
LOADS = 4
VMEM = pl.BlockSpec(memory_space=pltpu.VMEM)
HBM = pl.BlockSpec(memory_space=pltpu.HBM)


def factors(n):
    assert n > 1 and n & (n - 1) == 0
    c = 2
    m = n // c
    y = 1
    while 4 * y * y <= m:
        y *= 2
    return m // y, y, c


def place(n, index):
    _, y, c = factors(n)
    return index // (y * c), (index // c) % y, index % c


def bits(size):
    return [1 << i for i in range(size.bit_length() - 1)]


def z_order(fz):
    return ([fz - 1] if fz > 1 else []) + list(range(1, fz - 1))


def pairs(n, dz, dy, dc):
    _, fy, fc = factors(n)
    out = []
    for i in range(n):
        z, y, c = place(n, i)
        out.append((i, ((z ^ dz) * fy + (y ^ dy)) * fc + (c ^ dc)))
    return out


def cost(flops, size):
    return pl.CostEstimate(flops=flops, bytes_accessed=size, transcendentals=0)


def params():
    return pltpu.CompilerParams(vmem_limit_bytes=24 * 1024 * 1024)


def in_hbm(x):
    return pltpu.with_memory_space_constraint(x, pltpu.HBM)


def in_vmem(x):
    return pltpu.with_memory_space_constraint(x, pltpu.VMEM)


def column(n, chunk, chunks, sub, dy, dc):
    _, fy, fc = factors(n)
    _, y, c = place(n, lax.axis_index("lat"))
    return pl.multiple_of((((c ^ dc) * fy + (y ^ dy)) * chunks + chunk) * sub, sub)


def hold(x, *after):
    def kernel(x_ref, *refs):
        refs[-1][...] = x_ref[...]

    return pl.pallas_call(
        kernel,
        out_shape=jax.ShapeDtypeStruct(x.shape, x.dtype),
        in_specs=[VMEM] * (1 + len(after)),
        out_specs=VMEM,
        input_output_aliases={0: 0},
        compiler_params=params(),
        name="hold",
    )(*[in_vmem(a) for a in (x, *after)])


def loads_of(decoder_hbm, col, buf, sem):
    count = sem.shape[0]
    step = buf.shape[0] // count
    return [
        pltpu.make_async_copy(
            decoder_hbm.at[pl.ds(i * step, step), pl.ds(col, buf.shape[1])],
            buf.at[pl.ds(i * step, step)],
            sem.at[i],
        )
        for i in range(count)
    ]


def decode_kernel(n, own, chunks, parts, first, *refs):
    fz, fy, fc = factors(n)
    me = lax.axis_index("lat")
    refs = list(refs)
    if first:
        ids_hbm, codes_hbm = refs.pop(0), refs.pop(0)
    else:
        dense_ref = refs.pop(0)
    decoder_hbm, targets_hbm = refs.pop(0), refs.pop(0)
    if len(refs) > 4 + len(parts) and not first:
        refs.pop(0)
    outs = [refs.pop(0) for _ in parts]
    if first:
        dense_ref = refs.pop(0)
    buf, sem, targets_ref, small = refs[:4]
    smalls_in = [(targets_hbm, targets_ref)]
    if first:
        ids_ref, codes_ref = refs[4:]
        smalls_in = [(ids_hbm, ids_ref), (codes_hbm, codes_ref)] + smalls_in
    smalls = [pltpu.make_async_copy(a, b, small.at[i]) for i, (a, b) in enumerate(smalls_in)]
    for copy in smalls:
        copy.start()
    rows, lat_dev = dense_ref.shape
    sub = outs[0].shape[1] // fy
    cols = [column(n, p, chunks, sub, o, dc) for p, dc in parts for o in range(fy)]
    loads = [loads_of(decoder_hbm, col, buf.at[i], sem.at[i]) for i, col in enumerate(cols)]
    for copies in loads:
        for copy in copies:
            copy.start()
    for copy in smalls:
        copy.wait()
    if first:
        k_count = ids_ref.shape[1]
        assert lat_dev <= 512
        half = lat_dev // 2
        lanes = (lax.broadcasted_iota(jnp.int32, (ROW_STEP, lat_dev), 1) - half).astype(jnp.bfloat16)

        def body(g, carry):
            at = pl.ds(pl.multiple_of(g * ROW_STEP, ROW_STEP), ROW_STEP)
            ids = ids_ref[at, :] - (me * lat_dev + half)
            ids = jnp.where((ids >= -half) & (ids < half), ids, half + 44).astype(jnp.bfloat16)
            codes = codes_ref[at, :]
            acc = jnp.zeros((ROW_STEP, lat_dev), jnp.bfloat16)
            for k in range(k_count):
                acc = jnp.where(ids[:, k : k + 1] == lanes, codes[:, k : k + 1], acc)
            dense_ref[at, :] = acc
            return carry

        lax.fori_loop(0, rows // ROW_STEP, body, 0)
    per = SUBLANES // own
    tile = pl.ds(pl.multiple_of(me // per * SUBLANES, SUBLANES), SUBLANES)
    mine = lax.broadcasted_iota(jnp.int32, (SUBLANES, sub), 0) // own == me % per
    for i, col in enumerate(cols):
        for copy in loads[i]:
            copy.wait()
        out_ref = outs[i // fy]
        here = slice(i % fy * sub, (i % fy + 1) * sub)
        out_ref[:, here] = jnp.dot(dense_ref[...], buf[i], preferred_element_type=jnp.float32)
        target = targets_ref[:, pl.ds(col, sub)].astype(jnp.float32)
        target = jnp.concatenate([target] * per, axis=0)
        out_ref[tile, here] -= jnp.where(mine, target, 0.0)


def decode(n, chunks, sub, parts, decoder, targets, start=None, dense=None, after=None):
    _, fy, _ = factors(n)
    first = start is not None
    rows = start[0].shape[0] if first else dense.shape[0]
    lat_dev = decoder.shape[0]
    out = [pltpu.VMEM((rows, fy * sub), jnp.float32)] * len(parts)
    count = len(parts) * fy
    scratch = [
        pltpu.VMEM((count, lat_dev, sub), jnp.bfloat16),
        pltpu.SemaphoreType.DMA((count, 1)),
        pltpu.VMEM(targets.shape, targets.dtype),
        pltpu.SemaphoreType.DMA((3,)),
    ]
    if first:
        args = [in_hbm(x) for x in (*start, decoder, targets)]
        specs = [HBM] * 4
        out.append(pltpu.VMEM((rows, lat_dev), jnp.bfloat16))
        scratch += [pltpu.VMEM(x.shape, x.dtype) for x in start]
    else:
        args, specs = [dense, in_hbm(decoder), in_hbm(targets)], [VMEM, HBM, HBM]
        if after is not None:
            args.append(in_vmem(after))
            specs.append(VMEM)
    return pl.pallas_call(
        functools.partial(decode_kernel, n, rows // n, chunks, parts, first),
        out_shape=out,
        in_specs=specs,
        out_specs=[VMEM] * len(out),
        scratch_shapes=scratch,
        compiler_params=params(),
        cost_estimate=cost(2 * rows * lat_dev * count * sub, 4 * lat_dev * count * sub),
        name="decode",
    )(*args)


def fetch_kernel(n, places, decoder_hbm, ids_hbm, _, *refs):
    outs = refs[: len(places)]
    ids_ref, token_ref, sem, ids_sem = refs[len(places) :]
    copies = [pltpu.make_async_copy(ids_hbm, ids_ref, ids_sem)]
    for i, (dc, dy) in enumerate(places):
        col = column(n, 0, 1, outs[i].shape[1], dy, dc)
        copies += loads_of(decoder_hbm, col, outs[i], sem.at[i])
    for copy in copies:
        copy.start()
    token_ref[...] = jnp.zeros_like(token_ref)
    for copy in copies:
        copy.wait()


def fetch(n, width, places, decoder, ids, after):
    block = pltpu.VMEM((decoder.shape[0], width), decoder.dtype)
    return pl.pallas_call(
        functools.partial(fetch_kernel, n, places),
        out_shape=[block] * len(places)
        + [pltpu.VMEM(ids.shape, ids.dtype), pltpu.VMEM((SUBLANES, LANES), jnp.float32)],
        in_specs=[HBM, HBM, VMEM],
        out_specs=[VMEM] * (2 + len(places)),
        scratch_shapes=[pltpu.SemaphoreType.DMA((len(places), LOADS)), pltpu.SemaphoreType.DMA],
        compiler_params=params(),
        cost_estimate=cost(0, decoder.shape[0] * len(places) * width * 2),
        name="fetch",
    )(in_hbm(decoder), in_hbm(ids), in_vmem(after))


def grad_kernel(n, counts, with_prev, final, *refs):
    refs = list(refs)
    errs = [[refs.pop(0) for _ in range(count)] for count in counts]
    columns = [refs.pop(0) for _ in counts]
    total = refs.pop(0)[...] if with_prev else None
    for parts, columns_ref in zip(errs, columns):
        err = parts[0][...] if len(parts) == 1 else jnp.concatenate([e[...] for e in parts], axis=0)
        part = lax.dot_general(
            err,
            columns_ref[...],
            (((1,), (1,)), ((), ())),
            preferred_element_type=jnp.float32,
        )
        total = part if total is None else total + part
    if not final:
        refs[0][...] = total
        return
    ids_ref, loss_ref, out_ref, totals_ref = refs
    totals_ref[...] = total
    rows, k_count = ids_ref.shape
    lat_dev = total.shape[1]
    own = out_ref.shape[1]
    fz, _, _ = factors(n)
    me = lax.axis_index("lat")
    z, _, _ = place(n, me)
    group = rows // fz
    places = lax.broadcasted_iota(jnp.int32, (ROW_STEP, LANES), 1)
    pad = jnp.zeros((ROW_STEP, LANES - k_count), jnp.int32)
    for q, j in enumerate([0] + z_order(fz)):
        for s in range(0, group, ROW_STEP):
            first = (z ^ j) * group + s
            rows_at = pl.ds(pl.multiple_of(first, ROW_STEP), ROW_STEP)
            ids = jnp.concatenate([ids_ref[rows_at, :] - me * lat_dev, pad], axis=1)
            held = jnp.where(places < k_count, ids // LANES, -1)
            inside = ids % LANES
            acc = jnp.zeros((ROW_STEP, LANES), jnp.float32)
            if q == 0:
                acc = jnp.where(places == k_count, loss_ref[s : s + ROW_STEP, :], acc)
            here = slice(q * group + s, q * group + s + ROW_STEP)
            for t in range(lat_dev // LANES):
                values = totals_ref[here, t * LANES : (t + 1) * LANES]
                found = jnp.take_along_axis(values, inside, axis=1, mode="promise_in_bounds")
                acc = jnp.where(held == t, found, acc)
            for d in range(ROW_STEP // own):
                out_ref[first // own + d] = acc[d * own : (d + 1) * own, :]


def grad(n, rows, pieces, columns, prev, final=None):
    lat_dev, wide = columns[pieces[0][0]].shape
    counts = tuple(len(e) for _, e in pieces)
    args = [x for _, e in pieces for x in e] + [in_vmem(columns[at]) for at, _ in pieces]
    if prev is not None:
        args.append(in_vmem(prev))
    if final is not None:
        args += list(final)
    totals = pltpu.VMEM((rows, lat_dev), jnp.float32)
    size = wide * len(pieces)
    return pl.pallas_call(
        functools.partial(grad_kernel, n, counts, prev is not None, final is not None),
        out_shape=totals if final is None else pltpu.VMEM((n, rows // n, LANES), jnp.float32),
        in_specs=[VMEM] * len(args),
        out_specs=VMEM,
        scratch_shapes=[] if final is None else [totals],
        compiler_params=params(),
        cost_estimate=cost(2 * rows * lat_dev * size, 4 * lat_dev * size),
        name="grad",
    )(*args)


def own_kernel(n, blocks, own, *refs):
    errs, out_ref = refs[:-1], refs[-1]
    _, fy, fc = factors(n)
    _, y, c = place(n, lax.axis_index("lat"))
    group, sub = errs[0].shape
    row = lax.broadcasted_iota(jnp.int32, (own, group), 0) + (y * fc + c) * own
    want = lax.broadcasted_iota(jnp.int32, (own, group), 1)
    mine = jnp.where(row == want, 1.0, 0.0).astype(jnp.bfloat16)
    for err, (dc, dy) in zip(errs, blocks):
        rows = jnp.dot(mine, err[...], preferred_element_type=jnp.float32)
        out_ref[:, pl.ds(column(n, 0, 1, sub, dy, dc), sub)] = rows.astype(jnp.bfloat16)


def own_rows(n, blocks, own, width, errs):
    return pl.pallas_call(
        functools.partial(own_kernel, n, tuple(blocks), own),
        out_shape=jax.ShapeDtypeStruct((own, width), jnp.bfloat16),
        in_specs=[VMEM] * len(errs),
        out_specs=VMEM,
        compiler_params=params(),
        name="own_rows",
    )(*errs)


def local(codes, indices, decoder, targets):
    width = decoder.shape[1]
    rows, k_count = codes.shape
    n = lax.axis_size("lat")
    own = rows // n
    fz, fy, fc = factors(n)
    group = rows // fz
    chunks = CHUNKS
    sub = width // (fc * fy * chunks)
    z, _, _ = place(n, lax.axis_index("lat"))

    def swap(x, dz=0, dy=0, dc=0):
        return lax.ppermute(x, "lat", pairs(n, dz, dy, dc))

    def join(xs, axis):
        return xs[0] if len(xs) == 1 else jnp.concatenate(xs, axis=axis)

    def in_order(xs, after=None):
        for i, x in enumerate(xs):
            if after is not None:
                xs[i] = hold(x, after)
            after = xs[i]
        return xs

    others = tuple((p, 1) for p in range(chunks))
    *parts, dense = decode(n, chunks, sub, others, decoder, targets, (indices, codes))
    came = [swap(part, dc=1) for part in parts]
    summed, leaving, after = [], [], None
    for p in range(chunks):
        (part,) = decode(n, chunks, sub, ((p, 0),), decoder, targets, dense=dense, after=after)
        total = part + came[p]
        blocks = [total[:, o * sub : (o + 1) * sub] for o in range(fy)]
        got = None
        for b in reversed(bits(fy)):
            if got is not None:
                blocks = [blocks[o] + got[:, o * sub : (o + 1) * sub] for o in range(2 * b)]
            after = join(blocks[b:], 1)
            got = swap(after, dy=b)
        leaving.append(after)
        summed.append((blocks[0], got))

    places = tuple((dc, dy) for dy in range(fy) for dc in range(fc))
    *columns, ids, token = fetch(n, chunks * sub, places, decoder, indices, leaving[-1])
    columns = dict(zip(places, columns))
    sums, moved = [], []
    for p, (x, y) in enumerate(summed):
        x = x + (hold(y, token) if p == 0 else y)
        sums.append(lax.dynamic_slice_in_dim(x, z * group, group, 0))
        moved.append(
            [
                swap(lax.dynamic_slice_in_dim(x, (z ^ j) * group, group, 0), dz=j)
                for j in z_order(fz)
            ]
        )
    errs, loss, after = [], 0.0, sums[-1]
    for p in range(chunks):
        diff = sum(in_order(moved[p], after), sums[p])
        loss = loss + jnp.sum(diff * diff, axis=1, keepdims=True)
        errs.append(diff.astype(jnp.bfloat16))
        after = errs[p]

    err = join(errs, 1)
    come = [swap(err, dz=j) for j in z_order(fz)]
    near = [((0, 0), [join([err] + come[:-1], 0), come[-1]])]
    for b in bits(fy):
        last = [((0, b | at[1]), in_order([swap(e, dy=b) for e in parts])) for at, parts in near]
        near += last
    near = near[: -len(last)]
    totals = grad(n, rows, near, columns, None)
    last[-1][1][-1] = hold(last[-1][1][-1], totals)

    def to_core(pieces):
        return [((1, at[1]), [swap(join(parts, 0), dc=1)]) for at, parts in pieces]

    far = [(at, [hold(e, last[-1][1][-1])]) for at, (e,) in to_core(near)]
    far_last = to_core(last)
    totals = grad(n, rows, far + last, columns, totals)
    back = grad(n, rows, far_last, columns, totals, (in_vmem(ids), loss))
    pieces = near + far + last + far_last
    error = own_rows(n, [at for at, _ in pieces], own, width, [e[0][:group] for _, e in pieces])

    back = jnp.sum(lax.all_to_all(back, "lat", 0, 0, tiled=True), axis=0)
    return error, back[:, k_count] / width, back[:, :k_count]


def solution(mesh):
    in_specs = (P("groups", None), P("groups", None), P("lat", None), P(("groups", "lat"), None))
    out_specs = (P(("groups", "lat"), None), P(("groups", "lat")), P(("groups", "lat"), None))
    return jax.shard_map(local, mesh=mesh, in_specs=in_specs, out_specs=out_specs, check_vma=False)
```

```python
import functools

import jax
import jax.numpy as jnp
from jax import lax
from jax.experimental import pallas as pl
from jax.experimental.pallas import tpu as pltpu
from jax.sharding import PartitionSpec as P

CHUNKS = 2
ROW_STEP = 16
LANES = 128
SUBLANES = 8
LOADS = 4
VMEM = pl.BlockSpec(memory_space=pltpu.VMEM)
HBM = pl.BlockSpec(memory_space=pltpu.HBM)


def factors(n):
    assert n > 1 and n & (n - 1) == 0
    c = 2
    m = n // c
    y = 1
    while 4 * y * y <= m:
        y *= 2
    return m // y, y, c


def place(n, index):
    _, y, c = factors(n)
    return index // (y * c), (index // c) % y, index % c


def bits(size):
    return [1 << i for i in range(size.bit_length() - 1)]


def z_order(fz):
    return ([fz - 1] if fz > 1 else []) + list(range(1, fz - 1))


def pairs(n, dz, dy, dc):
    _, fy, fc = factors(n)
    out = []
    for i in range(n):
        z, y, c = place(n, i)
        out.append((i, ((z ^ dz) * fy + (y ^ dy)) * fc + (c ^ dc)))
    return out


def cost(flops, size):
    return pl.CostEstimate(flops=flops, bytes_accessed=size, transcendentals=0)


def params():
    return pltpu.CompilerParams(vmem_limit_bytes=12 * 1024 * 1024)


def in_hbm(x):
    return pltpu.with_memory_space_constraint(x, pltpu.HBM)


def in_vmem(x):
    return pltpu.with_memory_space_constraint(x, pltpu.VMEM)


def column(n, chunk, chunks, sub, dy, dc):
    _, fy, fc = factors(n)
    _, y, c = place(n, lax.axis_index("lat"))
    return pl.multiple_of((((c ^ dc) * fy + (y ^ dy)) * chunks + chunk) * sub, sub)


def hold(x, *after):
    def kernel(x_ref, *refs):
        refs[-1][...] = x_ref[...]

    return pl.pallas_call(
        kernel,
        out_shape=jax.ShapeDtypeStruct(x.shape, x.dtype),
        in_specs=[VMEM] * (1 + len(after)),
        out_specs=VMEM,
        input_output_aliases={0: 0},
        compiler_params=params(),
        name="hold",
    )(*[in_vmem(a) for a in (x, *after)])


def loads_of(decoder_hbm, col, buf, sem):
    count = sem.shape[0]
    step = buf.shape[0] // count
    return [
        pltpu.make_async_copy(
            decoder_hbm.at[pl.ds(i * step, step), pl.ds(col, buf.shape[1])],
            buf.at[pl.ds(i * step, step)],
            sem.at[i],
        )
        for i in range(count)
    ]


def decode_kernel(n, own, chunks, parts, first, *refs):
    fz, fy, fc = factors(n)
    me = lax.axis_index("lat")
    refs = list(refs)
    if first:
        ids_hbm, codes_hbm = refs.pop(0), refs.pop(0)
    else:
        dense_ref = refs.pop(0)
    decoder_hbm, targets_hbm = refs.pop(0), refs.pop(0)
    if len(refs) > 4 + len(parts) and not first:
        refs.pop(0)
    outs = [refs.pop(0) for _ in parts]
    if first:
        dense_ref = refs.pop(0)
    buf, sem, targets_ref, small = refs[:4]
    smalls_in = [(targets_hbm, targets_ref)]
    if first:
        ids_ref, codes_ref = refs[4:]
        smalls_in = [(ids_hbm, ids_ref), (codes_hbm, codes_ref)] + smalls_in
    smalls = [pltpu.make_async_copy(a, b, small.at[i]) for i, (a, b) in enumerate(smalls_in)]
    for copy in smalls:
        copy.start()
    rows, lat_dev = dense_ref.shape
    sub = outs[0].shape[1] // fy
    cols = [column(n, p, chunks, sub, o, dc) for p, dc in parts for o in range(fy)]
    loads = [loads_of(decoder_hbm, col, buf.at[i], sem.at[i]) for i, col in enumerate(cols)]
    for copies in loads:
        for copy in copies:
            copy.start()
    for copy in smalls:
        copy.wait()
    if first:
        k_count = ids_ref.shape[1]
        assert lat_dev <= 512
        half = lat_dev // 2
        lanes = (lax.broadcasted_iota(jnp.int32, (ROW_STEP, lat_dev), 1) - half).astype(jnp.bfloat16)

        def body(g, carry):
            at = pl.ds(pl.multiple_of(g * ROW_STEP, ROW_STEP), ROW_STEP)
            ids = ids_ref[at, :] - (me * lat_dev + half)
            ids = jnp.where((ids >= -half) & (ids < half), ids, half + 44).astype(jnp.bfloat16)
            codes = codes_ref[at, :]
            acc = jnp.zeros((ROW_STEP, lat_dev), jnp.bfloat16)
            for k in range(k_count):
                acc = jnp.where(ids[:, k : k + 1] == lanes, codes[:, k : k + 1], acc)
            dense_ref[at, :] = acc
            return carry

        lax.fori_loop(0, rows // ROW_STEP, body, 0)
    per = SUBLANES // own
    tile = pl.ds(pl.multiple_of(me // per * SUBLANES, SUBLANES), SUBLANES)
    mine = lax.broadcasted_iota(jnp.int32, (SUBLANES, sub), 0) // own == me % per
    for i, col in enumerate(cols):
        for copy in loads[i]:
            copy.wait()
        out_ref = outs[i // fy]
        here = slice(i % fy * sub, (i % fy + 1) * sub)
        out_ref[:, here] = jnp.dot(dense_ref[...], buf[i], preferred_element_type=jnp.float32)
        target = targets_ref[:, pl.ds(col, sub)].astype(jnp.float32)
        target = jnp.concatenate([target] * per, axis=0)
        out_ref[tile, here] -= jnp.where(mine, target, 0.0)


def decode(n, chunks, sub, parts, decoder, targets, start=None, dense=None, after=None):
    _, fy, _ = factors(n)
    first = start is not None
    rows = start[0].shape[0] if first else dense.shape[0]
    lat_dev = decoder.shape[0]
    out = [pltpu.VMEM((rows, fy * sub), jnp.float32)] * len(parts)
    count = len(parts) * fy
    scratch = [
        pltpu.VMEM((count, lat_dev, sub), jnp.bfloat16),
        pltpu.SemaphoreType.DMA((count, 1)),
        pltpu.VMEM(targets.shape, targets.dtype),
        pltpu.SemaphoreType.DMA((3,)),
    ]
    if first:
        args = [in_hbm(x) for x in (*start, decoder, targets)]
        specs = [HBM] * 4
        out.append(pltpu.VMEM((rows, lat_dev), jnp.bfloat16))
        scratch += [pltpu.VMEM(x.shape, x.dtype) for x in start]
    else:
        args, specs = [dense, in_hbm(decoder), in_hbm(targets)], [VMEM, HBM, HBM]
        if after is not None:
            args.append(in_vmem(after))
            specs.append(VMEM)
    return pl.pallas_call(
        functools.partial(decode_kernel, n, rows // n, chunks, parts, first),
        out_shape=out,
        in_specs=specs,
        out_specs=[VMEM] * len(out),
        scratch_shapes=scratch,
        compiler_params=params(),
        cost_estimate=cost(2 * rows * lat_dev * count * sub, 4 * lat_dev * count * sub),
        name="decode",
    )(*args)


def fetch_kernel(n, places, decoder_hbm, ids_hbm, _, *refs):
    outs = refs[: len(places)]
    ids_ref, token_ref, sem, ids_sem = refs[len(places) :]
    copies = [pltpu.make_async_copy(ids_hbm, ids_ref, ids_sem)]
    for i, (dc, dy) in enumerate(places):
        col = column(n, 0, 1, outs[i].shape[1], dy, dc)
        copies += loads_of(decoder_hbm, col, outs[i], sem.at[i])
    for copy in copies:
        copy.start()
    token_ref[...] = jnp.zeros_like(token_ref)
    for copy in copies:
        copy.wait()


def fetch(n, width, places, decoder, ids, after):
    block = pltpu.VMEM((decoder.shape[0], width), decoder.dtype)
    return pl.pallas_call(
        functools.partial(fetch_kernel, n, places),
        out_shape=[block] * len(places)
        + [pltpu.VMEM(ids.shape, ids.dtype), pltpu.VMEM((SUBLANES, LANES), jnp.float32)],
        in_specs=[HBM, HBM, VMEM],
        out_specs=[VMEM] * (2 + len(places)),
        scratch_shapes=[pltpu.SemaphoreType.DMA((len(places), LOADS)), pltpu.SemaphoreType.DMA],
        compiler_params=params(),
        cost_estimate=cost(0, decoder.shape[0] * len(places) * width * 2),
        name="fetch",
    )(in_hbm(decoder), in_hbm(ids), in_vmem(after))


def grad_kernel(n, counts, with_prev, final, *refs):
    refs = list(refs)
    errs = [[refs.pop(0) for _ in range(count)] for count in counts]
    columns = [refs.pop(0) for _ in counts]
    total = refs.pop(0)[...] if with_prev else None
    for parts, columns_ref in zip(errs, columns):
        err = parts[0][...] if len(parts) == 1 else jnp.concatenate([e[...] for e in parts], axis=0)
        part = lax.dot_general(
            err,
            columns_ref[...],
            (((1,), (1,)), ((), ())),
            preferred_element_type=jnp.float32,
        )
        total = part if total is None else total + part
    if not final:
        refs[0][...] = total
        return
    ids_ref, loss_ref, out_ref, totals_ref = refs
    totals_ref[...] = total
    rows, k_count = ids_ref.shape
    lat_dev = total.shape[1]
    own = out_ref.shape[1]
    fz, _, _ = factors(n)
    me = lax.axis_index("lat")
    z, _, _ = place(n, me)
    group = rows // fz
    places = lax.broadcasted_iota(jnp.int32, (ROW_STEP, LANES), 1)
    pad = jnp.zeros((ROW_STEP, LANES - k_count), jnp.int32)
    for q, j in enumerate([0] + z_order(fz)):
        for s in range(0, group, ROW_STEP):
            first = (z ^ j) * group + s
            rows_at = pl.ds(pl.multiple_of(first, ROW_STEP), ROW_STEP)
            ids = jnp.concatenate([ids_ref[rows_at, :] - me * lat_dev, pad], axis=1)
            held = jnp.where(places < k_count, ids // LANES, -1)
            inside = ids % LANES
            acc = jnp.zeros((ROW_STEP, LANES), jnp.float32)
            if q == 0:
                acc = jnp.where(places == k_count, loss_ref[s : s + ROW_STEP, :], acc)
            here = slice(q * group + s, q * group + s + ROW_STEP)
            for t in range(lat_dev // LANES):
                values = totals_ref[here, t * LANES : (t + 1) * LANES]
                found = jnp.take_along_axis(values, inside, axis=1, mode="promise_in_bounds")
                acc = jnp.where(held == t, found, acc)
            for d in range(ROW_STEP // own):
                out_ref[first // own + d] = acc[d * own : (d + 1) * own, :]


def grad(n, rows, pieces, columns, prev, final=None):
    lat_dev, wide = columns[pieces[0][0]].shape
    counts = tuple(len(e) for _, e in pieces)
    args = [x for _, e in pieces for x in e] + [in_vmem(columns[at]) for at, _ in pieces]
    if prev is not None:
        args.append(in_vmem(prev))
    if final is not None:
        args += list(final)
    totals = pltpu.VMEM((rows, lat_dev), jnp.float32)
    size = wide * len(pieces)
    return pl.pallas_call(
        functools.partial(grad_kernel, n, counts, prev is not None, final is not None),
        out_shape=totals if final is None else pltpu.VMEM((n, rows // n, LANES), jnp.float32),
        in_specs=[VMEM] * len(args),
        out_specs=VMEM,
        scratch_shapes=[] if final is None else [totals],
        compiler_params=params(),
        cost_estimate=cost(2 * rows * lat_dev * size, 4 * lat_dev * size),
        name="grad",
    )(*args)


def own_kernel(n, blocks, own, *refs):
    errs, out_ref = refs[:-1], refs[-1]
    _, fy, fc = factors(n)
    _, y, c = place(n, lax.axis_index("lat"))
    group, sub = errs[0].shape
    row = lax.broadcasted_iota(jnp.int32, (own, group), 0) + (y * fc + c) * own
    want = lax.broadcasted_iota(jnp.int32, (own, group), 1)
    mine = jnp.where(row == want, 1.0, 0.0).astype(jnp.bfloat16)
    for err, (dc, dy) in zip(errs, blocks):
        rows = jnp.dot(mine, err[...], preferred_element_type=jnp.float32)
        out_ref[:, pl.ds(column(n, 0, 1, sub, dy, dc), sub)] = rows.astype(jnp.bfloat16)


def own_rows(n, blocks, own, width, errs):
    return pl.pallas_call(
        functools.partial(own_kernel, n, tuple(blocks), own),
        out_shape=jax.ShapeDtypeStruct((own, width), jnp.bfloat16),
        in_specs=[VMEM] * len(errs),
        out_specs=VMEM,
        compiler_params=params(),
        name="own_rows",
    )(*errs)


def local(codes, indices, decoder, targets):
    width = decoder.shape[1]
    rows, k_count = codes.shape
    n = lax.axis_size("lat")
    own = rows // n
    fz, fy, fc = factors(n)
    group = rows // fz
    chunks = CHUNKS
    sub = width // (fc * fy * chunks)
    z, _, _ = place(n, lax.axis_index("lat"))

    def swap(x, dz=0, dy=0, dc=0):
        return lax.ppermute(x, "lat", pairs(n, dz, dy, dc))

    def join(xs, axis):
        return xs[0] if len(xs) == 1 else jnp.concatenate(xs, axis=axis)

    def in_order(xs, after=None):
        for i, x in enumerate(xs):
            if after is not None:
                xs[i] = hold(x, after)
            after = xs[i]
        return xs

    others = tuple((p, 1) for p in range(chunks))
    *parts, dense = decode(n, chunks, sub, others, decoder, targets, (indices, codes))
    came = [swap(part, dc=1) for part in parts]
    summed, leaving, after = [], [], None
    for p in range(chunks):
        (part,) = decode(n, chunks, sub, ((p, 0),), decoder, targets, dense=dense, after=after)
        total = part + came[p]
        blocks = [total[:, o * sub : (o + 1) * sub] for o in range(fy)]
        got = None
        for b in reversed(bits(fy)):
            if got is not None:
                blocks = [blocks[o] + got[:, o * sub : (o + 1) * sub] for o in range(2 * b)]
            after = join(blocks[b:], 1)
            got = swap(after, dy=b)
        leaving.append(after)
        summed.append((blocks[0], got))

    places = tuple((dc, dy) for dy in range(fy) for dc in range(fc))
    *columns, ids, token = fetch(n, chunks * sub, places, decoder, indices, leaving[-1])
    columns = dict(zip(places, columns))
    sums, moved = [], []
    for p, (x, y) in enumerate(summed):
        x = x + (hold(y, token) if p == 0 else y)
        sums.append(lax.dynamic_slice_in_dim(x, z * group, group, 0))
        moved.append(
            [
                swap(lax.dynamic_slice_in_dim(x, (z ^ j) * group, group, 0), dz=j)
                for j in z_order(fz)
            ]
        )
    errs, loss, after = [], 0.0, sums[-1]
    for p in range(chunks):
        diff = sum(in_order(moved[p], after), sums[p])
        loss = loss + jnp.sum(diff * diff, axis=1, keepdims=True)
        errs.append(diff.astype(jnp.bfloat16))
        after = errs[p]

    err = join(errs, 1)
    come = [swap(err, dz=j) for j in z_order(fz)]
    near = [((0, 0), [join([err] + come[:-1], 0), come[-1]])]
    for b in bits(fy):
        last = [((0, b | at[1]), in_order([swap(e, dy=b) for e in parts])) for at, parts in near]
        near += last
    near = near[: -len(last)]
    totals = grad(n, rows, near, columns, None)
    last[-1][1][-1] = hold(last[-1][1][-1], totals)

    def to_core(pieces):
        return [((1, at[1]), [swap(join(parts, 0), dc=1)]) for at, parts in pieces]

    far = [(at, [hold(e, last[-1][1][-1])]) for at, (e,) in to_core(near)]
    far_last = to_core(last)
    totals = grad(n, rows, far, columns, totals)
    totals = grad(n, rows, last, columns, totals)
    back = grad(n, rows, far_last, columns, totals, (in_vmem(ids), loss))
    pieces = near + far + last + far_last
    error = own_rows(n, [at for at, _ in pieces], own, width, [e[0][:group] for _, e in pieces])

    back = jnp.sum(lax.all_to_all(back, "lat", 0, 0, tiled=True), axis=0)
    return error, back[:, k_count] / width, back[:, :k_count]


def solution(mesh):
    in_specs = (P("groups", None), P("groups", None), P("lat", None), P(("groups", "lat"), None))
    out_specs = (P(("groups", "lat"), None), P(("groups", "lat")), P(("groups", "lat"), None))
    return jax.shard_map(local, mesh=mesh, in_specs=in_specs, out_specs=out_specs, check_vma=False)
```

```python
import functools

import jax
import jax.numpy as jnp
from jax import lax
from jax.experimental import pallas as pl
from jax.experimental.pallas import tpu as pltpu
from jax.sharding import PartitionSpec as P

CHUNKS = 2
ROW_STEP = 16
LANES = 128
SUBLANES = 8
LOADS = 4
VMEM = pl.BlockSpec(memory_space=pltpu.VMEM)
HBM = pl.BlockSpec(memory_space=pltpu.HBM)


def factors(n):
    assert n > 1 and n & (n - 1) == 0
    c = 2
    m = n // c
    y = 1
    while 4 * y * y <= m:
        y *= 2
    return m // y, y, c


def place(n, index):
    _, y, c = factors(n)
    return index // (y * c), (index // c) % y, index % c


def bits(size):
    return [1 << i for i in range(size.bit_length() - 1)]


def z_order(fz):
    return ([fz - 1] if fz > 1 else []) + list(range(1, fz - 1))


def pairs(n, dz, dy, dc):
    _, fy, fc = factors(n)
    out = []
    for i in range(n):
        z, y, c = place(n, i)
        out.append((i, ((z ^ dz) * fy + (y ^ dy)) * fc + (c ^ dc)))
    return out


def cost(flops, size):
    return pl.CostEstimate(flops=flops, bytes_accessed=size, transcendentals=0)


def params():
    return pltpu.CompilerParams(vmem_limit_bytes=12 * 1024 * 1024)


def in_hbm(x):
    return pltpu.with_memory_space_constraint(x, pltpu.HBM)


def in_vmem(x):
    return pltpu.with_memory_space_constraint(x, pltpu.VMEM)


def column(n, chunk, chunks, sub, dy, dc):
    _, fy, fc = factors(n)
    _, y, c = place(n, lax.axis_index("lat"))
    return pl.multiple_of((((c ^ dc) * fy + (y ^ dy)) * chunks + chunk) * sub, sub)


def hold(x, *after):
    def kernel(x_ref, *refs):
        refs[-1][...] = x_ref[...]

    return pl.pallas_call(
        kernel,
        out_shape=jax.ShapeDtypeStruct(x.shape, x.dtype),
        in_specs=[VMEM] * (1 + len(after)),
        out_specs=VMEM,
        input_output_aliases={0: 0},
        compiler_params=params(),
        name="hold",
    )(*[in_vmem(a) for a in (x, *after)])


def loads_of(decoder_hbm, col, buf, sem):
    count = sem.shape[0]
    step = buf.shape[0] // count
    return [
        pltpu.make_async_copy(
            decoder_hbm.at[pl.ds(i * step, step), pl.ds(col, buf.shape[1])],
            buf.at[pl.ds(i * step, step)],
            sem.at[i],
        )
        for i in range(count)
    ]


def decode_kernel(n, own, chunks, parts, first, *refs):
    fz, fy, fc = factors(n)
    me = lax.axis_index("lat")
    refs = list(refs)
    if first:
        ids_hbm, codes_hbm = refs.pop(0), refs.pop(0)
    else:
        dense_ref = refs.pop(0)
    decoder_hbm, targets_hbm = refs.pop(0), refs.pop(0)
    if len(refs) > 4 + len(parts) and not first:
        refs.pop(0)
    outs = [refs.pop(0) for _ in parts]
    if first:
        dense_ref = refs.pop(0)
    buf, sem, targets_ref, small = refs[:4]
    smalls_in = [(targets_hbm, targets_ref)]
    if first:
        ids_ref, codes_ref = refs[4:]
        smalls_in = [(ids_hbm, ids_ref), (codes_hbm, codes_ref)] + smalls_in
    smalls = [pltpu.make_async_copy(a, b, small.at[i]) for i, (a, b) in enumerate(smalls_in)]
    for copy in smalls:
        copy.start()
    rows, lat_dev = dense_ref.shape
    sub = outs[0].shape[1] // fy
    cols = [column(n, p, chunks, sub, o, dc) for p, dc in parts for o in range(fy)]
    loads = [loads_of(decoder_hbm, col, buf.at[i], sem.at[i]) for i, col in enumerate(cols)]
    for copies in loads:
        for copy in copies:
            copy.start()
    for copy in smalls:
        copy.wait()
    if first:
        k_count = ids_ref.shape[1]
        assert lat_dev <= 512
        half = lat_dev // 2
        lanes = (lax.broadcasted_iota(jnp.int32, (ROW_STEP, lat_dev), 1) - half).astype(jnp.bfloat16)

        def body(g, carry):
            at = pl.ds(pl.multiple_of(g * ROW_STEP, ROW_STEP), ROW_STEP)
            ids = ids_ref[at, :] - (me * lat_dev + half)
            ids = jnp.where((ids >= -half) & (ids < half), ids, half + 44).astype(jnp.bfloat16)
            codes = codes_ref[at, :]
            acc = jnp.zeros((ROW_STEP, lat_dev), jnp.bfloat16)
            for k in range(k_count):
                acc = jnp.where(ids[:, k : k + 1] == lanes, codes[:, k : k + 1], acc)
            dense_ref[at, :] = acc
            return carry

        lax.fori_loop(0, rows // ROW_STEP, body, 0)
    per = SUBLANES // own
    tile = pl.ds(pl.multiple_of(me // per * SUBLANES, SUBLANES), SUBLANES)
    mine = lax.broadcasted_iota(jnp.int32, (SUBLANES, sub), 0) // own == me % per
    for i, col in enumerate(cols):
        for copy in loads[i]:
            copy.wait()
        out_ref = outs[i // fy]
        here = slice(i % fy * sub, (i % fy + 1) * sub)
        out_ref[:, here] = jnp.dot(dense_ref[...], buf[i], preferred_element_type=jnp.float32)
        target = targets_ref[:, pl.ds(col, sub)].astype(jnp.float32)
        target = jnp.concatenate([target] * per, axis=0)
        out_ref[tile, here] -= jnp.where(mine, target, 0.0)


def decode(n, chunks, sub, parts, decoder, targets, start=None, dense=None, after=None):
    _, fy, _ = factors(n)
    first = start is not None
    rows = start[0].shape[0] if first else dense.shape[0]
    lat_dev = decoder.shape[0]
    out = [pltpu.VMEM((rows, fy * sub), jnp.float32)] * len(parts)
    count = len(parts) * fy
    scratch = [
        pltpu.VMEM((count, lat_dev, sub), jnp.bfloat16),
        pltpu.SemaphoreType.DMA((count, 1)),
        pltpu.VMEM(targets.shape, targets.dtype),
        pltpu.SemaphoreType.DMA((3,)),
    ]
    if first:
        args = [in_hbm(x) for x in (*start, decoder, targets)]
        specs = [HBM] * 4
        out.append(pltpu.VMEM((rows, lat_dev), jnp.bfloat16))
        scratch += [pltpu.VMEM(x.shape, x.dtype) for x in start]
    else:
        args, specs = [dense, in_hbm(decoder), in_hbm(targets)], [VMEM, HBM, HBM]
        if after is not None:
            args.append(in_vmem(after))
            specs.append(VMEM)
    return pl.pallas_call(
        functools.partial(decode_kernel, n, rows // n, chunks, parts, first),
        out_shape=out,
        in_specs=specs,
        out_specs=[VMEM] * len(out),
        scratch_shapes=scratch,
        compiler_params=params(),
        cost_estimate=cost(2 * rows * lat_dev * count * sub, 4 * lat_dev * count * sub),
        name="decode",
    )(*args)


def fetch_kernel(n, places, decoder_hbm, ids_hbm, _, *refs):
    outs = refs[: len(places)]
    ids_ref, token_ref, sem, ids_sem = refs[len(places) :]
    copies = [pltpu.make_async_copy(ids_hbm, ids_ref, ids_sem)]
    for i, (dc, dy) in enumerate(places):
        col = column(n, 0, 1, outs[i].shape[1], dy, dc)
        copies += loads_of(decoder_hbm, col, outs[i], sem.at[i])
    for copy in copies:
        copy.start()
    token_ref[...] = jnp.zeros_like(token_ref)
    for copy in copies:
        copy.wait()


def fetch(n, width, places, decoder, ids, after):
    block = pltpu.VMEM((decoder.shape[0], width), decoder.dtype)
    return pl.pallas_call(
        functools.partial(fetch_kernel, n, places),
        out_shape=[block] * len(places)
        + [pltpu.VMEM(ids.shape, ids.dtype), pltpu.VMEM((SUBLANES, LANES), jnp.float32)],
        in_specs=[HBM, HBM, VMEM],
        out_specs=[VMEM] * (2 + len(places)),
        scratch_shapes=[pltpu.SemaphoreType.DMA((len(places), LOADS)), pltpu.SemaphoreType.DMA],
        compiler_params=params(),
        cost_estimate=cost(0, decoder.shape[0] * len(places) * width * 2),
        name="fetch",
    )(in_hbm(decoder), in_hbm(ids), in_vmem(after))


def grad_kernel(n, counts, with_prev, final, *refs):
    refs = list(refs)
    errs = [[refs.pop(0) for _ in range(count)] for count in counts]
    columns = [refs.pop(0) for _ in counts]
    total = refs.pop(0)[...] if with_prev else None
    for parts, columns_ref in zip(errs, columns):
        err = parts[0][...] if len(parts) == 1 else jnp.concatenate([e[...] for e in parts], axis=0)
        part = lax.dot_general(
            err,
            columns_ref[...],
            (((1,), (1,)), ((), ())),
            preferred_element_type=jnp.float32,
        )
        total = part if total is None else total + part
    if not final:
        refs[0][...] = total
        return
    ids_ref, loss_ref, out_ref, totals_ref = refs
    totals_ref[...] = total
    rows, k_count = ids_ref.shape
    lat_dev = total.shape[1]
    own = out_ref.shape[1]
    fz, _, _ = factors(n)
    me = lax.axis_index("lat")
    z, _, _ = place(n, me)
    group = rows // fz
    places = lax.broadcasted_iota(jnp.int32, (ROW_STEP, LANES), 1)
    pad = jnp.zeros((ROW_STEP, LANES - k_count), jnp.int32)
    for q, j in enumerate([0] + z_order(fz)):
        for s in range(0, group, ROW_STEP):
            first = (z ^ j) * group + s
            rows_at = pl.ds(pl.multiple_of(first, ROW_STEP), ROW_STEP)
            ids = jnp.concatenate([ids_ref[rows_at, :] - me * lat_dev, pad], axis=1)
            held = jnp.where(places < k_count, ids // LANES, -1)
            inside = ids % LANES
            acc = jnp.zeros((ROW_STEP, LANES), jnp.float32)
            if q == 0:
                acc = jnp.where(places == k_count, loss_ref[s : s + ROW_STEP, :], acc)
            here = slice(q * group + s, q * group + s + ROW_STEP)
            for t in range(lat_dev // LANES):
                values = totals_ref[here, t * LANES : (t + 1) * LANES]
                found = jnp.take_along_axis(values, inside, axis=1, mode="promise_in_bounds")
                acc = jnp.where(held == t, found, acc)
            for d in range(ROW_STEP // own):
                out_ref[first // own + d] = acc[d * own : (d + 1) * own, :]


def grad(n, rows, pieces, columns, prev, final=None):
    lat_dev, wide = columns[pieces[0][0]].shape
    counts = tuple(len(e) for _, e in pieces)
    args = [x for _, e in pieces for x in e] + [in_vmem(columns[at]) for at, _ in pieces]
    if prev is not None:
        args.append(in_vmem(prev))
    if final is not None:
        args += list(final)
    totals = pltpu.VMEM((rows, lat_dev), jnp.float32)
    size = wide * len(pieces)
    return pl.pallas_call(
        functools.partial(grad_kernel, n, counts, prev is not None, final is not None),
        out_shape=totals if final is None else pltpu.VMEM((n, rows // n, LANES), jnp.float32),
        in_specs=[VMEM] * len(args),
        out_specs=VMEM,
        scratch_shapes=[] if final is None else [totals],
        compiler_params=params(),
        cost_estimate=cost(2 * rows * lat_dev * size, 4 * lat_dev * size),
        name="grad",
    )(*args)


def own_kernel(n, blocks, own, *refs):
    errs, out_ref = refs[:-1], refs[-1]
    _, fy, fc = factors(n)
    _, y, c = place(n, lax.axis_index("lat"))
    group, sub = errs[0].shape
    row = lax.broadcasted_iota(jnp.int32, (own, group), 0) + (y * fc + c) * own
    want = lax.broadcasted_iota(jnp.int32, (own, group), 1)
    mine = jnp.where(row == want, 1.0, 0.0).astype(jnp.bfloat16)
    for err, (dc, dy) in zip(errs, blocks):
        rows = jnp.dot(mine, err[...], preferred_element_type=jnp.float32)
        out_ref[:, pl.ds(column(n, 0, 1, sub, dy, dc), sub)] = rows.astype(jnp.bfloat16)


def own_rows(n, blocks, own, width, errs):
    return pl.pallas_call(
        functools.partial(own_kernel, n, tuple(blocks), own),
        out_shape=jax.ShapeDtypeStruct((own, width), jnp.bfloat16),
        in_specs=[VMEM] * len(errs),
        out_specs=VMEM,
        compiler_params=params(),
        name="own_rows",
    )(*errs)


def local(codes, indices, decoder, targets):
    width = decoder.shape[1]
    rows, k_count = codes.shape
    n = lax.axis_size("lat")
    own = rows // n
    fz, fy, fc = factors(n)
    group = rows // fz
    chunks = CHUNKS
    sub = width // (fc * fy * chunks)
    z, _, _ = place(n, lax.axis_index("lat"))

    def swap(x, dz=0, dy=0, dc=0):
        return lax.ppermute(x, "lat", pairs(n, dz, dy, dc))

    def join(xs, axis):
        return xs[0] if len(xs) == 1 else jnp.concatenate(xs, axis=axis)

    def in_order(xs, after=None):
        for i, x in enumerate(xs):
            if after is not None:
                xs[i] = hold(x, after)
            after = xs[i]
        return xs

    others = tuple((p, 1) for p in range(chunks))
    *parts, dense = decode(n, chunks, sub, others, decoder, targets, (indices, codes))
    came = [swap(part, dc=1) for part in parts]
    summed, leaving, after = [], [], None
    for p in range(chunks):
        (part,) = decode(n, chunks, sub, ((p, 0),), decoder, targets, dense=dense, after=after)
        total = part + came[p]
        blocks = [total[:, o * sub : (o + 1) * sub] for o in range(fy)]
        got = None
        for b in reversed(bits(fy)):
            if got is not None:
                blocks = [blocks[o] + got[:, o * sub : (o + 1) * sub] for o in range(2 * b)]
            after = join(blocks[b:], 1)
            got = swap(after, dy=b)
        leaving.append(after)
        summed.append((blocks[0], got))

    places = tuple((dc, dy) for dy in range(fy) for dc in range(fc))
    *columns, ids, token = fetch(n, chunks * sub, places, decoder, indices, leaving[-1])
    columns = dict(zip(places, columns))
    sums, moved = [], []
    for p, (x, y) in enumerate(summed):
        x = x + (hold(y, token) if p == 0 else y)
        sums.append(lax.dynamic_slice_in_dim(x, z * group, group, 0))
        moved.append(
            [
                swap(lax.dynamic_slice_in_dim(x, (z ^ j) * group, group, 0), dz=j)
                for j in z_order(fz)
            ]
        )
    errs, loss, after = [], 0.0, sums[-1]
    for p in range(chunks):
        diff = sum(in_order(moved[p], after), sums[p])
        loss = loss + jnp.sum(diff * diff, axis=1, keepdims=True)
        errs.append(diff.astype(jnp.bfloat16))
        after = errs[p]

    err = join(errs, 1)
    come = [swap(err, dz=j) for j in z_order(fz)]
    near = [((0, 0), [join([err] + come[:-1], 0), come[-1]])]
    for b in bits(fy):
        last = [((0, b | at[1]), in_order([swap(e, dy=b) for e in parts])) for at, parts in near]
        near += last
    near = near[: -len(last)]
    totals = grad(n, rows, near, columns, None)
    last[-1][1][-1] = hold(last[-1][1][-1], totals)

    far = [((1, at[1]), [hold(swap(join(e, 0), dc=1), last[-1][1][-1])]) for at, e in near]
    far_last = [((1, at[1]), [swap(e, dc=1) for e in parts]) for at, parts in last]
    totals = grad(n, rows, last, columns, totals)
    totals = grad(n, rows, far, columns, totals)
    back = grad(n, rows, far_last, columns, totals, (in_vmem(ids), loss))
    pieces = near + far + last + far_last
    error = own_rows(n, [at for at, _ in pieces], own, width, [e[0][:group] for _, e in pieces])

    back = jnp.sum(lax.all_to_all(back, "lat", 0, 0, tiled=True), axis=0)
    return error, back[:, k_count] / width, back[:, :k_count]


def solution(mesh):
    in_specs = (P("groups", None), P("groups", None), P("lat", None), P(("groups", "lat"), None))
    out_specs = (P(("groups", "lat"), None), P(("groups", "lat")), P(("groups", "lat"), None))
    return jax.shard_map(local, mesh=mesh, in_specs=in_specs, out_specs=out_specs, check_vma=False)
```

```python
import functools

import jax
import jax.numpy as jnp
from jax import lax
from jax.experimental import pallas as pl
from jax.experimental.pallas import tpu as pltpu
from jax.sharding import PartitionSpec as P

CHUNKS = 2
ROW_STEP = 16
LANES = 128
SUBLANES = 8
LOADS = 4
VMEM = pl.BlockSpec(memory_space=pltpu.VMEM)
HBM = pl.BlockSpec(memory_space=pltpu.HBM)


def factors(n):
    assert n > 1 and n & (n - 1) == 0
    c = 2
    m = n // c
    y = 1
    while 4 * y * y <= m:
        y *= 2
    return m // y, y, c


def place(n, index):
    _, y, c = factors(n)
    return index // (y * c), (index // c) % y, index % c


def bits(size):
    return [1 << i for i in range(size.bit_length() - 1)]


def z_order(fz):
    return ([fz - 1] if fz > 1 else []) + list(range(1, fz - 1))


def pairs(n, dz, dy, dc):
    _, fy, fc = factors(n)
    out = []
    for i in range(n):
        z, y, c = place(n, i)
        out.append((i, ((z ^ dz) * fy + (y ^ dy)) * fc + (c ^ dc)))
    return out


def cost(flops, size):
    return pl.CostEstimate(flops=flops, bytes_accessed=size, transcendentals=0)


def params():
    return pltpu.CompilerParams(vmem_limit_bytes=12 * 1024 * 1024)


def in_hbm(x):
    return pltpu.with_memory_space_constraint(x, pltpu.HBM)


def in_vmem(x):
    return pltpu.with_memory_space_constraint(x, pltpu.VMEM)


def column(n, chunk, chunks, sub, dy, dc):
    _, fy, fc = factors(n)
    _, y, c = place(n, lax.axis_index("lat"))
    return pl.multiple_of((((c ^ dc) * fy + (y ^ dy)) * chunks + chunk) * sub, sub)


def hold(x, *after):
    def kernel(x_ref, *refs):
        refs[-1][...] = x_ref[...]

    return pl.pallas_call(
        kernel,
        out_shape=jax.ShapeDtypeStruct(x.shape, x.dtype),
        in_specs=[VMEM] * (1 + len(after)),
        out_specs=VMEM,
        input_output_aliases={0: 0},
        compiler_params=params(),
        name="hold",
    )(*[in_vmem(a) for a in (x, *after)])


def loads_of(decoder_hbm, col, buf, sem):
    count = sem.shape[0]
    step = buf.shape[0] // count
    return [
        pltpu.make_async_copy(
            decoder_hbm.at[pl.ds(i * step, step), pl.ds(col, buf.shape[1])],
            buf.at[pl.ds(i * step, step)],
            sem.at[i],
        )
        for i in range(count)
    ]


def decode_kernel(n, own, chunks, parts, first, *refs):
    fz, fy, fc = factors(n)
    me = lax.axis_index("lat")
    refs = list(refs)
    if first:
        ids_hbm, codes_hbm = refs.pop(0), refs.pop(0)
    else:
        dense_ref = refs.pop(0)
    decoder_hbm, targets_hbm = refs.pop(0), refs.pop(0)
    if len(refs) > 4 + len(parts) and not first:
        refs.pop(0)
    outs = [refs.pop(0) for _ in parts]
    if first:
        dense_ref = refs.pop(0)
    buf, sem, targets_ref, small = refs[:4]
    smalls_in = [(targets_hbm, targets_ref)]
    if first:
        ids_ref, codes_ref = refs[4:]
        smalls_in = [(ids_hbm, ids_ref), (codes_hbm, codes_ref)] + smalls_in
    smalls = [pltpu.make_async_copy(a, b, small.at[i]) for i, (a, b) in enumerate(smalls_in)]
    for copy in smalls:
        copy.start()
    rows, lat_dev = dense_ref.shape
    sub = outs[0].shape[1] // fy
    cols = [column(n, p, chunks, sub, o, dc) for p, dc in parts for o in range(fy)]
    loads = [loads_of(decoder_hbm, col, buf.at[i], sem.at[i]) for i, col in enumerate(cols)]
    for copies in loads:
        for copy in copies:
            copy.start()
    for copy in smalls:
        copy.wait()
    if first:
        k_count = ids_ref.shape[1]
        assert lat_dev <= 512
        half = lat_dev // 2
        lanes = (lax.broadcasted_iota(jnp.int32, (ROW_STEP, lat_dev), 1) - half).astype(jnp.bfloat16)

        def body(g, carry):
            at = pl.ds(pl.multiple_of(g * ROW_STEP, ROW_STEP), ROW_STEP)
            ids = ids_ref[at, :] - (me * lat_dev + half)
            ids = jnp.where((ids >= -half) & (ids < half), ids, half + 44).astype(jnp.bfloat16)
            codes = codes_ref[at, :]
            acc = jnp.zeros((ROW_STEP, lat_dev), jnp.bfloat16)
            for k in range(k_count):
                acc = jnp.where(ids[:, k : k + 1] == lanes, codes[:, k : k + 1], acc)
            dense_ref[at, :] = acc
            return carry

        lax.fori_loop(0, rows // ROW_STEP, body, 0)
    per = SUBLANES // own
    tile = pl.ds(pl.multiple_of(me // per * SUBLANES, SUBLANES), SUBLANES)
    mine = lax.broadcasted_iota(jnp.int32, (SUBLANES, sub), 0) // own == me % per
    for i, col in enumerate(cols):
        for copy in loads[i]:
            copy.wait()
        out_ref = outs[i // fy]
        here = slice(i % fy * sub, (i % fy + 1) * sub)
        out_ref[:, here] = jnp.dot(dense_ref[...], buf[i], preferred_element_type=jnp.float32)
        target = targets_ref[:, pl.ds(col, sub)].astype(jnp.float32)
        target = jnp.concatenate([target] * per, axis=0)
        out_ref[tile, here] -= jnp.where(mine, target, 0.0)


def decode(n, chunks, sub, parts, decoder, targets, start=None, dense=None, after=None):
    _, fy, _ = factors(n)
    first = start is not None
    rows = start[0].shape[0] if first else dense.shape[0]
    lat_dev = decoder.shape[0]
    out = [pltpu.VMEM((rows, fy * sub), jnp.float32)] * len(parts)
    count = len(parts) * fy
    scratch = [
        pltpu.VMEM((count, lat_dev, sub), jnp.bfloat16),
        pltpu.SemaphoreType.DMA((count, 1)),
        pltpu.VMEM(targets.shape, targets.dtype),
        pltpu.SemaphoreType.DMA((3,)),
    ]
    if first:
        args = [in_hbm(x) for x in (*start, decoder, targets)]
        specs = [HBM] * 4
        out.append(pltpu.VMEM((rows, lat_dev), jnp.bfloat16))
        scratch += [pltpu.VMEM(x.shape, x.dtype) for x in start]
    else:
        args, specs = [dense, in_hbm(decoder), in_hbm(targets)], [VMEM, HBM, HBM]
        if after is not None:
            args.append(in_vmem(after))
            specs.append(VMEM)
    return pl.pallas_call(
        functools.partial(decode_kernel, n, rows // n, chunks, parts, first),
        out_shape=out,
        in_specs=specs,
        out_specs=[VMEM] * len(out),
        scratch_shapes=scratch,
        compiler_params=params(),
        cost_estimate=cost(2 * rows * lat_dev * count * sub, 4 * lat_dev * count * sub),
        name="decode",
    )(*args)


def fetch_kernel(n, places, decoder_hbm, ids_hbm, _, *refs):
    outs = refs[: len(places)]
    ids_ref, token_ref, sem, ids_sem = refs[len(places) :]
    copies = [pltpu.make_async_copy(ids_hbm, ids_ref, ids_sem)]
    for i, (dc, dy) in enumerate(places):
        col = column(n, 0, 1, outs[i].shape[1], dy, dc)
        copies += loads_of(decoder_hbm, col, outs[i], sem.at[i])
    for copy in copies:
        copy.start()
    token_ref[...] = jnp.zeros_like(token_ref)
    for copy in copies:
        copy.wait()


def fetch(n, width, places, decoder, ids, after):
    block = pltpu.VMEM((decoder.shape[0], width), decoder.dtype)
    return pl.pallas_call(
        functools.partial(fetch_kernel, n, places),
        out_shape=[block] * len(places)
        + [pltpu.VMEM(ids.shape, ids.dtype), pltpu.VMEM((SUBLANES, LANES), jnp.float32)],
        in_specs=[HBM, HBM, VMEM],
        out_specs=[VMEM] * (2 + len(places)),
        scratch_shapes=[pltpu.SemaphoreType.DMA((len(places), LOADS)), pltpu.SemaphoreType.DMA],
        compiler_params=params(),
        cost_estimate=cost(0, decoder.shape[0] * len(places) * width * 2),
        name="fetch",
    )(in_hbm(decoder), in_hbm(ids), in_vmem(after))


def grad_kernel(n, counts, with_prev, final, *refs):
    refs = list(refs)
    errs = [[refs.pop(0) for _ in range(count)] for count in counts]
    columns = [refs.pop(0) for _ in counts]
    total = refs.pop(0)[...] if with_prev else None
    for parts, columns_ref in zip(errs, columns):
        err = parts[0][...] if len(parts) == 1 else jnp.concatenate([e[...] for e in parts], axis=0)
        part = lax.dot_general(
            err,
            columns_ref[...],
            (((1,), (1,)), ((), ())),
            preferred_element_type=jnp.float32,
        )
        total = part if total is None else total + part
    if not final:
        refs[0][...] = total
        return
    ids_ref, loss_ref, out_ref, totals_ref = refs
    totals_ref[...] = total
    rows, k_count = ids_ref.shape
    lat_dev = total.shape[1]
    own = out_ref.shape[1]
    fz, _, _ = factors(n)
    me = lax.axis_index("lat")
    z, _, _ = place(n, me)
    group = rows // fz
    places = lax.broadcasted_iota(jnp.int32, (ROW_STEP, LANES), 1)
    pad = jnp.zeros((ROW_STEP, LANES - k_count), jnp.int32)
    for q, j in enumerate([0] + z_order(fz)):
        for s in range(0, group, ROW_STEP):
            first = (z ^ j) * group + s
            rows_at = pl.ds(pl.multiple_of(first, ROW_STEP), ROW_STEP)
            ids = jnp.concatenate([ids_ref[rows_at, :] - me * lat_dev, pad], axis=1)
            held = jnp.where(places < k_count, ids // LANES, -1)
            inside = ids % LANES
            acc = jnp.zeros((ROW_STEP, LANES), jnp.float32)
            if q == 0:
                acc = jnp.where(places == k_count, loss_ref[s : s + ROW_STEP, :], acc)
            here = slice(q * group + s, q * group + s + ROW_STEP)
            for t in range(lat_dev // LANES):
                values = totals_ref[here, t * LANES : (t + 1) * LANES]
                found = jnp.take_along_axis(values, inside, axis=1, mode="promise_in_bounds")
                acc = jnp.where(held == t, found, acc)
            for d in range(ROW_STEP // own):
                out_ref[first // own + d] = acc[d * own : (d + 1) * own, :]


def grad(n, rows, pieces, columns, prev, final=None):
    lat_dev, wide = columns[pieces[0][0]].shape
    counts = tuple(len(e) for _, e in pieces)
    args = [x for _, e in pieces for x in e] + [in_vmem(columns[at]) for at, _ in pieces]
    if prev is not None:
        args.append(in_vmem(prev))
    if final is not None:
        args += list(final)
    totals = pltpu.VMEM((rows, lat_dev), jnp.float32)
    size = wide * len(pieces)
    return pl.pallas_call(
        functools.partial(grad_kernel, n, counts, prev is not None, final is not None),
        out_shape=totals if final is None else pltpu.VMEM((n, rows // n, LANES), jnp.float32),
        in_specs=[VMEM] * len(args),
        out_specs=VMEM,
        scratch_shapes=[] if final is None else [totals],
        compiler_params=params(),
        cost_estimate=cost(2 * rows * lat_dev * size, 4 * lat_dev * size),
        name="grad",
    )(*args)


def own_kernel(n, blocks, own, *refs):
    errs, out_ref = refs[:-1], refs[-1]
    _, fy, fc = factors(n)
    _, y, c = place(n, lax.axis_index("lat"))
    group, sub = errs[0].shape
    row = lax.broadcasted_iota(jnp.int32, (own, group), 0) + (y * fc + c) * own
    want = lax.broadcasted_iota(jnp.int32, (own, group), 1)
    mine = jnp.where(row == want, 1.0, 0.0).astype(jnp.bfloat16)
    for err, (dc, dy) in zip(errs, blocks):
        rows = jnp.dot(mine, err[...], preferred_element_type=jnp.float32)
        out_ref[:, pl.ds(column(n, 0, 1, sub, dy, dc), sub)] = rows.astype(jnp.bfloat16)


def own_rows(n, blocks, own, width, errs):
    return pl.pallas_call(
        functools.partial(own_kernel, n, tuple(blocks), own),
        out_shape=jax.ShapeDtypeStruct((own, width), jnp.bfloat16),
        in_specs=[VMEM] * len(errs),
        out_specs=VMEM,
        compiler_params=params(),
        name="own_rows",
    )(*errs)


def local(codes, indices, decoder, targets):
    width = decoder.shape[1]
    rows, k_count = codes.shape
    n = lax.axis_size("lat")
    own = rows // n
    fz, fy, fc = factors(n)
    group = rows // fz
    chunks = CHUNKS
    sub = width // (fc * fy * chunks)
    z, _, _ = place(n, lax.axis_index("lat"))

    def swap(x, dz=0, dy=0, dc=0):
        return lax.ppermute(x, "lat", pairs(n, dz, dy, dc))

    def join(xs, axis):
        return xs[0] if len(xs) == 1 else jnp.concatenate(xs, axis=axis)

    def in_order(xs, after=None):
        for i, x in enumerate(xs):
            if after is not None:
                xs[i] = hold(x, after)
            after = xs[i]
        return xs

    others = tuple((p, 1) for p in range(chunks))
    *parts, dense = decode(n, chunks, sub, others, decoder, targets, (indices, codes))
    came = [swap(part, dc=1) for part in parts]
    summed, leaving, after = [], [], None
    for p in range(chunks):
        (part,) = decode(n, chunks, sub, ((p, 0),), decoder, targets, dense=dense, after=after)
        total = part + came[p]
        blocks = [total[:, o * sub : (o + 1) * sub] for o in range(fy)]
        got = None
        for b in reversed(bits(fy)):
            if got is not None:
                blocks = [blocks[o] + got[:, o * sub : (o + 1) * sub] for o in range(2 * b)]
            after = join(blocks[b:], 1)
            got = swap(after, dy=b)
        leaving.append(after)
        summed.append((blocks[0], got))

    places = tuple((dc, dy) for dy in range(fy // 2) for dc in range(fc))
    *columns, ids, token = fetch(n, chunks * sub, places, decoder, indices, leaving[-1])
    columns = dict(zip(places, columns))
    sums, moved = [], []
    for p, (x, y) in enumerate(summed):
        x = x + (hold(y, token) if p == 0 else y)
        sums.append(lax.dynamic_slice_in_dim(x, z * group, group, 0))
        moved.append(
            [
                swap(lax.dynamic_slice_in_dim(x, (z ^ j) * group, group, 0), dz=j)
                for j in z_order(fz)
            ]
        )
    errs, loss, after = [], 0.0, sums[-1]
    for p in range(chunks):
        diff = sum(in_order(moved[p], after), sums[p])
        loss = loss + jnp.sum(diff * diff, axis=1, keepdims=True)
        errs.append(diff.astype(jnp.bfloat16))
        after = errs[p]

    err = join(errs, 1)
    come = [swap(err, dz=j) for j in z_order(fz)]
    near = [((0, 0), [join([err] + come[:-1], 0), come[-1]])]
    for b in bits(fy):
        last = [((0, b | at[1]), in_order([swap(e, dy=b) for e in parts])) for at, parts in near]
        near += last
    near = near[: -len(last)]
    totals = grad(n, rows, near, columns, None)
    places = tuple((dc, dy) for dy in range(fy // 2, fy) for dc in range(fc))
    *more, _, token = fetch(n, chunks * sub, places, decoder, indices, come[-1])
    columns.update(zip(places, more))
    last[-1][1][-1] = hold(last[-1][1][-1], totals, token)

    far = [((1, at[1]), [hold(swap(join(e, 0), dc=1), last[-1][1][-1])]) for at, e in near]
    far_last = [((1, at[1]), [swap(e, dc=1) for e in parts]) for at, parts in last]
    totals = grad(n, rows, last, columns, totals)
    totals = grad(n, rows, far, columns, totals)
    back = grad(n, rows, far_last, columns, totals, (in_vmem(ids), loss))
    pieces = near + far + last + far_last
    error = own_rows(n, [at for at, _ in pieces], own, width, [e[0][:group] for _, e in pieces])

    back = jnp.sum(lax.all_to_all(back, "lat", 0, 0, tiled=True), axis=0)
    return error, back[:, k_count] / width, back[:, :k_count]


def solution(mesh):
    in_specs = (P("groups", None), P("groups", None), P("lat", None), P(("groups", "lat"), None))
    out_specs = (P(("groups", "lat"), None), P(("groups", "lat")), P(("groups", "lat"), None))
    return jax.shard_map(local, mesh=mesh, in_specs=in_specs, out_specs=out_specs, check_vma=False)
```

```python
import functools

import jax
import jax.numpy as jnp
from jax import lax
from jax.experimental import pallas as pl
from jax.experimental.pallas import tpu as pltpu
from jax.sharding import PartitionSpec as P

CHUNKS = 2
ROW_STEP = 16
LANES = 128
SUBLANES = 8
LOADS = 4
VMEM = pl.BlockSpec(memory_space=pltpu.VMEM)
HBM = pl.BlockSpec(memory_space=pltpu.HBM)


def factors(n):
    assert n > 1 and n & (n - 1) == 0
    c = 2
    m = n // c
    y = 1
    while 4 * y * y <= m:
        y *= 2
    return m // y, y, c


def place(n, index):
    _, y, c = factors(n)
    return index // (y * c), (index // c) % y, index % c


def bits(size):
    return [1 << i for i in range(size.bit_length() - 1)]


def z_order(fz):
    return ([fz - 1] if fz > 1 else []) + list(range(1, fz - 1))


def pairs(n, dz, dy, dc):
    _, fy, fc = factors(n)
    out = []
    for i in range(n):
        z, y, c = place(n, i)
        out.append((i, ((z ^ dz) * fy + (y ^ dy)) * fc + (c ^ dc)))
    return out


def cost(flops, size):
    return pl.CostEstimate(flops=flops, bytes_accessed=size, transcendentals=0)


def params():
    return pltpu.CompilerParams(vmem_limit_bytes=12 * 1024 * 1024)


def in_hbm(x):
    return pltpu.with_memory_space_constraint(x, pltpu.HBM)


def in_vmem(x):
    return pltpu.with_memory_space_constraint(x, pltpu.VMEM)


def column(n, chunk, chunks, sub, dy, dc):
    _, fy, fc = factors(n)
    _, y, c = place(n, lax.axis_index("lat"))
    return pl.multiple_of((((c ^ dc) * fy + (y ^ dy)) * chunks + chunk) * sub, sub)


def hold(x, *after):
    def kernel(x_ref, *refs):
        refs[-1][...] = x_ref[...]

    return pl.pallas_call(
        kernel,
        out_shape=jax.ShapeDtypeStruct(x.shape, x.dtype),
        in_specs=[VMEM] * (1 + len(after)),
        out_specs=VMEM,
        input_output_aliases={0: 0},
        compiler_params=params(),
        name="hold",
    )(*[in_vmem(a) for a in (x, *after)])


def loads_of(decoder_hbm, col, buf, sem):
    count = sem.shape[0]
    step = buf.shape[0] // count
    return [
        pltpu.make_async_copy(
            decoder_hbm.at[pl.ds(i * step, step), pl.ds(col, buf.shape[1])],
            buf.at[pl.ds(i * step, step)],
            sem.at[i],
        )
        for i in range(count)
    ]


def decode_kernel(n, own, chunks, parts, first, *refs):
    fz, fy, fc = factors(n)
    me = lax.axis_index("lat")
    refs = list(refs)
    if first:
        ids_hbm, codes_hbm = refs.pop(0), refs.pop(0)
    else:
        dense_ref = refs.pop(0)
    decoder_hbm, targets_hbm = refs.pop(0), refs.pop(0)
    if len(refs) > 4 + len(parts) and not first:
        refs.pop(0)
    outs = [refs.pop(0) for _ in parts]
    if first:
        dense_ref = refs.pop(0)
    buf, sem, targets_ref, small = refs[:4]
    smalls_in = [(targets_hbm, targets_ref)]
    if first:
        ids_ref, codes_ref = refs[4:]
        smalls_in = [(ids_hbm, ids_ref), (codes_hbm, codes_ref)] + smalls_in
    smalls = [pltpu.make_async_copy(a, b, small.at[i]) for i, (a, b) in enumerate(smalls_in)]
    for copy in smalls:
        copy.start()
    rows, lat_dev = dense_ref.shape
    sub = outs[0].shape[1] // fy
    cols = [column(n, p, chunks, sub, o, dc) for p, dc in parts for o in range(fy)]
    loads = [loads_of(decoder_hbm, col, buf.at[i], sem.at[i]) for i, col in enumerate(cols)]
    for copies in loads:
        for copy in copies:
            copy.start()
    for copy in smalls:
        copy.wait()
    if first:
        k_count = ids_ref.shape[1]
        assert lat_dev <= 512
        half = lat_dev // 2
        lanes = (lax.broadcasted_iota(jnp.int32, (ROW_STEP, lat_dev), 1) - half).astype(jnp.bfloat16)

        def body(g, carry):
            at = pl.ds(pl.multiple_of(g * ROW_STEP, ROW_STEP), ROW_STEP)
            ids = ids_ref[at, :] - (me * lat_dev + half)
            ids = jnp.where((ids >= -half) & (ids < half), ids, half + 44).astype(jnp.bfloat16)
            codes = codes_ref[at, :]
            acc = jnp.zeros((ROW_STEP, lat_dev), jnp.bfloat16)
            for k in range(k_count):
                acc = jnp.where(ids[:, k : k + 1] == lanes, codes[:, k : k + 1], acc)
            dense_ref[at, :] = acc
            return carry

        lax.fori_loop(0, rows // ROW_STEP, body, 0)
    per = SUBLANES // own
    tile = pl.ds(pl.multiple_of(me // per * SUBLANES, SUBLANES), SUBLANES)
    mine = lax.broadcasted_iota(jnp.int32, (SUBLANES, sub), 0) // own == me % per
    for i, col in enumerate(cols):
        for copy in loads[i]:
            copy.wait()
        out_ref = outs[i // fy]
        here = slice(i % fy * sub, (i % fy + 1) * sub)
        out_ref[:, here] = jnp.dot(dense_ref[...], buf[i], preferred_element_type=jnp.float32)
        target = targets_ref[:, pl.ds(col, sub)].astype(jnp.float32)
        target = jnp.concatenate([target] * per, axis=0)
        out_ref[tile, here] -= jnp.where(mine, target, 0.0)


def decode(n, chunks, sub, parts, decoder, targets, start=None, dense=None, after=None):
    _, fy, _ = factors(n)
    first = start is not None
    rows = start[0].shape[0] if first else dense.shape[0]
    lat_dev = decoder.shape[0]
    out = [pltpu.VMEM((rows, fy * sub), jnp.float32)] * len(parts)
    count = len(parts) * fy
    scratch = [
        pltpu.VMEM((count, lat_dev, sub), jnp.bfloat16),
        pltpu.SemaphoreType.DMA((count, 1)),
        pltpu.VMEM(targets.shape, targets.dtype),
        pltpu.SemaphoreType.DMA((3,)),
    ]
    if first:
        args = [in_hbm(x) for x in (*start, decoder, targets)]
        specs = [HBM] * 4
        out.append(pltpu.VMEM((rows, lat_dev), jnp.bfloat16))
        scratch += [pltpu.VMEM(x.shape, x.dtype) for x in start]
    else:
        args, specs = [dense, in_hbm(decoder), in_hbm(targets)], [VMEM, HBM, HBM]
        if after is not None:
            args.append(in_vmem(after))
            specs.append(VMEM)
    return pl.pallas_call(
        functools.partial(decode_kernel, n, rows // n, chunks, parts, first),
        out_shape=out,
        in_specs=specs,
        out_specs=[VMEM] * len(out),
        scratch_shapes=scratch,
        compiler_params=params(),
        cost_estimate=cost(2 * rows * lat_dev * count * sub, 4 * lat_dev * count * sub),
        name="decode",
    )(*args)


def fetch_kernel(n, places, decoder_hbm, ids_hbm, _, *refs):
    outs = refs[: len(places)]
    ids_ref, token_ref, sem, ids_sem = refs[len(places) :]
    copies = [pltpu.make_async_copy(ids_hbm, ids_ref, ids_sem)]
    for i, (dc, dy) in enumerate(places):
        col = column(n, 0, 1, outs[i].shape[1], dy, dc)
        copies += loads_of(decoder_hbm, col, outs[i], sem.at[i])
    for copy in copies:
        copy.start()
    token_ref[...] = jnp.zeros_like(token_ref)
    for copy in copies:
        copy.wait()


def fetch(n, width, places, decoder, ids, after):
    block = pltpu.VMEM((decoder.shape[0], width), decoder.dtype)
    return pl.pallas_call(
        functools.partial(fetch_kernel, n, places),
        out_shape=[block] * len(places)
        + [pltpu.VMEM(ids.shape, ids.dtype), pltpu.VMEM((SUBLANES, LANES), jnp.float32)],
        in_specs=[HBM, HBM, VMEM],
        out_specs=[VMEM] * (2 + len(places)),
        scratch_shapes=[pltpu.SemaphoreType.DMA((len(places), LOADS)), pltpu.SemaphoreType.DMA],
        compiler_params=params(),
        cost_estimate=cost(0, decoder.shape[0] * len(places) * width * 2),
        name="fetch",
    )(in_hbm(decoder), in_hbm(ids), in_vmem(after))


def grad_kernel(n, counts, with_prev, final, *refs):
    refs = list(refs)
    errs = [[refs.pop(0) for _ in range(count)] for count in counts]
    columns = [refs.pop(0) for _ in counts]
    total = refs.pop(0)[...] if with_prev else None
    for parts, columns_ref in zip(errs, columns):
        err = parts[0][...] if len(parts) == 1 else jnp.concatenate([e[...] for e in parts], axis=0)
        part = lax.dot_general(
            err,
            columns_ref[...],
            (((1,), (1,)), ((), ())),
            preferred_element_type=jnp.float32,
        )
        total = part if total is None else total + part
    if not final:
        refs[0][...] = total
        return
    ids_ref, loss_ref, out_ref, totals_ref = refs
    totals_ref[...] = total
    rows, k_count = ids_ref.shape
    lat_dev = total.shape[1]
    own = out_ref.shape[1]
    fz, _, _ = factors(n)
    me = lax.axis_index("lat")
    z, _, _ = place(n, me)
    group = rows // fz
    places = lax.broadcasted_iota(jnp.int32, (ROW_STEP, LANES), 1)
    pad = jnp.zeros((ROW_STEP, LANES - k_count), jnp.int32)
    for q, j in enumerate([0] + z_order(fz)):
        for s in range(0, group, ROW_STEP):
            first = (z ^ j) * group + s
            rows_at = pl.ds(pl.multiple_of(first, ROW_STEP), ROW_STEP)
            ids = jnp.concatenate([ids_ref[rows_at, :] - me * lat_dev, pad], axis=1)
            held = jnp.where(places < k_count, ids // LANES, -1)
            inside = ids % LANES
            acc = jnp.zeros((ROW_STEP, LANES), jnp.float32)
            if q == 0:
                acc = jnp.where(places == k_count, loss_ref[s : s + ROW_STEP, :], acc)
            here = slice(q * group + s, q * group + s + ROW_STEP)
            for t in range(lat_dev // LANES):
                values = totals_ref[here, t * LANES : (t + 1) * LANES]
                found = jnp.take_along_axis(values, inside, axis=1, mode="promise_in_bounds")
                acc = jnp.where(held == t, found, acc)
            for d in range(ROW_STEP // own):
                out_ref[first // own + d] = acc[d * own : (d + 1) * own, :]


def grad(n, rows, pieces, columns, prev, final=None):
    lat_dev, wide = columns[pieces[0][0]].shape
    counts = tuple(len(e) for _, e in pieces)
    args = [x for _, e in pieces for x in e] + [in_vmem(columns[at]) for at, _ in pieces]
    if prev is not None:
        args.append(in_vmem(prev))
    if final is not None:
        args += list(final)
    totals = pltpu.VMEM((rows, lat_dev), jnp.float32)
    size = wide * len(pieces)
    return pl.pallas_call(
        functools.partial(grad_kernel, n, counts, prev is not None, final is not None),
        out_shape=totals if final is None else pltpu.VMEM((n, rows // n, LANES), jnp.float32),
        in_specs=[VMEM] * len(args),
        out_specs=VMEM,
        scratch_shapes=[] if final is None else [totals],
        compiler_params=params(),
        cost_estimate=cost(2 * rows * lat_dev * size, 4 * lat_dev * size),
        name="grad",
    )(*args)


def own_kernel(n, blocks, own, *refs):
    errs, out_ref = refs[:-1], refs[-1]
    _, fy, fc = factors(n)
    _, y, c = place(n, lax.axis_index("lat"))
    group, sub = errs[0].shape
    row = lax.broadcasted_iota(jnp.int32, (own, group), 0) + (y * fc + c) * own
    want = lax.broadcasted_iota(jnp.int32, (own, group), 1)
    mine = jnp.where(row == want, 1.0, 0.0).astype(jnp.bfloat16)
    for err, (dc, dy) in zip(errs, blocks):
        rows = jnp.dot(mine, err[...], preferred_element_type=jnp.float32)
        out_ref[:, pl.ds(column(n, 0, 1, sub, dy, dc), sub)] = rows.astype(jnp.bfloat16)


def own_rows(n, blocks, own, width, errs):
    return pl.pallas_call(
        functools.partial(own_kernel, n, tuple(blocks), own),
        out_shape=jax.ShapeDtypeStruct((own, width), jnp.bfloat16),
        in_specs=[VMEM] * len(errs),
        out_specs=VMEM,
        compiler_params=params(),
        name="own_rows",
    )(*errs)


def local(codes, indices, decoder, targets):
    width = decoder.shape[1]
    rows, k_count = codes.shape
    n = lax.axis_size("lat")
    own = rows // n
    fz, fy, fc = factors(n)
    group = rows // fz
    chunks = CHUNKS
    sub = width // (fc * fy * chunks)
    z, _, _ = place(n, lax.axis_index("lat"))

    def swap(x, dz=0, dy=0, dc=0):
        return lax.ppermute(x, "lat", pairs(n, dz, dy, dc))

    def join(xs, axis):
        return xs[0] if len(xs) == 1 else jnp.concatenate(xs, axis=axis)

    def in_order(xs, after=None):
        for i, x in enumerate(xs):
            if after is not None:
                xs[i] = hold(x, after)
            after = xs[i]
        return xs

    others = tuple((p, 1) for p in range(chunks))
    *parts, dense = decode(n, chunks, sub, others, decoder, targets, (indices, codes))
    came = [swap(part, dc=1) for part in parts]
    summed, leaving, after = [], [], None
    for p in range(chunks):
        (part,) = decode(n, chunks, sub, ((p, 0),), decoder, targets, dense=dense, after=after)
        total = part + came[p]
        blocks = [total[:, o * sub : (o + 1) * sub] for o in range(fy)]
        got = None
        for b in reversed(bits(fy)):
            if got is not None:
                blocks = [blocks[o] + got[:, o * sub : (o + 1) * sub] for o in range(2 * b)]
            after = join(blocks[b:], 1)
            got = swap(after, dy=b)
        leaving.append(after)
        summed.append((blocks[0], got))

    places = tuple((dc, dy) for dy in range(fy) for dc in range(fc))
    *columns, ids, token = fetch(n, chunks * sub, places, decoder, indices, leaving[-1])
    columns = dict(zip(places, columns))
    sums, moved = [], []
    for p, (x, y) in enumerate(summed):
        x = x + (hold(y, token) if p == 0 else y)
        sums.append(lax.dynamic_slice_in_dim(x, z * group, group, 0))
        moved.append(
            [
                swap(lax.dynamic_slice_in_dim(x, (z ^ j) * group, group, 0), dz=j)
                for j in z_order(fz)
            ]
        )
    errs, loss, after = [], 0.0, sums[-1]
    for p in range(chunks):
        diff = sum(in_order(moved[p], after), sums[p])
        loss = loss + jnp.sum(diff * diff, axis=1, keepdims=True)
        errs.append(diff.astype(jnp.bfloat16))
        after = errs[p]

    err = join(errs, 1)
    come = [swap(err, dz=j) for j in z_order(fz)]
    near = [((0, 0), [join([err] + come[:-1], 0), come[-1]])]
    for b in bits(fy):
        last = [((0, b | at[1]), in_order([swap(e, dy=b) for e in parts])) for at, parts in near]
        near += last
    near = near[: -len(last)]
    half = rows // 2

    def halves(parts):
        whole = join(parts, 0)
        return [whole[:group], whole[group : group + half], whole[group + half :]]

    far = [((1, at[1]), [swap(e, dc=1) for e in halves(parts)]) for at, parts in near]
    totals = grad(n, rows, near, columns, None)
    totals = grad(n, rows, far, columns, totals)
    last[-1][1][-1] = hold(last[-1][1][-1], totals)
    far_last = [((1, at[1]), [swap(join(parts, 0), dc=1)]) for at, parts in last]
    totals = grad(n, rows, last, columns, totals)
    back = grad(n, rows, far_last, columns, totals, (in_vmem(ids), loss))
    pieces = near + far + last + far_last
    error = own_rows(n, [at for at, _ in pieces], own, width, [e[0][:group] for _, e in pieces])

    back = jnp.sum(lax.all_to_all(back, "lat", 0, 0, tiled=True), axis=0)
    return error, back[:, k_count] / width, back[:, :k_count]


def solution(mesh):
    in_specs = (P("groups", None), P("groups", None), P("lat", None), P(("groups", "lat"), None))
    out_specs = (P(("groups", "lat"), None), P(("groups", "lat")), P(("groups", "lat"), None))
    return jax.shard_map(local, mesh=mesh, in_specs=in_specs, out_specs=out_specs, check_vma=False)
```
